32 devices in a mesh: req: 8 (over y, x, core), tp: 4 (over z).
Axes of the slice: x: 2, y: 2, z: 4, core: 2. Of those that a mesh axis runs over, the one named last changes fastest.
Arguments:
- hidden: bfloat16 [2048, 5120], P('req', 'tp'), may hold values from -8 to 8
- q_new: bfloat16 [2048, 5120], P('req', 'tp'), may hold values from -8 to 8
- k_new: bfloat16 [2048, 5120], P('req', 'tp'), may hold values from -8 to 8
- v_new: bfloat16 [2048, 5120], P('req', 'tp'), may hold values from -8 to 8
- cache_k: bfloat16 [8, 4096, 5120], P('req', None, 'tp'), may hold values from -8 to 8
- cache_v: bfloat16 [8, 4096, 5120], P('req', None, 'tp'), may hold values from -8 to 8
- cache_len: int32 [8], replicated, may hold values from 1 to 4096, 8192 in all
- w_out: bfloat16 [5120, 5120], P('tp', 'req'), may hold values from -0.625 to 0.625
- q_cross: bfloat16 [2048, 5120], P('req', 'tp'), may hold values from -8 to 8
- text_k: bfloat16 [4, 512, 5120], P(None, 'req', 'tp'), may hold values from -8 to 8
- text_v: bfloat16 [4, 512, 5120], P(None, 'req', 'tp'), may hold values from -12 to 12
- prompt_of: int32 [8], P('req'), may hold values from 0 to 3, as said below
Outputs:
- hidden_out: bfloat16 [2048, 5120], P('req', 'tp')
- cross_heads: bfloat16 [2048, 5120], P('req', 'tp')
The draws below stay inside these ranges and needn't reach their ends.
Inputs may be any that keep to these rules, and one draw needn't show every extreme that they name: `cache_len`: cache rows at or beyond a request's length hold no data; the longest request fills all 4096 rows. `prompt_of`: each of the 4 prompts serves exactly 2 requests.
All inputs are finite; a program needn't handle non-finite values.
Results may differ from the reference program's by a relative error of at most 0.014.
Values may be sent and summed in bfloat16 or wider, within the bound.
No kernel may reach another device: no remote copies, remote signals or barrier semaphores. Data moves between devices by JAX's collectives and lax.ppermute only.
A program may use at most 128 MiB of HBM per device.

```python
import math
import jax
import jax.numpy as jnp
import numpy as np
from jax import lax

D = 5120
HEADS = 40
HD = 128
TEXT = 512
NEW = 256
CACHE = 4096
PROMPTS = 4
F = 5120
REQS = 8
TOKENS = 2048


def shared_signs(key):
    base_key = jax.random.fold_in(key, 101)
    key_order = jax.random.fold_in(base_key, 0)
    prompt_ids = (jax.random.permutation(key_order, REQS) % PROMPTS).astype(jnp.int32)
    return prompt_ids


def rough_normal(key, tag, shape):
    return jnp.clip(jax.random.normal(jax.random.fold_in(key, tag), shape, jnp.float32), -8.0, 8.0)


def draw_q_new(key, part):
    values = rough_normal(key, 1, (REQS, NEW, F))
    return values.reshape(TOKENS, F).astype(jnp.bfloat16)


def draw_k_new(key, part):
    values = rough_normal(key, 2, (REQS, NEW, F))
    return values.reshape(TOKENS, F).astype(jnp.bfloat16)


def draw_cache_k(key, part):
    values = rough_normal(key, 3, (REQS, CACHE, F))
    return values.astype(jnp.bfloat16)


def draw_q_cross(key, part):
    values = rough_normal(key, 4, (REQS, NEW, F))
    return values.reshape(TOKENS, F).astype(jnp.bfloat16)


def draw_text_k(key, part):
    values = rough_normal(key, 5, (PROMPTS, TEXT, F))
    return values.astype(jnp.bfloat16)


def draw_prompt_of(key, part):
    return shared_signs(key)


def steps_of(own_key, extent, shards, least, largest):
    gain = 1.0
    for axis_at, parts in shards:
        heights = jax.random.uniform(jax.random.fold_in(jax.random.fold_in(own_key, 6), axis_at), (parts,), jnp.float32, least / len(shards), largest / len(shards))
        gain = gain * jnp.repeat(jnp.exp(heights), extent[axis_at] // parts).reshape((-1,) + (1,) * (len(extent) - 1 - axis_at))
    return gain


def length_profile(count, total, reach, slope):
    loads = [(1 << 20) // math.isqrt(grade ** slope) + 1 for grade in range(2, count + 1)]
    spare, given = total - reach - (count - 1), [1] * (count - 1)
    while spare > 0:
        free = [i for i in range(count - 1) if given[i] < reach]
        whole, budget = sum([loads[i] for i in free]), spare
        for i in free:
            extra = min(reach - given[i], max(1, budget * loads[i] // whole), spare)
            given[i] = given[i] + extra
            spare = spare - extra
    return np.array([reach] + given)


def uneven_parts(own_key, amount, total, reach, lean):
    if amount == 2:
        one = jax.random.randint(own_key, (), max(1, total - reach), min(reach, total - 1) + 1)
        return jnp.stack([one, total - one])
    tallies = jnp.asarray(length_profile(amount, total, reach, lean), jnp.int32)
    pairs = (amount - 1) // 2
    source_of, receiver = tallies[1:1 + 2 * pairs:2], tallies[2:2 + 2 * pairs:2]
    room = jnp.minimum(source_of - 1, reach - receiver)
    moved = jax.random.randint(jax.random.fold_in(own_key, 1), (pairs,), 0, 1 << 20) % (room + 1)
    tallies = tallies.at[1:1 + 2 * pairs:2].set(source_of - moved).at[2:2 + 2 * pairs:2].set(receiver + moved)
    return tallies[jax.random.permutation(jax.random.fold_in(own_key, 2), amount)]


def scatter_about(own_key, dims, width, most, pieces=(), kind=jnp.bfloat16):
    result = jax.random.normal(own_key, dims, jnp.float32) * width
    if len(pieces) > 0:
        result = steps_of(own_key, dims, pieces, -0.22, 0.18) * result
    return jnp.clip(result, min=-most, max=most).astype(kind)


def setup_inputs(seed: int = 0) -> dict:
    key_list = jax.random.split(jax.random.key(seed), 13)
    hidden = scatter_about(key_list[0], (TOKENS, D), 1.0, 8.0, ((0, 8), (1, 4)))
    q_new = draw_q_new(jax.random.fold_in(key_list[12], 71), 0)
    k_new = draw_k_new(jax.random.fold_in(key_list[12], 71), 0)
    v_new = scatter_about(key_list[3], (TOKENS, F), 1.0, 8.0, ((0, 8), (1, 4)))
    cache_k = draw_cache_k(jax.random.fold_in(key_list[12], 71), 0)
    cache_v = scatter_about(key_list[5], (REQS, CACHE, F), 1.0, 8.0, ((0, 8), (2, 4)))
    cache_len = uneven_parts(key_list[6], REQS, REQS * CACHE // 4, CACHE, 2).astype(jnp.int32)
    w_out = scatter_about(key_list[7], (F, D), (F // 64) ** -0.5, 0.625, ((0, 4), (1, 8)))
    q_cross = draw_q_cross(jax.random.fold_in(key_list[12], 71), 0)
    text_k = draw_text_k(jax.random.fold_in(key_list[12], 71), 0)
    text_v = scatter_about(key_list[10], (PROMPTS, TEXT, F), 2.0, 12.0, ((1, 8), (2, 4)))
    prompt_of = draw_prompt_of(jax.random.fold_in(key_list[12], 71), 0)
    return dict(hidden=hidden, q_new=q_new, k_new=k_new, v_new=v_new, cache_k=cache_k, cache_v=cache_v, cache_len=cache_len, w_out=w_out, q_cross=q_cross, text_k=text_k, text_v=text_v, prompt_of=prompt_of)


NEG_FILL = -1e30


def attend_all(queries, keys, values, visible):
    scores = jnp.einsum("qhd,khd->hqk", queries.astype(jnp.float32), keys.astype(jnp.float32)) * (HD ** -0.5)
    scores = jnp.where(visible[None], scores, NEG_FILL)
    maxima = jnp.max(scores, axis=-1, keepdims=True)
    weights = jnp.where(visible[None], jnp.exp(scores - maxima), jnp.float32(0.0))
    masses = jnp.sum(weights, axis=-1)
    rounded = lax.optimization_barrier(weights.astype(jnp.bfloat16))
    output = jnp.einsum("hqk,khd->hqd", rounded.astype(jnp.float32), values.astype(jnp.float32)) / masses[..., None]
    return output.transpose(1, 0, 2).reshape(queries.shape[0], HEADS * HD).astype(jnp.bfloat16)


def reference(hidden, q_new, k_new, v_new, cache_k, cache_v, cache_len, w_out, q_cross, text_k, text_v, prompt_of):
    def self_request(items):
        queries, new_keys, new_values, old_keys, old_values, length = items
        keys = jnp.concatenate([old_keys, new_keys], axis=0).reshape(CACHE + NEW, HEADS, HD)
        values = jnp.concatenate([old_values, new_values], axis=0).reshape(CACHE + NEW, HEADS, HD)
        row_ids = jnp.arange(NEW, dtype=jnp.int32)[:, None]
        col_ids = jnp.arange(CACHE + NEW, dtype=jnp.int32)[None, :]
        visible = jnp.where(col_ids < CACHE, col_ids < length, (col_ids - CACHE) <= row_ids)
        return attend_all(queries.reshape(NEW, HEADS, HD), keys, values, visible)

    self_heads = lax.map(self_request, (q_new.reshape(REQS, NEW, F), k_new.reshape(REQS, NEW, F), v_new.reshape(REQS, NEW, F), cache_k, cache_v, cache_len))
    self_heads = self_heads.reshape(TOKENS, F)
    projected = jnp.dot(self_heads, w_out, preferred_element_type=jnp.float32)
    hidden_out = (hidden.astype(jnp.float32) + projected).astype(jnp.bfloat16)

    def cross_request(items):
        queries, prompt = items
        keys = jnp.take(text_k, prompt, axis=0).reshape(TEXT, HEADS, HD)
        values = jnp.take(text_v, prompt, axis=0).reshape(TEXT, HEADS, HD)
        visible = jnp.ones((NEW, TEXT), dtype=bool)
        return attend_all(queries.reshape(NEW, HEADS, HD), keys, values, visible)

    cross_heads = lax.map(cross_request, (q_cross.reshape(REQS, NEW, F), prompt_of)).reshape(TOKENS, F)
    return hidden_out, cross_heads
```

```python
import functools

import jax
import jax.numpy as jnp
from jax import lax
from jax.experimental import pallas as pl
from jax.experimental.pallas import tpu as pltpu
from jax.sharding import PartitionSpec as P

HD = 128
CACHE_BLOCK = 1024
HEAD_GROUPS = 2
NEG_FILL = -1e30
LOG2E = 1.4426950408889634
VMEM_LIMIT = 48 * 2**20


def attend(queries, keys, values, state, visible):
    top_old, mass, total = state
    scale = HD ** (-0.5) * LOG2E
    scores = lax.dot_general(
        queries, keys, (((1,), (1,)), ((), ())), preferred_element_type=jnp.float32
    )
    if visible is not None:
        scores = jnp.where(visible, scores, NEG_FILL)
    top = jnp.maximum(top_old, jnp.max(scores, axis=1, keepdims=True))
    shrink = jnp.exp2((top_old - top) * scale)
    weights = jnp.exp2(scores * scale - top[:, :1] * scale)
    mass = mass * shrink + jnp.sum(weights, axis=1, keepdims=True)
    total = total * shrink + lax.dot_general(
        weights.astype(jnp.bfloat16),
        values,
        (((1,), (0,)), ((), ())),
        preferred_element_type=jnp.float32,
    )
    return top, mass, total


def self_kernel(
    block_rows, heads, first_query, length_ref, q_ref, kn_ref, vn_ref, kc_ref, vc_ref, o_ref,
    top_ref, mass_ref, total_ref,
):
    step, steps = pl.program_id(0), pl.num_programs(0)
    left = length_ref[0] - step * block_rows
    rows, new_rows = q_ref.shape[0], kn_ref.shape[0]

    @pl.when(step == 0)
    def _():
        top_ref[...] = jnp.full_like(top_ref, NEG_FILL)
        mass_ref[...] = jnp.zeros_like(mass_ref)
        total_ref[...] = jnp.zeros_like(total_ref)

    def visit(head, k_ref, v_ref, visible):
        cols = slice(head * HD, (head + 1) * HD)
        state = (top_ref[head], mass_ref[head], total_ref[head])
        state = attend(q_ref[:, cols], k_ref[:, cols], v_ref[:, cols], state, visible)
        top_ref[head], mass_ref[head], total_ref[head] = state
        return state

    @pl.when(jnp.logical_and(step < steps - 1, left >= block_rows))
    def _():
        for head in range(heads):
            visit(head, kc_ref, vc_ref, None)

    @pl.when(jnp.logical_and(step < steps - 1, jnp.logical_and(left > 0, left < block_rows)))
    def _():
        visible = lax.broadcasted_iota(jnp.int32, (rows, block_rows), 1) < left
        for head in range(heads):
            visit(head, kc_ref, vc_ref, visible)

    @pl.when(step == steps - 1)
    def _():
        key_ids = lax.broadcasted_iota(jnp.int32, (rows, new_rows), 1)
        query_ids = lax.broadcasted_iota(jnp.int32, (rows, new_rows), 0) + first_query
        for head in range(heads):
            _, mass, total = visit(head, kn_ref, vn_ref, key_ids <= query_ids)
            o_ref[:, head * HD : (head + 1) * HD] = (total / mass).astype(o_ref.dtype)


def self_attention(queries, new_keys, new_values, keys, values, length, first_row, rows, group, width):
    new_rows = queries.shape[0]
    capacity = keys.shape[0]
    block_rows = min(CACHE_BLOCK, capacity)
    heads = width // HD
    blocks = capacity // block_rows
    new_spec = pl.BlockSpec((first_row + rows, width), lambda i, n: (0, group))
    cache_spec = pl.BlockSpec(
        (block_rows, width), lambda i, n: (jnp.minimum(i, (n[0] - 1) // block_rows), group)
    )
    return pl.pallas_call(
        functools.partial(self_kernel, block_rows, heads, first_row),
        grid_spec=pltpu.PrefetchScalarGridSpec(
            num_scalar_prefetch=1,
            grid=(blocks + 1,),
            in_specs=[
                pl.BlockSpec((rows, width), lambda i, n: (first_row // rows, group)),
                new_spec,
                new_spec,
                cache_spec,
                cache_spec,
            ],
            out_specs=pl.BlockSpec((rows, width), lambda i, n: (0, 0)),
            scratch_shapes=[
                pltpu.VMEM((heads, rows, HD), jnp.float32),
                pltpu.VMEM((heads, rows, HD), jnp.float32),
                pltpu.VMEM((heads, rows, HD), jnp.float32),
            ],
        ),
        out_shape=jax.ShapeDtypeStruct((rows, width), jnp.bfloat16),
        compiler_params=pltpu.CompilerParams(vmem_limit_bytes=VMEM_LIMIT),
        cost_estimate=pl.CostEstimate(
            flops=4 * rows * (capacity + new_rows) * width,
            bytes_accessed=4 * (capacity + new_rows) * width,
            transcendentals=rows * (capacity + new_rows) * heads,
        ),
        name="self_attention",
    )(length.reshape(1), queries, new_keys, new_values, keys, values)


def cross_kernel(heads, q_ref, *refs):
    pieces, o_ref = refs[:-1], refs[-1]
    rows = q_ref.shape[0]
    for head in range(heads):
        cols = slice(head * HD, (head + 1) * HD)
        keys = jnp.concatenate([piece[0, :, cols] for piece in pieces], axis=0)
        values = jnp.concatenate([piece[1, :, cols] for piece in pieces], axis=0)
        state = (
            jnp.full((rows, HD), NEG_FILL, jnp.float32),
            jnp.zeros((rows, HD), jnp.float32),
            jnp.zeros((rows, HD), jnp.float32),
        )
        _, mass, total = attend(q_ref[:, cols], keys, values, state, None)
        o_ref[:, cols] = (total / mass).astype(o_ref.dtype)


def cross_attention(queries, pieces):
    rows, width = queries.shape
    return pl.pallas_call(
        functools.partial(cross_kernel, width // HD),
        out_shape=jax.ShapeDtypeStruct((rows, width), jnp.bfloat16),
        compiler_params=pltpu.CompilerParams(vmem_limit_bytes=VMEM_LIMIT),
        name="cross_attention",
    )(queries, *pieces)


def pick_kernel(count, place_ref, prompt_ref, k_ref, v_ref, *refs):
    outs, sems = refs[:count], refs[count]
    copies = []
    for step in range(count):
        prompt = prompt_ref[place_ref[0] ^ step]
        copies.append(pltpu.make_async_copy(k_ref.at[prompt], outs[step].at[0], sems.at[2 * step]))
        copies.append(
            pltpu.make_async_copy(v_ref.at[prompt], outs[step].at[1], sems.at[2 * step + 1])
        )
    for copy in copies:
        copy.start()
    for copy in copies:
        copy.wait()


def pick_text(place, prompts, text_k, text_v):
    count = prompts.shape[0]
    _, rows, width = text_k.shape
    scalars = pl.BlockSpec(memory_space=pltpu.SMEM)
    hbm = pl.BlockSpec(memory_space=pl.ANY)
    return pl.pallas_call(
        functools.partial(pick_kernel, count),
        in_specs=[scalars, scalars, hbm, hbm],
        out_specs=[hbm] * count,
        out_shape=[jax.ShapeDtypeStruct((2, rows, width), text_k.dtype)] * count,
        scratch_shapes=[pltpu.SemaphoreType.DMA((2 * count,))],
        name="pick_text",
    )(place.reshape(1), prompts, text_k, text_v)


def project_kernel(count, place_ref, own_ref, near_ref, *refs):
    held, passed = refs[:count], refs[count : 2 * count]
    o_ref, weights, sems = refs[2 * count :]
    chip, holder = place_ref[0], place_ref[1]
    rows = own_ref.shape[0]

    def each(choice, act):
        for step in range(count):
            act(pltpu.make_async_copy(choice[step], weights.at[step], sems.at[step]))

    @pl.when(holder == 1)
    def _():
        each(held, lambda copy: copy.start())

    @pl.when(holder == 0)
    def _():
        each(passed, lambda copy: copy.start())

    for step in range(count):
        pltpu.make_async_copy(held[step], weights.at[step], sems.at[step]).wait()
        at = chip ^ step
        for part, x_ref in enumerate((own_ref, near_ref)):
            o_ref[at, part * rows : (part + 1) * rows, :] = jnp.dot(
                x_ref[...], weights[step], preferred_element_type=jnp.float32
            ).astype(o_ref.dtype)


def project(chip, holder, own, near, held, passed):
    count = len(held)
    rows, depth = own.shape
    columns = held[0].shape[1]
    hbm = pl.BlockSpec(memory_space=pl.ANY)
    vmem = pl.BlockSpec(memory_space=pltpu.VMEM)
    return pl.pallas_call(
        functools.partial(project_kernel, count),
        in_specs=[pl.BlockSpec(memory_space=pltpu.SMEM), vmem, vmem] + [hbm] * (2 * count),
        out_specs=vmem,
        out_shape=jax.ShapeDtypeStruct((count, 2 * rows, columns), jnp.bfloat16),
        scratch_shapes=[
            pltpu.VMEM((count, depth, columns), jnp.bfloat16),
            pltpu.SemaphoreType.DMA((count,)),
        ],
        compiler_params=pltpu.CompilerParams(vmem_limit_bytes=VMEM_LIMIT),
        name="project",
    )(jnp.stack([chip, holder]).astype(jnp.int32), own, near, *held, *passed)


def per_device(
    reqs,
    tps,
    hidden,
    q_new,
    k_new,
    v_new,
    cache_k,
    cache_v,
    cache_len,
    w_out,
    q_cross,
    text_k,
    text_v,
    prompt_of,
):
    rows, width = q_new.shape
    chips = reqs // 2
    place = lax.axis_index("req")
    chip, core = place // 2, place % 2
    side = chip % 2
    holder = core == side
    length = lax.dynamic_index_in_dim(cache_len, place, 0, keepdims=False)

    def swap(array, distance):
        return lax.ppermute(array, "req", [(i, i ^ distance) for i in range(reqs)])

    held = [w_out]
    held.append(
        lax.ppermute(
            w_out,
            "req",
            [(2 * i + 1 - i % 2, 2 * (i ^ 1) + 1 - i % 2) for i in range(chips)],
        )
    )
    bit = 2
    while bit < chips:
        pairs = [(2 * i + i % 2, 2 * (i ^ bit) + i % 2) for i in range(chips)]
        held += [lax.ppermute(block, "req", pairs) for block in held]
        bit *= 2
    across = [(2 * i + i % 2, 2 * i + 1 - i % 2) for i in range(chips)]
    passed = [lax.ppermute(block, "req", across) for block in held]

    prompts = lax.all_gather(prompt_of, "req", axis=0, tiled=True)
    pieces = pick_text(place, prompts, text_k, text_v)
    pieces = [pieces[0]] + [swap(pieces[i], i) for i in range(1, reqs)]

    groups = HEAD_GROUPS if (width // HD) % HEAD_GROUPS == 0 else 1
    group_width = width // groups
    parts = [
        self_attention(
            q_new, k_new, v_new, cache_k[0], cache_v[0], length, 0, rows, group, group_width
        )
        for group in range(groups)
    ]
    own = jnp.concatenate(parts, axis=1)
    near = swap(own, 2)
    terms = project(chip, holder, own, near, held, passed)
    summed = lax.psum_scatter(terms, "tp", scatter_dimension=0, tiled=True)
    kept, given = summed[:, :rows], summed[:, rows:]
    received = swap(given, 2)
    ordered = jnp.where(
        side == 0, jnp.stack([kept, received], axis=1), jnp.stack([received, kept], axis=1)
    )
    ordered = ordered.transpose(2, 0, 1, 3).reshape(rows, -1)
    hidden_out = (hidden.astype(jnp.float32) + ordered.astype(jnp.float32)).astype(jnp.bfloat16)
    cross_heads = cross_attention(q_cross, pieces)
    return (hidden_out, cross_heads)


def solution(mesh):
    placed = (
        P("req", "tp"),
        P("req", "tp"),
        P("req", "tp"),
        P("req", "tp"),
        P("req", None, "tp"),
        P("req", None, "tp"),
        P(),
        P("tp", "req"),
        P("req", "tp"),
        P(None, "req", "tp"),
        P(None, "req", "tp"),
        P("req"),
    )
    return jax.shard_map(
        functools.partial(per_device, mesh.shape["req"], mesh.shape["tp"]),
        mesh=mesh,
        in_specs=placed,
        out_specs=(P("req", "tp"), P("req", "tp")),
        check_vma=False,
    )
```

```python
import functools

import jax
import jax.numpy as jnp
from jax import lax
from jax.experimental import pallas as pl
from jax.experimental.pallas import tpu as pltpu
from jax.sharding import PartitionSpec as P

HD = 128
CACHE_BLOCK = 1024
HEAD_GROUPS = 2
TAG_ROWS = 16
NEG_FILL = -1e30
LOG2E = 1.4426950408889634
VMEM_LIMIT = 48 * 2**20


def attend(queries, keys, values, state, visible):
    top_old, mass, total = state
    scale = HD ** (-0.5) * LOG2E
    scores = lax.dot_general(
        queries, keys, (((1,), (1,)), ((), ())), preferred_element_type=jnp.float32
    )
    if visible is not None:
        scores = jnp.where(visible, scores, NEG_FILL)
    top = jnp.maximum(top_old, jnp.max(scores, axis=1, keepdims=True))
    shrink = jnp.exp2((top_old - top) * scale)
    weights = jnp.exp2(scores * scale - top[:, :1] * scale)
    mass = mass * shrink + jnp.sum(weights, axis=1, keepdims=True)
    total = total * shrink + lax.dot_general(
        weights.astype(jnp.bfloat16),
        values,
        (((1,), (0,)), ((), ())),
        preferred_element_type=jnp.float32,
    )
    return top, mass, total


def self_kernel(
    block_rows, heads, first_query, length_ref, q_ref, kn_ref, vn_ref, kc_ref, vc_ref, o_ref,
    top_ref, mass_ref, total_ref,
):
    step, steps = pl.program_id(0), pl.num_programs(0)
    left = length_ref[0] - step * block_rows
    rows, new_rows = q_ref.shape[0], kn_ref.shape[0]

    @pl.when(step == 0)
    def _():
        top_ref[...] = jnp.full_like(top_ref, NEG_FILL)
        mass_ref[...] = jnp.zeros_like(mass_ref)
        total_ref[...] = jnp.zeros_like(total_ref)

    def visit(head, k_ref, v_ref, visible):
        cols = slice(head * HD, (head + 1) * HD)
        state = (top_ref[head], mass_ref[head], total_ref[head])
        state = attend(q_ref[:, cols], k_ref[:, cols], v_ref[:, cols], state, visible)
        top_ref[head], mass_ref[head], total_ref[head] = state
        return state

    @pl.when(jnp.logical_and(step < steps - 1, left >= block_rows))
    def _():
        for head in range(heads):
            visit(head, kc_ref, vc_ref, None)

    @pl.when(jnp.logical_and(step < steps - 1, jnp.logical_and(left > 0, left < block_rows)))
    def _():
        visible = lax.broadcasted_iota(jnp.int32, (rows, block_rows), 1) < left
        for head in range(heads):
            visit(head, kc_ref, vc_ref, visible)

    @pl.when(step == steps - 1)
    def _():
        key_ids = lax.broadcasted_iota(jnp.int32, (rows, new_rows), 1)
        query_ids = lax.broadcasted_iota(jnp.int32, (rows, new_rows), 0) + first_query
        for head in range(heads):
            _, mass, total = visit(head, kn_ref, vn_ref, key_ids <= query_ids)
            o_ref[:, head * HD : (head + 1) * HD] = (total / mass).astype(o_ref.dtype)


def self_attention(queries, new_keys, new_values, keys, values, length, first_row, rows, group, width):
    new_rows = queries.shape[0]
    capacity = keys.shape[0]
    block_rows = min(CACHE_BLOCK, capacity)
    heads = width // HD
    blocks = capacity // block_rows
    new_spec = pl.BlockSpec((first_row + rows, width), lambda i, n: (0, group))
    cache_spec = pl.BlockSpec(
        (block_rows, width), lambda i, n: (jnp.minimum(i, (n[0] - 1) // block_rows), group)
    )
    return pl.pallas_call(
        functools.partial(self_kernel, block_rows, heads, first_row),
        grid_spec=pltpu.PrefetchScalarGridSpec(
            num_scalar_prefetch=1,
            grid=(blocks + 1,),
            in_specs=[
                pl.BlockSpec((rows, width), lambda i, n: (first_row // rows, group)),
                new_spec,
                new_spec,
                cache_spec,
                cache_spec,
            ],
            out_specs=pl.BlockSpec((rows, width), lambda i, n: (0, 0)),
            scratch_shapes=[
                pltpu.VMEM((heads, rows, HD), jnp.float32),
                pltpu.VMEM((heads, rows, HD), jnp.float32),
                pltpu.VMEM((heads, rows, HD), jnp.float32),
            ],
        ),
        out_shape=jax.ShapeDtypeStruct((rows, width), jnp.bfloat16),
        compiler_params=pltpu.CompilerParams(vmem_limit_bytes=VMEM_LIMIT),
        cost_estimate=pl.CostEstimate(
            flops=4 * rows * (capacity + new_rows) * width,
            bytes_accessed=4 * (capacity + new_rows) * width,
            transcendentals=rows * (capacity + new_rows) * heads,
        ),
        name="self_attention",
    )(length.reshape(1), queries, new_keys, new_values, keys, values)


def cross_kernel(heads, pieces_count, prompts_ref, side_ref, q_ref, near_ref, *refs):
    pieces, (own_ref, other_ref) = refs[:pieces_count], refs[pieces_count:]
    rows = q_ref.shape[0]
    span = pieces[0].shape[2]
    width = heads * HD
    first = pl.multiple_of(side_ref[0] * width, HD)
    for part in range(2):
        prompt = prompts_ref[part]
        for head in range(heads):
            cols = slice(head * HD, (head + 1) * HD)
            if part == 0:
                queries = q_ref[:, pl.ds(pl.multiple_of(first + head * HD, HD), HD)]
            else:
                queries = near_ref[:rows, cols]
            keys = jnp.concatenate([piece[0, prompt, :, cols] for piece in pieces], axis=0)
            values = jnp.concatenate([piece[1, prompt, :, cols] for piece in pieces], axis=0)
            state = (
                jnp.full((rows, HD), NEG_FILL, jnp.float32),
                jnp.zeros((rows, HD), jnp.float32),
                jnp.zeros((rows, HD), jnp.float32),
            )
            _, mass, total = attend(queries, keys, values, state, None)
            target = other_ref if part else own_ref
            target[:, cols] = (total / mass).astype(target.dtype)


def cross_attention(prompts, side, queries, near, pieces):
    rows, width = queries.shape
    half = width // 2
    scalars = pl.BlockSpec(memory_space=pltpu.SMEM)
    vmem = pl.BlockSpec(memory_space=pltpu.VMEM)
    return pl.pallas_call(
        functools.partial(cross_kernel, half // HD, len(pieces)),
        in_specs=[scalars, scalars] + [vmem] * (2 + len(pieces)),
        out_specs=[vmem, vmem],
        out_shape=[jax.ShapeDtypeStruct((rows, half), jnp.bfloat16)] * 2,
        compiler_params=pltpu.CompilerParams(vmem_limit_bytes=VMEM_LIMIT),
        name="cross_attention",
    )(prompts, side.reshape(1), queries, near, *pieces)


def pack_kernel(side_ref, prompt_ref, k_ref, v_ref, q_ref, keep_ref, give_ref, ask_ref):
    half = keep_ref.shape[3]
    kept = pl.ds(pl.multiple_of(side_ref[0] * half, HD), half)
    given = pl.ds(pl.multiple_of((1 - side_ref[0]) * half, HD), half)
    for part, source in enumerate((k_ref, v_ref)):
        keep_ref[part] = source[:, :, kept]
        give_ref[part] = source[:, :, given]
    rows = q_ref.shape[0]
    ask_ref[:rows, :] = q_ref[:, given]
    tag = jnp.full((TAG_ROWS, half), prompt_ref[0], jnp.int32)
    ask_ref[rows:, :] = tag.astype(jnp.float32).astype(ask_ref.dtype)


def pack(side, prompt_of, text_k, text_v, queries):
    prompts, text_rows, width = text_k.shape
    rows, half = queries.shape[0], width // 2
    text = jax.ShapeDtypeStruct((2, prompts, text_rows, half), text_k.dtype)
    scalars = pl.BlockSpec(memory_space=pltpu.SMEM)
    vmem = pl.BlockSpec(memory_space=pltpu.VMEM)
    return pl.pallas_call(
        pack_kernel,
        in_specs=[scalars, scalars, vmem, vmem, vmem],
        out_specs=[vmem] * 3,
        out_shape=[text, text, jax.ShapeDtypeStruct((rows + TAG_ROWS, half), queries.dtype)],
        compiler_params=pltpu.CompilerParams(vmem_limit_bytes=VMEM_LIMIT),
        name="pack",
    )(side.reshape(1), prompt_of, text_k, text_v, queries)


def whole_cross_kernel(heads, q_ref, k_ref, v_ref, o_ref):
    rows = q_ref.shape[0]
    for head in range(heads):
        cols = slice(head * HD, (head + 1) * HD)
        state = (
            jnp.full((rows, HD), NEG_FILL, jnp.float32),
            jnp.zeros((rows, HD), jnp.float32),
            jnp.zeros((rows, HD), jnp.float32),
        )
        _, mass, total = attend(q_ref[:, cols], k_ref[:, cols], v_ref[:, cols], state, None)
        o_ref[:, cols] = (total / mass).astype(o_ref.dtype)


def whole_cross(queries, prompt_of, text_k, text_v):
    keys, values = (
        lax.dynamic_index_in_dim(
            lax.all_gather(text, "req", axis=1, tiled=True), prompt_of[0], 0, keepdims=False
        )
        for text in (text_k, text_v)
    )
    return pl.pallas_call(
        functools.partial(whole_cross_kernel, queries.shape[1] // HD),
        out_shape=jax.ShapeDtypeStruct(queries.shape, jnp.bfloat16),
        compiler_params=pltpu.CompilerParams(vmem_limit_bytes=VMEM_LIMIT),
        name="whole_cross",
    )(queries, keys, values)


def project_kernel(count, groups, place_ref, *refs):
    own, near = refs[:groups], refs[groups : 2 * groups]
    refs = refs[2 * groups :]
    held, passed = refs[:count], refs[count : 2 * count]
    o_ref, weights, sems = refs[2 * count :]
    chip, holder = place_ref[0], place_ref[1]
    rows = own[0].shape[0]

    def each(choice, act):
        for step in range(count):
            act(pltpu.make_async_copy(choice[step], weights.at[step], sems.at[step]))

    @pl.when(holder == 1)
    def _():
        each(held, lambda copy: copy.start())

    @pl.when(holder == 0)
    def _():
        each(passed, lambda copy: copy.start())

    for step in range(count):
        pltpu.make_async_copy(held[step], weights.at[step], sems.at[step]).wait()
        at = chip ^ step
        for part, x_refs in enumerate((own, near)):
            x = jnp.concatenate([x_ref[...] for x_ref in x_refs], axis=1)
            o_ref[at, part * rows : (part + 1) * rows, :] = jnp.dot(
                x, weights[step], preferred_element_type=jnp.float32
            ).astype(o_ref.dtype)


def project(chip, holder, own, near, held, passed):
    count, groups = len(held), len(own)
    rows = own[0].shape[0]
    depth, columns = held[0].shape
    hbm = pl.BlockSpec(memory_space=pl.ANY)
    vmem = pl.BlockSpec(memory_space=pltpu.VMEM)
    return pl.pallas_call(
        functools.partial(project_kernel, count, groups),
        in_specs=[pl.BlockSpec(memory_space=pltpu.SMEM)] + [vmem] * (2 * groups) + [hbm] * (2 * count),
        out_specs=vmem,
        out_shape=jax.ShapeDtypeStruct((count, 2 * rows, columns), jnp.bfloat16),
        scratch_shapes=[
            pltpu.VMEM((count, depth, columns), jnp.bfloat16),
            pltpu.SemaphoreType.DMA((count,)),
        ],
        compiler_params=pltpu.CompilerParams(vmem_limit_bytes=VMEM_LIMIT),
        name="project",
    )(jnp.stack([chip, holder]).astype(jnp.int32), *own, *near, *held, *passed)


def after(value, *others):
    return lax.optimization_barrier((value, *others))[0]


def per_device(
    reqs,
    tps,
    hidden,
    q_new,
    k_new,
    v_new,
    cache_k,
    cache_v,
    cache_len,
    w_out,
    q_cross,
    text_k,
    text_v,
    prompt_of,
):
    rows, width = q_new.shape
    chips = reqs // 2
    place = lax.axis_index("req")
    chip, core = place // 2, place % 2
    side = chip % 2
    holder = core == side
    length = lax.dynamic_index_in_dim(cache_len, place, 0, keepdims=False)

    def swap(array, distance):
        return lax.ppermute(array, "req", [(i, i ^ distance) for i in range(reqs)])

    first_of = [2 * i + i % 2 for i in range(chips)]
    second_of = [2 * i + 1 - i % 2 for i in range(chips)]
    beside = lax.ppermute(
        w_out,
        "req",
        [(first_of[i], first_of[i ^ 2]) for i in range(chips)]
        + [(second_of[i], second_of[i ^ 1]) for i in range(chips)],
    )
    own_passed = lax.ppermute(w_out, "req", list(zip(first_of, second_of)))

    groups = HEAD_GROUPS if (width // HD) % HEAD_GROUPS == 0 else 1
    group_width = width // groups
    own, near = [], []
    for group in range(groups):
        queries = q_new if group == 0 else after(q_new, beside)
        own.append(
            self_attention(
                queries, k_new, v_new, cache_k[0], cache_v[0], length, 0, rows, group, group_width
            )
        )
        near.append(swap(own[-1], 2))
        if group == 0:
            beside = after(beside, own[0])
            across = lax.ppermute(
                beside, "req", [(second_of[i], second_of[i ^ 2]) for i in range(chips)]
            )
            beside_passed = swap(beside, 1)
    across_passed = lax.ppermute(across, "req", list(zip(second_of, first_of)))
    held = [w_out, beside_passed, beside, across_passed]
    passed = [own_passed, beside, beside_passed, across]
    bit = 4
    while bit < chips:
        held += [swap(block, 2 * bit) for block in held]
        passed += [swap(block, 2 * bit) for block in passed]
        bit *= 2
    terms = project(chip, holder, own, near, held, passed)
    summed = lax.psum_scatter(terms, "tp", scatter_dimension=0, tiled=True)

    def in_order(kept, received, axis):
        return jnp.where(
            side == 0,
            jnp.concatenate([kept, received], axis=axis),
            jnp.concatenate([received, kept], axis=axis),
        )

    if (width // HD) % 2 == 0:
        keep, give, ask = pack(side, prompt_of, text_k, text_v, after(q_cross, own[-1]))
        from_x = swap(give, 2)
        asked = swap(ask, 2)
        pieces = [keep, from_x]
        bit = 2
        while bit < chips:
            pieces += [swap(piece, 2 * bit) for piece in pieces]
            bit *= 2
        pieces += [swap(piece, 1) for piece in pieces]
        prompts = jnp.concatenate([prompt_of, asked[rows, :1].astype(jnp.int32)])
        mine, others = cross_attention(prompts, side, q_cross, asked, pieces)
        cross_heads = in_order(mine, swap(others, 2), 1)
    else:
        cross_heads = whole_cross(q_cross, prompt_of, text_k, text_v)

    kept, given = summed[:, :rows], summed[:, rows:]
    ordered = in_order(kept, swap(given, 2), 2).transpose(1, 0, 2).reshape(rows, width)
    hidden_out = (hidden.astype(jnp.float32) + ordered.astype(jnp.float32)).astype(jnp.bfloat16)
    return (hidden_out, cross_heads)


def solution(mesh):
    placed = (
        P("req", "tp"),
        P("req", "tp"),
        P("req", "tp"),
        P("req", "tp"),
        P("req", None, "tp"),
        P("req", None, "tp"),
        P(),
        P("tp", "req"),
        P("req", "tp"),
        P(None, "req", "tp"),
        P(None, "req", "tp"),
        P("req"),
    )
    return jax.shard_map(
        functools.partial(per_device, mesh.shape["req"], mesh.shape["tp"]),
        mesh=mesh,
        in_specs=placed,
        out_specs=(P("req", "tp"), P("req", "tp")),
        check_vma=False,
    )
```

```python
import functools

import jax
import jax.numpy as jnp
from jax import lax
from jax.experimental import pallas as pl
from jax.experimental.pallas import tpu as pltpu
from jax.sharding import PartitionSpec as P

HD = 128
CACHE_BLOCK = 1024
HEAD_GROUPS = 2
TAG_ROWS = 16
NEG_FILL = -1e30
LOG2E = 1.4426950408889634
VMEM_LIMIT = 60 * 2**20


def repeat_lanes(array, times):
    return jnp.concatenate([array] * times, axis=1) if times > 1 else array


def score(queries, keys):
    return lax.dot_general(
        queries, keys, (((1,), (1,)), ((), ())), preferred_element_type=jnp.float32
    )


def absorb(scores, values, state, visible):
    top_old, total = state
    scale = HD ** (-0.5) * LOG2E
    if visible is not None:
        scores = jnp.where(visible, scores, NEG_FILL)
    top = jnp.maximum(top_old, jnp.max(scores, axis=1, keepdims=True))
    shrink = jnp.exp2((top_old - top) * scale)
    shift = repeat_lanes(top * scale, scores.shape[1] // HD)
    weights = jnp.exp2(scores * scale - shift).astype(jnp.bfloat16)
    extended = jnp.concatenate([values, jnp.ones_like(values)], axis=1)
    total = total * repeat_lanes(shrink, 2) + jnp.dot(
        weights, extended, preferred_element_type=jnp.float32
    )
    return top, total


def empty_state(rows):
    return jnp.full((rows, HD), NEG_FILL, jnp.float32), jnp.zeros((rows, 2 * HD), jnp.float32)


def finished(total):
    return (total[:, :HD] / total[:, HD:]).astype(jnp.bfloat16)


def visit_heads(count, scores_of, use):
    ahead = scores_of(0)
    for head in range(count):
        scores = ahead
        if head + 1 < count:
            ahead = scores_of(head + 1)
        use(head, scores)


def self_kernel(
    block_rows, heads, first_query, length_ref, q_ref, kn_ref, vn_ref, kc_ref, vc_ref, o_ref,
    top_ref, total_ref,
):
    step, steps = pl.program_id(0), pl.num_programs(0)
    left = length_ref[0] - step * block_rows
    rows, new_rows = q_ref.shape[0], kn_ref.shape[0]

    @pl.when(step == 0)
    def _():
        for head in range(heads):
            top_ref[head], total_ref[head] = empty_state(rows)

    def visit(k_ref, v_ref, visible, last):
        def use(head, scores):
            cols = slice(head * HD, (head + 1) * HD)
            state = (top_ref[head], total_ref[head])
            top, total = absorb(scores, v_ref[:, cols], state, visible)
            if last:
                o_ref[:, cols] = finished(total)
            else:
                top_ref[head], total_ref[head] = top, total

        def scores_of(head):
            cols = slice(head * HD, (head + 1) * HD)
            return score(q_ref[:, cols], k_ref[:, cols])

        visit_heads(heads, scores_of, use)

    @pl.when(jnp.logical_and(step < steps - 1, left >= block_rows))
    def _():
        visit(kc_ref, vc_ref, None, False)

    @pl.when(jnp.logical_and(step < steps - 1, jnp.logical_and(left > 0, left < block_rows)))
    def _():
        visible = lax.broadcasted_iota(jnp.int32, (rows, block_rows), 1) < left
        visit(kc_ref, vc_ref, visible, False)

    @pl.when(step == steps - 1)
    def _():
        key_ids = lax.broadcasted_iota(jnp.int32, (rows, new_rows), 1)
        query_ids = lax.broadcasted_iota(jnp.int32, (rows, new_rows), 0) + first_query
        visit(kn_ref, vn_ref, key_ids <= query_ids, True)


def self_attention(queries, new_keys, new_values, keys, values, length, first_row, rows, group, width):
    new_rows = queries.shape[0]
    capacity = keys.shape[0]
    block_rows = min(CACHE_BLOCK, capacity)
    heads = width // HD
    blocks = capacity // block_rows
    new_spec = pl.BlockSpec((first_row + rows, width), lambda i, n: (0, group))
    cache_spec = pl.BlockSpec(
        (block_rows, width), lambda i, n: (jnp.minimum(i, (n[0] - 1) // block_rows), group)
    )
    return pl.pallas_call(
        functools.partial(self_kernel, block_rows, heads, first_row),
        grid_spec=pltpu.PrefetchScalarGridSpec(
            num_scalar_prefetch=1,
            grid=(blocks + 1,),
            in_specs=[
                pl.BlockSpec((rows, width), lambda i, n: (first_row // rows, group)),
                new_spec,
                new_spec,
                cache_spec,
                cache_spec,
            ],
            out_specs=pl.BlockSpec((rows, width), lambda i, n: (0, 0)),
            scratch_shapes=[
                pltpu.VMEM((heads, rows, HD), jnp.float32),
                pltpu.VMEM((heads, rows, 2 * HD), jnp.float32),
            ],
        ),
        out_shape=jax.ShapeDtypeStruct((rows, width), jnp.bfloat16),
        compiler_params=pltpu.CompilerParams(vmem_limit_bytes=VMEM_LIMIT),
        cost_estimate=pl.CostEstimate(
            flops=4 * rows * (capacity + new_rows) * width,
            bytes_accessed=4 * (capacity + new_rows) * width,
            transcendentals=rows * (capacity + new_rows) * heads,
        ),
        name="self_attention",
    )(length.reshape(1), queries, new_keys, new_values, keys, values)


def cross_kernel(heads, pieces_count, prompts_ref, side_ref, q_ref, near_ref, *refs):
    pieces, (own_ref, other_ref) = refs[:pieces_count], refs[pieces_count:]
    rows = q_ref.shape[0]
    width = heads * HD
    first = pl.multiple_of(side_ref[0] * width, HD)
    for part in range(2):
        prompt = prompts_ref[part]
        target = other_ref if part else own_ref

        def gathered(kind, head, prompt=prompt):
            cols = slice(head * HD, (head + 1) * HD)
            return jnp.concatenate([piece[kind, prompt, :, cols] for piece in pieces], axis=0)

        def scores_of(head, part=part, gathered=gathered):
            if part == 0:
                queries = q_ref[:, pl.ds(pl.multiple_of(first + head * HD, HD), HD)]
            else:
                queries = near_ref[:rows, head * HD : (head + 1) * HD]
            return score(queries, gathered(0, head))

        def use(head, scores, target=target, gathered=gathered):
            _, total = absorb(scores, gathered(1, head), empty_state(rows), None)
            target[:, head * HD : (head + 1) * HD] = finished(total)

        visit_heads(heads, scores_of, use)


def cross_attention(prompts, side, queries, near, pieces):
    rows, width = queries.shape
    half = width // 2
    scalars = pl.BlockSpec(memory_space=pltpu.SMEM)
    vmem = pl.BlockSpec(memory_space=pltpu.VMEM)
    return pl.pallas_call(
        functools.partial(cross_kernel, half // HD, len(pieces)),
        in_specs=[scalars, scalars] + [vmem] * (2 + len(pieces)),
        out_specs=[vmem, vmem],
        out_shape=[jax.ShapeDtypeStruct((rows, half), jnp.bfloat16)] * 2,
        compiler_params=pltpu.CompilerParams(vmem_limit_bytes=VMEM_LIMIT),
        name="cross_attention",
    )(prompts, side.reshape(1), queries, near, *pieces)


def pack_kernel(side_ref, prompt_ref, k_ref, v_ref, q_ref, keep_ref, give_ref, ask_ref):
    half = keep_ref.shape[3]
    kept = pl.ds(pl.multiple_of(side_ref[0] * half, HD), half)
    given = pl.ds(pl.multiple_of((1 - side_ref[0]) * half, HD), half)
    for part, source in enumerate((k_ref, v_ref)):
        keep_ref[part] = source[:, :, kept]
        give_ref[part] = source[:, :, given]
    rows = q_ref.shape[0]
    ask_ref[:rows, :] = q_ref[:, given]
    tag = jnp.full((TAG_ROWS, half), prompt_ref[0], jnp.int32)
    ask_ref[rows:, :] = tag.astype(jnp.float32).astype(ask_ref.dtype)


def pack(side, prompt_of, text_k, text_v, queries):
    prompts, text_rows, width = text_k.shape
    rows, half = queries.shape[0], width // 2
    text = jax.ShapeDtypeStruct((2, prompts, text_rows, half), text_k.dtype)
    scalars = pl.BlockSpec(memory_space=pltpu.SMEM)
    vmem = pl.BlockSpec(memory_space=pltpu.VMEM)
    return pl.pallas_call(
        pack_kernel,
        in_specs=[scalars, scalars, vmem, vmem, vmem],
        out_specs=[vmem] * 3,
        out_shape=[text, text, jax.ShapeDtypeStruct((rows + TAG_ROWS, half), queries.dtype)],
        compiler_params=pltpu.CompilerParams(vmem_limit_bytes=VMEM_LIMIT),
        name="pack",
    )(side.reshape(1), prompt_of, text_k, text_v, queries)


def whole_cross_kernel(heads, q_ref, k_ref, v_ref, o_ref):
    def scores_of(head):
        cols = slice(head * HD, (head + 1) * HD)
        return score(q_ref[:, cols], k_ref[:, cols])

    def use(head, scores):
        cols = slice(head * HD, (head + 1) * HD)
        _, total = absorb(scores, v_ref[:, cols], empty_state(q_ref.shape[0]), None)
        o_ref[:, cols] = finished(total)

    visit_heads(heads, scores_of, use)


def whole_cross(queries, prompt_of, text_k, text_v):
    keys, values = (
        lax.dynamic_index_in_dim(
            lax.all_gather(text, "req", axis=1, tiled=True), prompt_of[0], 0, keepdims=False
        )
        for text in (text_k, text_v)
    )
    return pl.pallas_call(
        functools.partial(whole_cross_kernel, queries.shape[1] // HD),
        out_shape=jax.ShapeDtypeStruct(queries.shape, jnp.bfloat16),
        compiler_params=pltpu.CompilerParams(vmem_limit_bytes=VMEM_LIMIT),
        name="whole_cross",
    )(queries, keys, values)


def project_kernel(count, groups, place_ref, *refs):
    own, near = refs[:groups], refs[groups : 2 * groups]
    refs = refs[2 * groups :]
    held, passed = refs[:count], refs[count : 2 * count]
    o_ref, weights, sems = refs[2 * count :]
    chip, holder = place_ref[0], place_ref[1]

    def each(choice, act):
        for step in range(count):
            act(pltpu.make_async_copy(choice[step], weights.at[step], sems.at[step]))

    @pl.when(holder == 1)
    def _():
        each(held, lambda copy: copy.start())

    @pl.when(holder == 0)
    def _():
        each(passed, lambda copy: copy.start())

    x = jnp.concatenate(
        [jnp.concatenate([x_ref[...] for x_ref in x_refs], axis=1) for x_refs in (own, near)], axis=0
    )
    for step in range(count):
        pltpu.make_async_copy(held[step], weights.at[step], sems.at[step]).wait()
        o_ref[chip ^ step] = jnp.dot(
            x, weights[step], preferred_element_type=jnp.float32
        ).astype(o_ref.dtype)


def project(chip, holder, own, near, held, passed):
    count, groups = len(held), len(own)
    rows = own[0].shape[0]
    depth, columns = held[0].shape
    hbm = pl.BlockSpec(memory_space=pl.ANY)
    vmem = pl.BlockSpec(memory_space=pltpu.VMEM)
    return pl.pallas_call(
        functools.partial(project_kernel, count, groups),
        in_specs=[pl.BlockSpec(memory_space=pltpu.SMEM)] + [vmem] * (2 * groups) + [hbm] * (2 * count),
        out_specs=vmem,
        out_shape=jax.ShapeDtypeStruct((count, 2 * rows, columns), jnp.bfloat16),
        scratch_shapes=[
            pltpu.VMEM((count, depth, columns), jnp.bfloat16),
            pltpu.SemaphoreType.DMA((count,)),
        ],
        compiler_params=pltpu.CompilerParams(vmem_limit_bytes=VMEM_LIMIT),
        name="project",
    )(jnp.stack([chip, holder]).astype(jnp.int32), *own, *near, *held, *passed)


def after(value, *others):
    return lax.optimization_barrier((value, *others))[0]


def per_device(
    reqs,
    tps,
    hidden,
    q_new,
    k_new,
    v_new,
    cache_k,
    cache_v,
    cache_len,
    w_out,
    q_cross,
    text_k,
    text_v,
    prompt_of,
):
    rows, width = q_new.shape
    chips = reqs // 2
    place = lax.axis_index("req")
    chip, core = place // 2, place % 2
    side = chip % 2
    holder = core == side
    length = lax.dynamic_index_in_dim(cache_len, place, 0, keepdims=False)

    def swap(array, distance):
        return lax.ppermute(array, "req", [(i, i ^ distance) for i in range(reqs)])

    first_of = [2 * i + i % 2 for i in range(chips)]
    second_of = [2 * i + 1 - i % 2 for i in range(chips)]
    beside = lax.ppermute(
        w_out,
        "req",
        [(first_of[i], first_of[i ^ 2]) for i in range(chips)]
        + [(second_of[i], second_of[i ^ 1]) for i in range(chips)],
    )
    own_passed = lax.ppermute(w_out, "req", list(zip(first_of, second_of)))

    groups = HEAD_GROUPS if (width // HD) % HEAD_GROUPS == 0 else 1
    group_width = width // groups
    own, near = [], []
    for group in range(groups):
        queries = q_new if group == 0 else after(q_new, beside)
        own.append(
            self_attention(
                queries, k_new, v_new, cache_k[0], cache_v[0], length, 0, rows, group, group_width
            )
        )
        near.append(swap(own[-1], 2))
        if group == 0:
            beside = after(beside, own[0])
            across = lax.ppermute(
                beside, "req", [(second_of[i], second_of[i ^ 2]) for i in range(chips)]
            )
            beside_passed = swap(beside, 1)
    across_passed = lax.ppermute(after(across, own[-1]), "req", list(zip(second_of, first_of)))
    held = [w_out, beside_passed, beside, across_passed]
    passed = [own_passed, beside, beside_passed, across]
    bit = 4
    while bit < chips:
        held += [swap(block, 2 * bit) for block in held]
        passed += [swap(block, 2 * bit) for block in passed]
        bit *= 2
    terms = project(chip, holder, own, near, held, passed)
    summed = lax.psum_scatter(terms, "tp", scatter_dimension=0, tiled=True)

    def in_order(kept, received, axis):
        return jnp.where(
            side == 0,
            jnp.concatenate([kept, received], axis=axis),
            jnp.concatenate([received, kept], axis=axis),
        )

    if (width // HD) % 2 == 0:
        keep, give, ask = pack(side, prompt_of, text_k, text_v, after(q_cross, own[-1]))
        from_x = swap(give, 2)
        asked = swap(ask, 2)
        pieces = [keep, from_x]
        bit = 2
        while bit < chips:
            pieces += [swap(piece, 2 * bit) for piece in pieces]
            bit *= 2
        pieces += [swap(piece, 1) for piece in pieces]
        prompts = jnp.concatenate([prompt_of, asked[rows, :1].astype(jnp.int32)])
        mine, others = cross_attention(prompts, side, q_cross, asked, pieces)
        cross_heads = in_order(mine, swap(others, 2), 1)
    else:
        cross_heads = whole_cross(q_cross, prompt_of, text_k, text_v)

    kept, given = summed[:, :rows], summed[:, rows:]
    ordered = in_order(kept, swap(given, 2), 2).transpose(1, 0, 2).reshape(rows, width)
    hidden_out = (hidden.astype(jnp.float32) + ordered.astype(jnp.float32)).astype(jnp.bfloat16)
    return (hidden_out, cross_heads)


def solution(mesh):
    placed = (
        P("req", "tp"),
        P("req", "tp"),
        P("req", "tp"),
        P("req", "tp"),
        P("req", None, "tp"),
        P("req", None, "tp"),
        P(),
        P("tp", "req"),
        P("req", "tp"),
        P(None, "req", "tp"),
        P(None, "req", "tp"),
        P("req"),
    )
    return jax.shard_map(
        functools.partial(per_device, mesh.shape["req"], mesh.shape["tp"]),
        mesh=mesh,
        in_specs=placed,
        out_specs=(P("req", "tp"), P("req", "tp")),
        check_vma=False,
    )
```

```python
import functools

import jax
import jax.numpy as jnp
from jax import lax
from jax.experimental import pallas as pl
from jax.experimental.pallas import tpu as pltpu
from jax.sharding import PartitionSpec as P

HD = 128
CACHE_BLOCK = 1024
TAG_ROWS = 16
NEG_FILL = -1e30
LOG2E = 1.4426950408889634
VMEM_LIMIT = 60 * 2**20
PEAK = 1.1535e15


def cost_of(seconds):
    return pl.CostEstimate(flops=int(seconds * PEAK), bytes_accessed=0, transcendentals=0)


def repeat_lanes(array, times):
    return jnp.concatenate([array] * times, axis=1) if times > 1 else array


def score(queries, keys):
    return lax.dot_general(
        queries, keys, (((1,), (1,)), ((), ())), preferred_element_type=jnp.float32
    )


def absorb(scores, values, state, visible):
    top_old, total = state
    scale = HD ** (-0.5) * LOG2E
    if visible is not None:
        scores = jnp.where(visible, scores, NEG_FILL)
    top = jnp.maximum(top_old, jnp.max(scores, axis=1, keepdims=True))
    shrink = jnp.exp2((top_old - top) * scale)
    shift = repeat_lanes(top * scale, scores.shape[1] // HD)
    weights = jnp.exp2(scores * scale - shift).astype(jnp.bfloat16)
    extended = jnp.concatenate([values, jnp.ones_like(values)], axis=1)
    total = total * repeat_lanes(shrink, 2) + jnp.dot(
        weights, extended, preferred_element_type=jnp.float32
    )
    return top, total


def empty_state(rows):
    return jnp.full((rows, HD), NEG_FILL, jnp.float32), jnp.zeros((rows, 2 * HD), jnp.float32)


def finished(total):
    return (total[:, :HD] / total[:, HD:]).astype(jnp.bfloat16)


def visit_heads(count, scores_of, use):
    ahead = scores_of(0)
    for head in range(count):
        scores = ahead
        if head + 1 < count:
            ahead = scores_of(head + 1)
        use(head, scores)


def self_kernel(
    block_rows, heads, length_ref, q_ref, kn_ref, vn_ref, kc_ref, vc_ref, o_ref, top_ref, total_ref
):
    step, steps = pl.program_id(0), pl.num_programs(0)
    left = length_ref[0] - step * block_rows
    rows, new_rows = q_ref.shape[0], kn_ref.shape[0]

    @pl.when(step == 0)
    def _():
        for head in range(heads):
            top_ref[head], total_ref[head] = empty_state(rows)

    def visit(k_ref, v_ref, visible, last):
        def use(head, scores):
            cols = slice(head * HD, (head + 1) * HD)
            state = (top_ref[head], total_ref[head])
            top, total = absorb(scores, v_ref[:, cols], state, visible)
            if last:
                o_ref[:, cols] = finished(total)
            else:
                top_ref[head], total_ref[head] = top, total

        def scores_of(head):
            cols = slice(head * HD, (head + 1) * HD)
            return score(q_ref[:, cols], k_ref[:, cols])

        visit_heads(heads, scores_of, use)

    @pl.when(jnp.logical_and(step < steps - 1, left >= block_rows))
    def _():
        visit(kc_ref, vc_ref, None, False)

    @pl.when(jnp.logical_and(step < steps - 1, jnp.logical_and(left > 0, left < block_rows)))
    def _():
        visible = lax.broadcasted_iota(jnp.int32, (rows, block_rows), 1) < left
        visit(kc_ref, vc_ref, visible, False)

    @pl.when(step == steps - 1)
    def _():
        key_ids = lax.broadcasted_iota(jnp.int32, (rows, new_rows), 1)
        query_ids = lax.broadcasted_iota(jnp.int32, (rows, new_rows), 0)
        visit(kn_ref, vn_ref, key_ids <= query_ids, True)


def self_attention(queries, new_keys, new_values, keys, values, length):
    rows, width = queries.shape
    new_rows, capacity = new_keys.shape[0], keys.shape[0]
    block_rows = min(CACHE_BLOCK, capacity)
    heads = width // HD
    whole = pl.BlockSpec((rows, width), lambda i, n: (0, 0))
    new = pl.BlockSpec((new_rows, width), lambda i, n: (0, 0))
    cached = pl.BlockSpec(
        (block_rows, width), lambda i, n: (jnp.minimum(i, (n[0] - 1) // block_rows), 0)
    )
    return pl.pallas_call(
        functools.partial(self_kernel, block_rows, heads),
        grid_spec=pltpu.PrefetchScalarGridSpec(
            num_scalar_prefetch=1,
            grid=(capacity // block_rows + 1,),
            in_specs=[whole, new, new, cached, cached],
            out_specs=whole,
            scratch_shapes=[
                pltpu.VMEM((heads, rows, HD), jnp.float32),
                pltpu.VMEM((heads, rows, 2 * HD), jnp.float32),
            ],
        ),
        out_shape=jax.ShapeDtypeStruct((rows, width), jnp.bfloat16),
        compiler_params=pltpu.CompilerParams(vmem_limit_bytes=VMEM_LIMIT),
        cost_estimate=cost_of(20e-6),
        name="self_attention",
    )(length.reshape(1), queries, new_keys, new_values, keys, values)


def cross_kernel(heads, pieces_count, spans, prompts_ref, side_ref, q_ref, near_ref, *refs):
    pieces, (own_ref, other_ref) = refs[:pieces_count], refs[pieces_count:]
    rows = q_ref.shape[0]
    width = heads * HD
    first = pl.multiple_of(side_ref[0] * width, HD)
    asked = 2 * spans[0] * spans[1]
    for part in range(2):
        prompt = prompts_ref[part]
        target = other_ref if part else own_ref

        def gathered(kind, head, prompt=prompt):
            cols = slice(head * HD, (head + 1) * HD)
            count, text_rows = spans
            at = pl.ds(pl.multiple_of((kind * count + prompt) * text_rows, text_rows), text_rows)
            return jnp.concatenate([piece[at, cols] for piece in pieces], axis=0)

        def scores_of(head, part=part, gathered=gathered):
            if part == 0:
                queries = q_ref[:, pl.ds(pl.multiple_of(first + head * HD, HD), HD)]
            else:
                queries = near_ref[asked : asked + rows, head * HD : (head + 1) * HD]
            return score(queries, gathered(0, head))

        def use(head, scores, target=target, gathered=gathered):
            _, total = absorb(scores, gathered(1, head), empty_state(rows), None)
            target[:, head * HD : (head + 1) * HD] = finished(total)

        visit_heads(heads, scores_of, use)


def cross_attention(prompts, side, queries, near, pieces, spans):
    rows, width = queries.shape
    half = width // 2
    scalars = pl.BlockSpec(memory_space=pltpu.SMEM)
    vmem = pl.BlockSpec(memory_space=pltpu.VMEM)
    return pl.pallas_call(
        functools.partial(cross_kernel, half // HD, len(pieces), spans),
        in_specs=[scalars, scalars] + [vmem] * (2 + len(pieces)),
        out_specs=[vmem, vmem],
        out_shape=[jax.ShapeDtypeStruct((rows, half), jnp.bfloat16)] * 2,
        compiler_params=pltpu.CompilerParams(vmem_limit_bytes=VMEM_LIMIT),
        cost_estimate=cost_of(0),
        name="cross_attention",
    )(prompts, side.reshape(1), queries, near, *pieces)


def prompts_kernel(prompt_ref, tag_ref, *refs):
    refs[-1][0] = prompt_ref[0]
    refs[-1][1] = jnp.max(tag_ref[...].astype(jnp.float32)).astype(jnp.int32)


def read_prompts(prompt_of, asked, gates):
    rows, half = asked.shape
    scalars = pl.BlockSpec(memory_space=pltpu.SMEM)
    return pl.pallas_call(
        prompts_kernel,
        grid=(1,),
        in_specs=[scalars, pl.BlockSpec((TAG_ROWS, half), lambda i: (rows // TAG_ROWS - 1, 0))]
        + [pl.BlockSpec(memory_space=pl.ANY)] * len(gates),
        out_specs=scalars,
        out_shape=jax.ShapeDtypeStruct((2,), jnp.int32),
        cost_estimate=cost_of(100e-6),
        name="read_prompts",
    )(prompt_of, asked, *gates)


def pack_kernel(side_ref, prompt_ref, k_ref, v_ref, q_ref, keep_ref, give_ref, ask_ref):
    half = keep_ref.shape[1]
    prompts, text_rows, _ = k_ref.shape
    kept = pl.ds(pl.multiple_of(side_ref[0] * half, HD), half)
    given = pl.ds(pl.multiple_of((1 - side_ref[0]) * half, HD), half)
    for part, source in enumerate((k_ref, v_ref)):
        for prompt in range(prompts):
            first = (part * prompts + prompt) * text_rows
            at = slice(first, first + text_rows)
            keep_ref[at, :] = source[prompt, :, kept]
            give_ref[at, :] = source[prompt, :, given]
            ask_ref[at, :] = source[prompt, :, given]
    first, rows = give_ref.shape[0], q_ref.shape[0]
    ask_ref[first : first + rows, :] = q_ref[:, given]
    tag = jnp.full((TAG_ROWS, half), prompt_ref[0], jnp.int32)
    ask_ref[first + rows :, :] = tag.astype(jnp.float32).astype(ask_ref.dtype)


def pack(side, prompt_of, text_k, text_v, queries):
    prompts, text_rows, width = text_k.shape
    rows, half = queries.shape[0], width // 2
    text = jax.ShapeDtypeStruct((2 * prompts * text_rows, half), text_k.dtype)
    ask = jax.ShapeDtypeStruct((text.shape[0] + rows + TAG_ROWS, half), queries.dtype)
    scalars = pl.BlockSpec(memory_space=pltpu.SMEM)
    vmem = pl.BlockSpec(memory_space=pltpu.VMEM)
    return pl.pallas_call(
        pack_kernel,
        in_specs=[scalars, scalars, vmem, vmem, vmem],
        out_specs=[vmem] * 3,
        out_shape=[text, text, ask],
        compiler_params=pltpu.CompilerParams(vmem_limit_bytes=VMEM_LIMIT),
        cost_estimate=cost_of(3e-6),
        name="pack",
    )(side.reshape(1), prompt_of, text_k, text_v, queries)


def whole_cross_kernel(heads, q_ref, k_ref, v_ref, o_ref):
    def scores_of(head):
        cols = slice(head * HD, (head + 1) * HD)
        return score(q_ref[:, cols], k_ref[:, cols])

    def use(head, scores):
        cols = slice(head * HD, (head + 1) * HD)
        _, total = absorb(scores, v_ref[:, cols], empty_state(q_ref.shape[0]), None)
        o_ref[:, cols] = finished(total)

    visit_heads(heads, scores_of, use)


def whole_cross(queries, prompt_of, text_k, text_v):
    keys, values = (
        lax.dynamic_index_in_dim(
            lax.all_gather(text, "req", axis=1, tiled=True), prompt_of[0], 0, keepdims=False
        )
        for text in (text_k, text_v)
    )
    return pl.pallas_call(
        functools.partial(whole_cross_kernel, queries.shape[1] // HD),
        out_shape=jax.ShapeDtypeStruct(queries.shape, jnp.bfloat16),
        compiler_params=pltpu.CompilerParams(vmem_limit_bytes=VMEM_LIMIT),
        name="whole_cross",
    )(queries, keys, values)


def project_kernel(count, span, places, place_ref, own_ref, near_ref, *refs):
    held, passed = refs[:count], refs[count : 2 * count]
    outs = refs[2 * count : 2 * count + places]
    x_ref, weights, terms, x_sems, sems, out_sems = refs[2 * count + places :]
    chip, holder, at_tp = place_ref[0], place_ref[1], place_ref[2]
    rows, columns = own_ref.shape[0], held[0].shape[1]
    blocks = outs[0].shape[1]

    def rows_in(part):
        source = (near_ref, own_ref)[part]
        return pltpu.make_async_copy(
            source, x_ref.at[part * rows : (part + 1) * rows], x_sems.at[part]
        )

    def weights_in(choice, at):
        first = (at % span) * columns
        place = weights.at[at // span, :, first : first + columns]
        return pltpu.make_async_copy(choice[at], place, sems.at[at])

    def terms_out(at, distance, block):
        return pltpu.make_async_copy(terms.at[at], outs[distance].at[:, block], out_sems.at[at])

    for part in range(2):
        rows_in(part).start()

    @pl.when(holder == 1)
    def _():
        for at in range(count):
            weights_in(held, at).start()

    @pl.when(holder == 0)
    def _():
        for at in range(count):
            weights_in(passed, at).start()

    for part in range(2):
        rows_in(part).wait()
    for first in range(0, count, span):
        for at in range(first, first + span):
            weights_in(held, at).wait()
        product = jnp.dot(
            x_ref[...], weights[first // span], preferred_element_type=jnp.float32
        ).astype(terms.dtype)
        for at in range(first, first + span):
            cols = slice((at - first) * columns, (at - first + 1) * columns)
            source = chip ^ at
            block = lax.rem(source, blocks)
            away = lax.div(source, blocks) ^ at_tp
            for part in range(2):
                terms[at, part] = product[part * rows : (part + 1) * rows, cols]
            for distance in range(places):

                @pl.when(away == distance)
                def _(at=at, distance=distance, block=block):
                    terms_out(at, distance, block).start()

    for at in range(count):
        terms_out(at, 0, 0).wait()


def project(tps, place, own, near, held, passed):
    rows = own.shape[0]
    depth, columns = held[0].shape
    count = len(held)
    span = 2 if columns % HD == 0 else 1
    hbm = pl.BlockSpec(memory_space=pl.ANY)
    out = jax.ShapeDtypeStruct((2, count // tps, rows, columns), jnp.bfloat16)
    return pl.pallas_call(
        functools.partial(project_kernel, count, span, tps),
        in_specs=[pl.BlockSpec(memory_space=pltpu.SMEM)] + [hbm] * (2 + 2 * count),
        out_specs=[hbm] * tps,
        out_shape=[out] * tps,
        scratch_shapes=[
            pltpu.VMEM((2 * rows, depth), jnp.bfloat16),
            pltpu.VMEM((count // span, depth, span * columns), jnp.bfloat16),
            pltpu.VMEM((count, 2, rows, columns), jnp.bfloat16),
            pltpu.SemaphoreType.DMA((2,)),
            pltpu.SemaphoreType.DMA((count,)),
            pltpu.SemaphoreType.DMA((count,)),
        ],
        compiler_params=pltpu.CompilerParams(vmem_limit_bytes=VMEM_LIMIT),
        cost_estimate=cost_of(10e-6),
        name="project",
    )(place, own, near, *held, *passed)


def add_kernel(count, *refs):
    outs, (scratch, sems) = refs[count:-2], refs[-2:]
    copies = [
        pltpu.make_async_copy(refs[at], scratch.at[at], sems.at[at]) for at in range(count)
    ]
    for copy in copies:
        copy.start()
    for copy in copies:
        copy.wait()
    total = scratch[0].astype(jnp.float32)
    for at in range(1, count):
        total += scratch[at].astype(jnp.float32)
    total = total.astype(scratch.dtype)
    if len(outs) == 1:
        outs[0][...] = total
    else:
        for at, out in enumerate(outs):
            out[...] = total[at]


def add(*terms, parted=True):
    hbm = pl.BlockSpec(memory_space=pl.ANY)
    vmem = pl.BlockSpec(memory_space=pltpu.VMEM)
    shape, dtype = terms[0].shape, terms[0].dtype
    return pl.pallas_call(
        functools.partial(add_kernel, len(terms)),
        in_specs=[hbm] * len(terms),
        out_specs=[vmem] * shape[0] if parted else vmem,
        out_shape=(
            [jax.ShapeDtypeStruct(shape[1:], dtype)] * shape[0]
            if parted
            else jax.ShapeDtypeStruct(shape, dtype)
        ),
        scratch_shapes=[
            pltpu.VMEM((len(terms),) + shape, dtype),
            pltpu.SemaphoreType.DMA((len(terms),)),
        ],
        compiler_params=pltpu.CompilerParams(vmem_limit_bytes=VMEM_LIMIT),
        cost_estimate=cost_of(2e-6),
        name="add",
    )(*terms)


def to_tp(value, pairs):
    return lax.ppermute(value, "tp", pairs)


def apart(tps, distance):
    return [(i, i ^ distance) for i in range(tps)]


def after(value, *others):
    return lax.optimization_barrier((value, *others))[0]


def per_device(
    reqs,
    tps,
    hidden,
    q_new,
    k_new,
    v_new,
    cache_k,
    cache_v,
    cache_len,
    w_out,
    q_cross,
    text_k,
    text_v,
    prompt_of,
):
    rows, width = q_new.shape
    chips = reqs // 2
    place = lax.axis_index("req")
    chip, core = place // 2, place % 2
    side = chip % 2
    text_side = (chip // 2) % 2
    holder = core == side
    length = lax.dynamic_index_in_dim(cache_len, place, 0, keepdims=False)

    def swap(array, distance):
        return lax.ppermute(array, "req", [(i, i ^ distance) for i in range(reqs)])

    first_of = [2 * i + i % 2 for i in range(chips)]
    second_of = [2 * i + 1 - i % 2 for i in range(chips)]
    beside = lax.ppermute(
        w_out,
        "req",
        [(first_of[i], first_of[i ^ 2]) for i in range(chips)]
        + [(second_of[i], second_of[i ^ 1]) for i in range(chips)],
    )
    own_passed = lax.ppermute(w_out, "req", list(zip(first_of, second_of)))

    own = self_attention(q_new, k_new, v_new, cache_k[0], cache_v[0], length)
    near = swap(own, 2)
    beside = after(beside, own)
    across = lax.ppermute(
        beside, "req", [(second_of[i], second_of[i ^ 2]) for i in range(chips)]
    )
    beside_passed = swap(beside, 1)
    split_heads = (width // HD) % 2 == 0
    if split_heads:
        keep, give, ask = pack(text_side, prompt_of, text_k, text_v, after(q_cross, own))
        across = after(across, keep)
        give, keep, ask = after((give, keep, ask), near)
        asked = swap(ask, 4)
        if chips == 4:
            pieces = [keep, asked, swap(keep, 2), swap(give, 6)]
        else:
            pieces = [keep, asked[: give.shape[0]]]
            for bit in range(chips.bit_length() - 1):
                if bit != 1:
                    pieces += [swap(piece, 2 << bit) for piece in pieces]
        spans = text_k.shape[:2]
        prompts = read_prompts(prompt_of, asked, pieces[2:])

    across_passed = lax.ppermute(after(across, near), "req", list(zip(second_of, first_of)))
    held = [w_out, beside_passed, beside, across_passed]
    passed = [own_passed, beside, beside_passed, across]
    bit = 4
    while bit < chips:
        held += [swap(block, 2 * bit) for block in held]
        passed += [swap(block, 2 * bit) for block in passed]
        bit *= 2
    at = lax.axis_index("tp")
    order = jnp.stack([chip, holder, at]).astype(jnp.int32)

    terms = project(tps, order, own, near, held, passed)

    if split_heads and tps == 4 and chips == 4:
        far = to_tp(terms[3], [(0, 1), (3, 2)])
        inner = to_tp(terms[3], [(1, 2), (2, 1)])
        joined = add(terms[2], after(far, inner, prompts), parted=False)
        crossing = to_tp(joined, apart(4, 2))
        outer, pieces = after((terms[1], pieces), joined)
        outer = to_tp(outer, apart(4, 1))
        pieces += [swap(piece, 1) for piece in pieces]
        mine, others = cross_attention(prompts, text_side, q_cross, asked, pieces, spans)
        outer, crossing = after((outer, crossing), mine)
        given, kept = add(terms[0], inner, outer, crossing)
    else:
        given, kept = add(terms[0], *[to_tp(terms[d], apart(tps, d)) for d in range(1, tps)])
        if split_heads:
            pieces += [swap(piece, 1) for piece in pieces]
            mine, others = cross_attention(prompts, text_side, q_cross, asked, pieces, spans)

    def in_order(side, kept, received, axis):
        return jnp.where(
            side == 0,
            jnp.concatenate([kept, received], axis=axis),
            jnp.concatenate([received, kept], axis=axis),
        )

    if split_heads:
        cross_heads = in_order(text_side, mine, swap(others, 4), 1)
    else:
        cross_heads = whole_cross(q_cross, prompt_of, text_k, text_v)

    ordered = in_order(side, kept, swap(given, 2), 2).transpose(1, 0, 2).reshape(rows, width)
    hidden_out = (hidden.astype(jnp.float32) + ordered.astype(jnp.float32)).astype(jnp.bfloat16)
    return (hidden_out, cross_heads)


def solution(mesh):
    placed = (
        P("req", "tp"),
        P("req", "tp"),
        P("req", "tp"),
        P("req", "tp"),
        P("req", None, "tp"),
        P("req", None, "tp"),
        P(),
        P("tp", "req"),
        P("req", "tp"),
        P(None, "req", "tp"),
        P(None, "req", "tp"),
        P("req"),
    )
    return jax.shard_map(
        functools.partial(per_device, mesh.shape["req"], mesh.shape["tp"]),
        mesh=mesh,
        in_specs=placed,
        out_specs=(P("req", "tp"), P("req", "tp")),
        check_vma=False,
    )
```

```python
import functools

import jax
import jax.numpy as jnp
from jax import lax
from jax.experimental import pallas as pl
from jax.experimental.pallas import tpu as pltpu
from jax.sharding import PartitionSpec as P

HD = 128
CACHE_BLOCK = 1024
TAG_ROWS = 16
NEG_FILL = -1e30
LOG2E = 1.4426950408889634
VMEM_LIMIT = 64 * 2**20 - 2**17
PEAK = 1.1535e15


def cost_of(seconds):
    return pl.CostEstimate(flops=int(seconds * PEAK), bytes_accessed=0, transcendentals=0)


def repeat_lanes(array, times):
    return jnp.concatenate([array] * times, axis=1) if times > 1 else array


def score(queries, keys):
    return lax.dot_general(
        queries, keys, (((1,), (1,)), ((), ())), preferred_element_type=jnp.float32
    )


def absorb(scores, values, state, visible):
    top_old, total = state
    scale = HD ** (-0.5) * LOG2E
    if visible is not None:
        scores = jnp.where(visible, scores, NEG_FILL)
    top = jnp.maximum(top_old, jnp.max(scores, axis=1, keepdims=True))
    shrink = jnp.exp2((top_old - top) * scale)
    shift = repeat_lanes(top * scale, scores.shape[1] // HD)
    weights = jnp.exp2(scores * scale - shift).astype(jnp.bfloat16)
    extended = jnp.concatenate([values, jnp.ones_like(values)], axis=1)
    total = total * repeat_lanes(shrink, 2) + jnp.dot(
        weights, extended, preferred_element_type=jnp.float32
    )
    return top, total


def empty_state(rows):
    return jnp.full((rows, HD), NEG_FILL, jnp.float32), jnp.zeros((rows, 2 * HD), jnp.float32)


def finished(total):
    return (total[:, :HD] / total[:, HD:]).astype(jnp.bfloat16)


def visit_heads(count, scores_of, use):
    ahead = scores_of(0)
    for head in range(count):
        scores = ahead
        if head + 1 < count:
            ahead = scores_of(head + 1)
        use(head, scores)


def self_kernel(
    block_rows, heads, length_ref, q_ref, kn_ref, vn_ref, kc_ref, vc_ref, o_ref, top_ref, total_ref
):
    step, steps = pl.program_id(0), pl.num_programs(0)
    left = length_ref[0] - step * block_rows
    rows, new_rows = q_ref.shape[0], kn_ref.shape[0]

    @pl.when(step == 0)
    def _():
        for head in range(heads):
            top_ref[head], total_ref[head] = empty_state(rows)

    def visit(k_ref, v_ref, visible, last):
        def use(head, scores):
            cols = slice(head * HD, (head + 1) * HD)
            state = (top_ref[head], total_ref[head])
            top, total = absorb(scores, v_ref[:, cols], state, visible)
            if last:
                o_ref[:, cols] = finished(total)
            else:
                top_ref[head], total_ref[head] = top, total

        def scores_of(head):
            cols = slice(head * HD, (head + 1) * HD)
            return score(q_ref[:, cols], k_ref[:, cols])

        visit_heads(heads, scores_of, use)

    @pl.when(jnp.logical_and(step < steps - 1, left >= block_rows))
    def _():
        visit(kc_ref, vc_ref, None, False)

    @pl.when(jnp.logical_and(step < steps - 1, jnp.logical_and(left > 0, left < block_rows)))
    def _():
        visible = lax.broadcasted_iota(jnp.int32, (rows, block_rows), 1) < left
        visit(kc_ref, vc_ref, visible, False)

    @pl.when(step == steps - 1)
    def _():
        key_ids = lax.broadcasted_iota(jnp.int32, (rows, new_rows), 1)
        query_ids = lax.broadcasted_iota(jnp.int32, (rows, new_rows), 0)
        visit(kn_ref, vn_ref, key_ids <= query_ids, True)


def self_attention(queries, new_keys, new_values, keys, values, length):
    rows, width = queries.shape
    new_rows, capacity = new_keys.shape[0], keys.shape[0]
    block_rows = min(CACHE_BLOCK, capacity)
    heads = width // HD
    whole = pl.BlockSpec((rows, width), lambda i, n: (0, 0))
    new = pl.BlockSpec((new_rows, width), lambda i, n: (0, 0))
    cached = pl.BlockSpec(
        (block_rows, width), lambda i, n: (jnp.minimum(i, (n[0] - 1) // block_rows), 0)
    )
    return pl.pallas_call(
        functools.partial(self_kernel, block_rows, heads),
        grid_spec=pltpu.PrefetchScalarGridSpec(
            num_scalar_prefetch=1,
            grid=(capacity // block_rows + 1,),
            in_specs=[whole, new, new, cached, cached],
            out_specs=whole,
            scratch_shapes=[
                pltpu.VMEM((heads, rows, HD), jnp.float32),
                pltpu.VMEM((heads, rows, 2 * HD), jnp.float32),
            ],
        ),
        out_shape=jax.ShapeDtypeStruct((rows, width), jnp.bfloat16),
        compiler_params=pltpu.CompilerParams(vmem_limit_bytes=VMEM_LIMIT),
        cost_estimate=cost_of(20e-6),
        name="self_attention",
    )(length.reshape(1), queries, new_keys, new_values, keys, values)


def cross_kernel(heads, pieces_count, spans, prompts_ref, side_ref, q_ref, near_ref, *refs):
    pieces, (own_ref, other_ref) = refs[:pieces_count], refs[pieces_count:]
    rows = q_ref.shape[0]
    width = heads * HD
    first = pl.multiple_of(side_ref[0] * width, HD)
    asked = 2 * spans[0] * spans[1]
    for part in range(2):
        prompt = prompts_ref[part]
        target = other_ref if part else own_ref

        def gathered(kind, head, prompt=prompt):
            cols = slice(head * HD, (head + 1) * HD)
            count, text_rows = spans
            at = pl.ds(pl.multiple_of((kind * count + prompt) * text_rows, text_rows), text_rows)
            return jnp.concatenate([piece[at, cols] for piece in pieces], axis=0)

        def scores_of(head, part=part, gathered=gathered):
            if part == 0:
                queries = q_ref[:, pl.ds(pl.multiple_of(first + head * HD, HD), HD)]
            else:
                queries = near_ref[asked : asked + rows, head * HD : (head + 1) * HD]
            return score(queries, gathered(0, head))

        def use(head, scores, target=target, gathered=gathered):
            _, total = absorb(scores, gathered(1, head), empty_state(rows), None)
            target[:, head * HD : (head + 1) * HD] = finished(total)

        visit_heads(heads, scores_of, use)


def cross_attention(prompts, side, queries, near, pieces, spans):
    rows, width = queries.shape
    half = width // 2
    scalars = pl.BlockSpec(memory_space=pltpu.SMEM)
    vmem = pl.BlockSpec(memory_space=pltpu.VMEM)
    return pl.pallas_call(
        functools.partial(cross_kernel, half // HD, len(pieces), spans),
        in_specs=[scalars, scalars] + [vmem] * (2 + len(pieces)),
        out_specs=[vmem, vmem],
        out_shape=[jax.ShapeDtypeStruct((rows, half), jnp.bfloat16)] * 2,
        compiler_params=pltpu.CompilerParams(vmem_limit_bytes=VMEM_LIMIT),
        cost_estimate=cost_of(0),
        name="cross_attention",
    )(prompts, side.reshape(1), queries, near, *pieces)


def prompts_kernel(prompt_ref, tag_ref, *refs):
    refs[-1][0] = prompt_ref[0]
    refs[-1][1] = jnp.max(tag_ref[...].astype(jnp.float32)).astype(jnp.int32)


def read_prompts(prompt_of, asked, gates):
    rows, half = asked.shape
    scalars = pl.BlockSpec(memory_space=pltpu.SMEM)
    return pl.pallas_call(
        prompts_kernel,
        grid=(1,),
        in_specs=[scalars, pl.BlockSpec((TAG_ROWS, half), lambda i: (rows // TAG_ROWS - 1, 0))]
        + [pl.BlockSpec(memory_space=pl.ANY)] * len(gates),
        out_specs=scalars,
        out_shape=jax.ShapeDtypeStruct((2,), jnp.int32),
        cost_estimate=cost_of(100e-6),
        name="read_prompts",
    )(prompt_of, asked, *gates)


def gate_kernel(value_ref, *refs):
    refs[-1][0] = value_ref[0]


def gate(value, *waited):
    scalars = pl.BlockSpec(memory_space=pltpu.SMEM)
    return pl.pallas_call(
        gate_kernel,
        in_specs=[scalars] + [pl.BlockSpec(memory_space=pltpu.HBM)] * len(waited),
        out_specs=scalars,
        out_shape=jax.ShapeDtypeStruct((1,), jnp.int32),
        cost_estimate=cost_of(100e-6),
        name="gate",
    )(value.reshape(1), *waited)[0]


def pack_kernel(side_ref, prompt_ref, k_ref, v_ref, q_ref, keep_ref, give_ref, ask_ref):
    half = keep_ref.shape[1]
    prompts, text_rows, _ = k_ref.shape
    kept = pl.ds(pl.multiple_of(side_ref[0] * half, HD), half)
    given = pl.ds(pl.multiple_of((1 - side_ref[0]) * half, HD), half)
    for part, source in enumerate((k_ref, v_ref)):
        for prompt in range(prompts):
            first = (part * prompts + prompt) * text_rows
            at = slice(first, first + text_rows)
            keep_ref[at, :] = source[prompt, :, kept]
            give_ref[at, :] = source[prompt, :, given]
            ask_ref[at, :] = source[prompt, :, given]
    first, rows = give_ref.shape[0], q_ref.shape[0]
    ask_ref[first : first + rows, :] = q_ref[:, given]
    tag = jnp.full((TAG_ROWS, half), prompt_ref[0], jnp.int32)
    ask_ref[first + rows :, :] = tag.astype(jnp.float32).astype(ask_ref.dtype)


def pack(side, prompt_of, text_k, text_v, queries):
    prompts, text_rows, width = text_k.shape
    rows, half = queries.shape[0], width // 2
    text = jax.ShapeDtypeStruct((2 * prompts * text_rows, half), text_k.dtype)
    ask = jax.ShapeDtypeStruct((text.shape[0] + rows + TAG_ROWS, half), queries.dtype)
    scalars = pl.BlockSpec(memory_space=pltpu.SMEM)
    vmem = pl.BlockSpec(memory_space=pltpu.VMEM)
    return pl.pallas_call(
        pack_kernel,
        in_specs=[scalars, scalars, vmem, vmem, vmem],
        out_specs=[vmem] * 3,
        out_shape=[text, text, ask],
        compiler_params=pltpu.CompilerParams(vmem_limit_bytes=VMEM_LIMIT),
        cost_estimate=cost_of(3e-6),
        name="pack",
    )(side.reshape(1), prompt_of, text_k, text_v, queries)


def whole_cross_kernel(heads, q_ref, k_ref, v_ref, o_ref):
    def scores_of(head):
        cols = slice(head * HD, (head + 1) * HD)
        return score(q_ref[:, cols], k_ref[:, cols])

    def use(head, scores):
        cols = slice(head * HD, (head + 1) * HD)
        _, total = absorb(scores, v_ref[:, cols], empty_state(q_ref.shape[0]), None)
        o_ref[:, cols] = finished(total)

    visit_heads(heads, scores_of, use)


def whole_cross(queries, prompt_of, text_k, text_v):
    keys, values = (
        lax.dynamic_index_in_dim(
            lax.all_gather(text, "req", axis=1, tiled=True), prompt_of[0], 0, keepdims=False
        )
        for text in (text_k, text_v)
    )
    return pl.pallas_call(
        functools.partial(whole_cross_kernel, queries.shape[1] // HD),
        out_shape=jax.ShapeDtypeStruct(queries.shape, jnp.bfloat16),
        compiler_params=pltpu.CompilerParams(vmem_limit_bytes=VMEM_LIMIT),
        name="whole_cross",
    )(queries, keys, values)


def project_kernel(count, span, places, joint, place_ref, own_ref, near_ref, *refs):
    held, passed = refs[:count], refs[count : 2 * count]
    outs = refs[2 * count : -6]
    x_ref, weights, terms, x_sems, sems, out_sems = refs[-6:]
    chip, holder, at_tp = place_ref[0], place_ref[1], place_ref[2]
    rows, columns = own_ref.shape[0], held[0].shape[1]
    blocks = outs[0].shape[0]
    if joint:
        outs = (*outs[: places - 1], outs[-1].at[0], *outs[places - 1 : -1], outs[-1].at[1])

    def rows_in(part):
        source = (near_ref, own_ref)[part]
        return pltpu.make_async_copy(
            source, x_ref.at[part * rows : (part + 1) * rows], x_sems.at[part]
        )

    def weights_in(choice, at):
        first = (at % span) * columns
        place = weights.at[at // span, :, first : first + columns]
        return pltpu.make_async_copy(choice[at], place, sems.at[at])

    def terms_out(at, part, distance, block):
        target = outs[part * places + distance].at[block]
        return pltpu.make_async_copy(terms.at[at, part], target, out_sems.at[at, part])

    for part in range(2):
        rows_in(part).start()

    @pl.when(holder == 1)
    def _():
        for at in range(count):
            weights_in(held, at).start()

    @pl.when(holder == 0)
    def _():
        for at in range(count):
            weights_in(passed, at).start()

    for part in range(2):
        rows_in(part).wait()
    for first in range(0, count, span):
        for at in range(first, first + span):
            weights_in(held, at).wait()
        product = jnp.dot(
            x_ref[...], weights[first // span], preferred_element_type=jnp.float32
        ).astype(terms.dtype)
        for at in range(first, first + span):
            cols = slice((at - first) * columns, (at - first + 1) * columns)
            source = chip ^ at
            block = lax.rem(source, blocks)
            away = lax.div(source, blocks) ^ at_tp
            for part in range(2):
                terms[at, part] = product[part * rows : (part + 1) * rows, cols]
            for distance in range(places):

                @pl.when(away == distance)
                def _(at=at, distance=distance, block=block):
                    for part in range(2):
                        terms_out(at, part, distance, block).start()

    for at in range(count):
        for part in range(2):
            terms_out(at, part, 0, 0).wait()


def project(tps, place, own, near, held, passed, joint):
    rows = own.shape[0]
    depth, columns = held[0].shape
    count = len(held)
    span = 2 if columns % HD == 0 else 1
    hbm = pl.BlockSpec(memory_space=pltpu.HBM)
    out = jax.ShapeDtypeStruct((count // tps, rows, columns), jnp.bfloat16)
    return pl.pallas_call(
        functools.partial(project_kernel, count, span, tps, joint),
        in_specs=[pl.BlockSpec(memory_space=pltpu.SMEM)] + [hbm] * (2 + 2 * count),
        out_specs=[hbm] * (2 * tps - joint),
        out_shape=(
            [out] * (2 * tps - 2) + [jax.ShapeDtypeStruct((2, *out.shape), out.dtype)]
            if joint
            else [out] * (2 * tps)
        ),
        scratch_shapes=[
            pltpu.VMEM((2 * rows, depth), jnp.bfloat16),
            pltpu.VMEM((count // span, depth, span * columns), jnp.bfloat16),
            pltpu.VMEM((count, 2, rows, columns), jnp.bfloat16),
            pltpu.SemaphoreType.DMA((2,)),
            pltpu.SemaphoreType.DMA((count,)),
            pltpu.SemaphoreType.DMA((count, 2)),
        ],
        compiler_params=pltpu.CompilerParams(vmem_limit_bytes=VMEM_LIMIT),
        cost_estimate=cost_of(10e-6),
        name="project",
    )(place, own, near, *held, *passed)


def fetch(sources, scratch, sems):
    copies = [
        pltpu.make_async_copy(source, scratch.at[at], sems.at[at])
        for at, source in enumerate(sources)
    ]
    for copy in copies:
        copy.start()
    for copy in copies:
        copy.wait()
    return [scratch[at].astype(jnp.float32) for at in range(len(copies))]


def add_kernel(halves, *refs):
    out, scratch, sems = refs[-3:]
    sources = [ref if half is None else ref.at[half] for ref, half in zip(refs, halves)]
    out[...] = sum(fetch(sources, scratch, sems)).astype(out.dtype)


def add(*terms):
    halves = tuple(term[1] if isinstance(term, tuple) else None for term in terms)
    terms = [term[0] if isinstance(term, tuple) else term for term in terms]
    shape, dtype = terms[0].shape, terms[0].dtype
    return pl.pallas_call(
        functools.partial(add_kernel, halves),
        in_specs=[pl.BlockSpec(memory_space=pltpu.HBM)] * len(terms),
        out_specs=pl.BlockSpec(memory_space=pltpu.VMEM),
        out_shape=jax.ShapeDtypeStruct(shape, dtype),
        scratch_shapes=[
            pltpu.VMEM((len(terms),) + shape, dtype),
            pltpu.SemaphoreType.DMA((len(terms),)),
        ],
        compiler_params=pltpu.CompilerParams(vmem_limit_bytes=VMEM_LIMIT),
        cost_estimate=cost_of(100e-6),
        name="add",
    )(*terms)


def join_kernel(near_ref, own_ref, far_ref, near_out, own_out, scratch, sems):
    near, own, *far = fetch((near_ref, own_ref, far_ref.at[0], far_ref.at[1]), scratch, sems)
    near_out[...] = (near + far[0]).astype(near_out.dtype)
    own_out[...] = (own + far[1]).astype(own_out.dtype)


def join(near, own, far):
    vmem = pl.BlockSpec(memory_space=pltpu.VMEM)
    return pl.pallas_call(
        join_kernel,
        in_specs=[pl.BlockSpec(memory_space=pltpu.HBM)] * 3,
        out_specs=[vmem] * 2,
        out_shape=[jax.ShapeDtypeStruct(near.shape, near.dtype)] * 2,
        scratch_shapes=[
            pltpu.VMEM((4,) + near.shape, near.dtype),
            pltpu.SemaphoreType.DMA((4,)),
        ],
        compiler_params=pltpu.CompilerParams(vmem_limit_bytes=VMEM_LIMIT),
        cost_estimate=cost_of(2e-6),
        name="join",
    )(near, own, far)


def finish_kernel(halves, side_ref, hidden_ref, *refs):
    o_ref, scratch, sems = refs[-3:]
    sources = [ref if half is None else ref.at[half] for ref, half in zip(refs, halves)]
    received, *parts = fetch(sources, scratch, sems)
    half = received.shape[2]
    kept = pl.ds(pl.multiple_of(side_ref[0] * half, HD), half)
    other = pl.ds(pl.multiple_of((1 - side_ref[0]) * half, HD), half)
    o_ref[:, other] = (hidden_ref[:, other].astype(jnp.float32) + received[0]).astype(o_ref.dtype)
    o_ref[:, kept] = (hidden_ref[:, kept].astype(jnp.float32) + sum(parts)[0]).astype(o_ref.dtype)


def finish(side, hidden, received, parts):
    terms = [received, *parts]
    halves = tuple(term[1] if isinstance(term, tuple) else None for term in terms)
    terms = [term[0] if isinstance(term, tuple) else term for term in terms]
    vmem = pl.BlockSpec(memory_space=pltpu.VMEM)
    hbm = pl.BlockSpec(memory_space=pltpu.HBM)
    return pl.pallas_call(
        functools.partial(finish_kernel, halves),
        in_specs=[pl.BlockSpec(memory_space=pltpu.SMEM), vmem] + [hbm] * len(terms),
        out_specs=vmem,
        out_shape=jax.ShapeDtypeStruct(hidden.shape, hidden.dtype),
        scratch_shapes=[
            pltpu.VMEM((len(terms),) + received.shape, received.dtype),
            pltpu.SemaphoreType.DMA((len(terms),)),
        ],
        compiler_params=pltpu.CompilerParams(vmem_limit_bytes=VMEM_LIMIT),
        cost_estimate=cost_of(2e-6),
        name="finish",
    )(side.reshape(1), hidden, *terms)


def to_tp(value, pairs):
    return lax.ppermute(value, "tp", pairs)


def apart(tps, distance):
    return [(i, i ^ distance) for i in range(tps)]


def after(value, *others):
    return lax.optimization_barrier((value, *others))[0]


def per_device(
    reqs,
    tps,
    hidden,
    q_new,
    k_new,
    v_new,
    cache_k,
    cache_v,
    cache_len,
    w_out,
    q_cross,
    text_k,
    text_v,
    prompt_of,
):
    rows, width = q_new.shape
    chips = reqs // 2
    place = lax.axis_index("req")
    chip, core = place // 2, place % 2
    side = chip % 2
    text_side = (chip // 2) % 2
    holder = core == side
    length = lax.dynamic_index_in_dim(cache_len, place, 0, keepdims=False)

    def swap(array, distance):
        return lax.ppermute(array, "req", [(i, i ^ distance) for i in range(reqs)])

    first_of = [2 * i + i % 2 for i in range(chips)]
    second_of = [2 * i + 1 - i % 2 for i in range(chips)]
    beside = lax.ppermute(
        w_out,
        "req",
        [(first_of[i], first_of[i ^ 2]) for i in range(chips)]
        + [(second_of[i], second_of[i ^ 1]) for i in range(chips)],
    )
    own_passed = lax.ppermute(w_out, "req", list(zip(first_of, second_of)))

    own = self_attention(q_new, k_new, v_new, cache_k[0], cache_v[0], length)
    near = swap(own, 2)
    beside = after(beside, own)
    across = lax.ppermute(
        beside, "req", [(second_of[i], second_of[i ^ 2]) for i in range(chips)]
    )
    beside_passed = swap(beside, 1)
    split_heads = (width // HD) % 2 == 0
    if split_heads:
        keep, give, ask = pack(text_side, prompt_of, text_k, text_v, after(q_cross, own))
        across = after(across, keep)
        give, keep, ask = after((give, keep, ask), near)
        asked = swap(ask, 4)
        if chips == 4:
            pieces = [keep, asked, swap(keep, 2), swap(give, 6)]
        else:
            pieces = [keep, asked[: give.shape[0]]]
            for bit in range(chips.bit_length() - 1):
                if bit != 1:
                    pieces += [swap(piece, 2 << bit) for piece in pieces]
        spans = text_k.shape[:2]
    across_passed = lax.ppermute(after(across, near), "req", list(zip(second_of, first_of)))
    held = [w_out, beside_passed, beside, across_passed]
    passed = [own_passed, beside, beside_passed, across]
    bit = 4
    while bit < chips:
        held += [swap(block, 2 * bit) for block in held]
        passed += [swap(block, 2 * bit) for block in passed]
        bit *= 2
    at = lax.axis_index("tp")
    order = jnp.stack([chip, holder, at]).astype(jnp.int32)

    def in_order(side, kept, received, axis):
        return jnp.where(
            side == 0,
            jnp.concatenate([kept, received], axis=axis),
            jnp.concatenate([received, kept], axis=axis),
        )

    line = split_heads and tps == 4 and chips == 4
    terms = project(tps, order, own, near, held, passed, line)
    if line:
        near_terms, own_terms, last = terms[:3], terms[3:6], terms[6]
        far, inner = to_tp(last, [(0, 1), (3, 2)]), to_tp(last, [(1, 2), (2, 1)])
        prompts = read_prompts(prompt_of, asked, pieces[2:])
        near_joined, own_joined = join(near_terms[2], own_terms[2], after(far, inner, prompts))
        near_outer, own_outer, *late = after(
            (near_terms[1], own_terms[1], *pieces), near_joined
        )
        near_outer, near_crossing = to_tp(near_outer, apart(4, 1)), to_tp(near_joined, apart(4, 2))
        own_outer, own_crossing = to_tp(own_outer, apart(4, 1)), to_tp(own_joined, apart(4, 2))
        pieces += [swap(piece, 1) for piece in late]
        mine, others = cross_attention(prompts, text_side, q_cross, asked, pieces, spans)
        answer = swap(others, 4)
        near_outer = after(near_outer, mine)
        given = add(near_terms[0], (inner, 0), near_outer, near_crossing)
        own_parts = [own_terms[0], (inner, 1), own_outer, own_crossing]
        cross_heads = in_order(text_side, mine, answer, 1)
        side = gate(side, own_outer, own_crossing, cross_heads)
    else:
        near_parts = [
            [part[0]] + [to_tp(part[d], apart(tps, d)) for d in range(1, tps)]
            for part in (terms[:tps], terms[tps:])
        ]
        given, own_parts = add(*near_parts[0]), near_parts[1]
        if split_heads:
            prompts = read_prompts(prompt_of, asked, [])
            pieces += [swap(piece, 1) for piece in pieces]
            mine, others = cross_attention(prompts, text_side, q_cross, asked, pieces, spans)
            answer = swap(others, 4)
            cross_heads = in_order(text_side, mine, answer, 1)

    if not split_heads:
        cross_heads = whole_cross(q_cross, prompt_of, text_k, text_v)

    received = swap(given, 2)
    if received.shape[0] == 1 and received.shape[2] % HD == 0:
        return finish(side, hidden, received, own_parts), cross_heads
    ordered = in_order(side, add(*own_parts), received, 2).transpose(1, 0, 2).reshape(rows, width)
    hidden_out = (hidden.astype(jnp.float32) + ordered.astype(jnp.float32)).astype(jnp.bfloat16)
    return (hidden_out, cross_heads)


def solution(mesh):
    placed = (
        P("req", "tp"),
        P("req", "tp"),
        P("req", "tp"),
        P("req", "tp"),
        P("req", None, "tp"),
        P("req", None, "tp"),
        P(),
        P("tp", "req"),
        P("req", "tp"),
        P(None, "req", "tp"),
        P(None, "req", "tp"),
        P("req"),
    )
    return jax.shard_map(
        functools.partial(per_device, mesh.shape["req"], mesh.shape["tp"]),
        mesh=mesh,
        in_specs=placed,
        out_specs=(P("req", "tp"), P("req", "tp")),
        check_vma=False,
    )
```

```python
import functools

import jax
import jax.numpy as jnp
from jax import lax
from jax.experimental import pallas as pl
from jax.experimental.pallas import tpu as pltpu
from jax.sharding import PartitionSpec as P

HD = 128
CACHE_BLOCK = 1024
TAG_ROWS = 16
NEG_FILL = -1e30
LOG2E = 1.4426950408889634
VMEM_LIMIT = 64 * 2**20 - 2**17
PEAK = 1.1535e15


def cost_of(seconds):
    return pl.CostEstimate(flops=int(seconds * PEAK), bytes_accessed=0, transcendentals=0)


def repeat_lanes(array, times):
    return jnp.concatenate([array] * times, axis=1) if times > 1 else array


def score(queries, keys):
    return lax.dot_general(
        queries, keys, (((1,), (1,)), ((), ())), preferred_element_type=jnp.float32
    )


def absorb(scores, values, state, visible):
    top_old, total = state
    scale = HD ** (-0.5) * LOG2E
    if visible is not None:
        scores = jnp.where(visible, scores, NEG_FILL)
    top = jnp.maximum(top_old, jnp.max(scores, axis=1, keepdims=True))
    shrink = jnp.exp2((top_old - top) * scale)
    shift = repeat_lanes(top * scale, scores.shape[1] // HD)
    weights = jnp.exp2(scores * scale - shift).astype(jnp.bfloat16)
    extended = jnp.concatenate([values, jnp.ones_like(values)], axis=1)
    total = total * repeat_lanes(shrink, 2) + jnp.dot(
        weights, extended, preferred_element_type=jnp.float32
    )
    return top, total


def empty_state(rows):
    return jnp.full((rows, HD), NEG_FILL, jnp.float32), jnp.zeros((rows, 2 * HD), jnp.float32)


def finished(total):
    return (total[:, :HD] / total[:, HD:]).astype(jnp.bfloat16)


def visit_heads(count, scores_of, use):
    ahead = scores_of(0)
    for head in range(count):
        scores = ahead
        if head + 1 < count:
            ahead = scores_of(head + 1)
        use(head, scores)


def self_kernel(
    block_rows, heads, length_ref, q_ref, kn_ref, vn_ref, kc_ref, vc_ref, o_ref, top_ref, total_ref
):
    step, steps = pl.program_id(0), pl.num_programs(0)
    left = length_ref[lax.axis_index("req")] - step * block_rows
    rows, new_rows = q_ref.shape[0], kn_ref.shape[0]

    @pl.when(step == 0)
    def _():
        for head in range(heads):
            top_ref[head], total_ref[head] = empty_state(rows)

    def visit(k_ref, v_ref, visible, last):
        def use(head, scores):
            cols = slice(head * HD, (head + 1) * HD)
            state = (top_ref[head], total_ref[head])
            top, total = absorb(scores, v_ref[:, cols], state, visible)
            if last:
                o_ref[:, cols] = finished(total)
            else:
                top_ref[head], total_ref[head] = top, total

        def scores_of(head):
            cols = slice(head * HD, (head + 1) * HD)
            return score(q_ref[:, cols], k_ref[:, cols])

        visit_heads(heads, scores_of, use)

    @pl.when(jnp.logical_and(step < steps - 1, left >= block_rows))
    def _():
        visit(kc_ref, vc_ref, None, False)

    @pl.when(jnp.logical_and(step < steps - 1, jnp.logical_and(left > 0, left < block_rows)))
    def _():
        visible = lax.broadcasted_iota(jnp.int32, (rows, block_rows), 1) < left
        visit(kc_ref, vc_ref, visible, False)

    @pl.when(step == steps - 1)
    def _():
        key_ids = lax.broadcasted_iota(jnp.int32, (rows, new_rows), 1)
        query_ids = lax.broadcasted_iota(jnp.int32, (rows, new_rows), 0)
        visit(kn_ref, vn_ref, key_ids <= query_ids, True)


def self_attention(queries, new_keys, new_values, keys, values, lengths):
    rows, width = queries.shape
    new_rows, capacity = new_keys.shape[0], keys.shape[0]
    block_rows = min(CACHE_BLOCK, capacity)
    heads = width // HD
    whole = pl.BlockSpec((rows, width), lambda i, n: (0, 0))
    new = pl.BlockSpec((new_rows, width), lambda i, n: (0, 0))

    def live_block(step, length_ref):
        length = length_ref[lax.axis_index("req")]
        return jnp.minimum(step, lax.div(length - 1, block_rows)), 0

    cached = pl.BlockSpec((block_rows, width), live_block)
    return pl.pallas_call(
        functools.partial(self_kernel, block_rows, heads),
        grid_spec=pltpu.PrefetchScalarGridSpec(
            num_scalar_prefetch=1,
            grid=(capacity // block_rows + 1,),
            in_specs=[whole, new, new, cached, cached],
            out_specs=whole,
            scratch_shapes=[
                pltpu.VMEM((heads, rows, HD), jnp.float32),
                pltpu.VMEM((heads, rows, 2 * HD), jnp.float32),
            ],
        ),
        out_shape=jax.ShapeDtypeStruct((rows, width), jnp.bfloat16),
        compiler_params=pltpu.CompilerParams(vmem_limit_bytes=VMEM_LIMIT),
        cost_estimate=cost_of(20e-6),
        name="self_attention",
    )(lengths, queries, new_keys, new_values, keys, values)


def cross_kernel(heads, pieces_count, spans, prompts_ref, side_ref, q_ref, near_ref, *refs):
    pieces, (own_ref, other_ref) = refs[:pieces_count], refs[pieces_count:]
    rows = q_ref.shape[0]
    width = heads * HD
    first = pl.multiple_of(side_ref[0] * width, HD)
    asked = 2 * spans[0] * spans[1]
    for part in range(2):
        prompt = prompts_ref[part]
        target = other_ref if part else own_ref

        def gathered(kind, head, prompt=prompt):
            cols = slice(head * HD, (head + 1) * HD)
            count, text_rows = spans
            at = pl.ds(pl.multiple_of((kind * count + prompt) * text_rows, text_rows), text_rows)
            return jnp.concatenate([piece[at, cols] for piece in pieces], axis=0)

        def scores_of(head, part=part, gathered=gathered):
            if part == 0:
                queries = q_ref[:, pl.ds(pl.multiple_of(first + head * HD, HD), HD)]
            else:
                queries = near_ref[asked : asked + rows, head * HD : (head + 1) * HD]
            return score(queries, gathered(0, head))

        def use(head, scores, target=target, gathered=gathered):
            _, total = absorb(scores, gathered(1, head), empty_state(rows), None)
            target[:, head * HD : (head + 1) * HD] = finished(total)

        visit_heads(heads, scores_of, use)


def cross_attention(prompts, side, queries, near, pieces, spans):
    rows, width = queries.shape
    half = width // 2
    scalars = pl.BlockSpec(memory_space=pltpu.SMEM)
    vmem = pl.BlockSpec(memory_space=pltpu.VMEM)
    return pl.pallas_call(
        functools.partial(cross_kernel, half // HD, len(pieces), spans),
        in_specs=[scalars, scalars] + [vmem] * (2 + len(pieces)),
        out_specs=[vmem, vmem],
        out_shape=[jax.ShapeDtypeStruct((rows, half), jnp.bfloat16)] * 2,
        compiler_params=pltpu.CompilerParams(vmem_limit_bytes=VMEM_LIMIT),
        cost_estimate=cost_of(0),
        name="cross_attention",
    )(prompts, side.reshape(1), queries, near, *pieces)


def prompts_kernel(prompt_ref, tag_ref, *refs):
    refs[-1][0] = prompt_ref[0]
    refs[-1][1] = jnp.max(tag_ref[...].astype(jnp.float32)).astype(jnp.int32)


def read_prompts(prompt_of, asked, gates):
    rows, half = asked.shape
    scalars = pl.BlockSpec(memory_space=pltpu.SMEM)
    return pl.pallas_call(
        prompts_kernel,
        grid=(1,),
        in_specs=[scalars, pl.BlockSpec((TAG_ROWS, half), lambda i: (rows // TAG_ROWS - 1, 0))]
        + [pl.BlockSpec(memory_space=pl.ANY)] * len(gates),
        out_specs=scalars,
        out_shape=jax.ShapeDtypeStruct((2,), jnp.int32),
        cost_estimate=cost_of(100e-6),
        name="read_prompts",
    )(prompt_of, asked, *gates)


def gate_kernel(value_ref, *refs):
    refs[-1][0] = value_ref[0]


def gate(value, *waited):
    scalars = pl.BlockSpec(memory_space=pltpu.SMEM)
    return pl.pallas_call(
        gate_kernel,
        in_specs=[scalars] + [pl.BlockSpec(memory_space=pltpu.HBM)] * len(waited),
        out_specs=scalars,
        out_shape=jax.ShapeDtypeStruct((1,), jnp.int32),
        cost_estimate=cost_of(100e-6),
        name="gate",
    )(value.reshape(1), *waited)[0]


def pack_kernel(side_ref, prompt_ref, k_ref, v_ref, q_ref, keep_ref, give_ref, ask_ref):
    half = keep_ref.shape[1]
    prompts, text_rows, _ = k_ref.shape
    kept = pl.ds(pl.multiple_of(side_ref[0] * half, HD), half)
    given = pl.ds(pl.multiple_of((1 - side_ref[0]) * half, HD), half)
    for part, source in enumerate((k_ref, v_ref)):
        for prompt in range(prompts):
            first = (part * prompts + prompt) * text_rows
            at = slice(first, first + text_rows)
            keep_ref[at, :] = source[prompt, :, kept]
            give_ref[at, :] = source[prompt, :, given]
            ask_ref[at, :] = source[prompt, :, given]
    first, rows = give_ref.shape[0], q_ref.shape[0]
    ask_ref[first : first + rows, :] = q_ref[:, given]
    tag = jnp.full((TAG_ROWS, half), prompt_ref[0], jnp.int32)
    ask_ref[first + rows :, :] = tag.astype(jnp.float32).astype(ask_ref.dtype)


def pack(side, prompt_of, text_k, text_v, queries):
    prompts, text_rows, width = text_k.shape
    rows, half = queries.shape[0], width // 2
    text = jax.ShapeDtypeStruct((2 * prompts * text_rows, half), text_k.dtype)
    ask = jax.ShapeDtypeStruct((text.shape[0] + rows + TAG_ROWS, half), queries.dtype)
    scalars = pl.BlockSpec(memory_space=pltpu.SMEM)
    vmem = pl.BlockSpec(memory_space=pltpu.VMEM)
    return pl.pallas_call(
        pack_kernel,
        in_specs=[scalars, scalars, vmem, vmem, vmem],
        out_specs=[vmem] * 3,
        out_shape=[text, text, ask],
        compiler_params=pltpu.CompilerParams(vmem_limit_bytes=VMEM_LIMIT),
        cost_estimate=cost_of(3e-6),
        name="pack",
    )(side.reshape(1), prompt_of, text_k, text_v, queries)


def whole_cross_kernel(heads, q_ref, k_ref, v_ref, o_ref):
    def scores_of(head):
        cols = slice(head * HD, (head + 1) * HD)
        return score(q_ref[:, cols], k_ref[:, cols])

    def use(head, scores):
        cols = slice(head * HD, (head + 1) * HD)
        _, total = absorb(scores, v_ref[:, cols], empty_state(q_ref.shape[0]), None)
        o_ref[:, cols] = finished(total)

    visit_heads(heads, scores_of, use)


def whole_cross(queries, prompt_of, text_k, text_v):
    keys, values = (
        lax.dynamic_index_in_dim(
            lax.all_gather(text, "req", axis=1, tiled=True), prompt_of[0], 0, keepdims=False
        )
        for text in (text_k, text_v)
    )
    return pl.pallas_call(
        functools.partial(whole_cross_kernel, queries.shape[1] // HD),
        out_shape=jax.ShapeDtypeStruct(queries.shape, jnp.bfloat16),
        compiler_params=pltpu.CompilerParams(vmem_limit_bytes=VMEM_LIMIT),
        name="whole_cross",
    )(queries, keys, values)


def project_kernel(count, flat, places, joint, own_ref, near_ref, *refs):
    held, passed = refs[:count], refs[count : 2 * count]
    outs = refs[2 * count : -6]
    x_ref, weights, terms, x_sems, sems, out_sems = refs[-6:]
    place, at_tp = lax.axis_index("req"), lax.axis_index("tp")
    chip = lax.div(place, 2)
    holder = lax.rem(place, 2) == lax.rem(chip, 2)
    rows, columns = own_ref.shape[0], held[0].shape[1]
    blocks = outs[0].shape[0]
    if joint:
        outs = (*outs[: places - 1], outs[-1].at[0], *outs[places - 1 : -1], outs[-1].at[1])

    def rows_in(part):
        source = (near_ref, own_ref)[part]
        return pltpu.make_async_copy(
            source, x_ref.at[part * rows : (part + 1) * rows], x_sems.at[part]
        )

    def weights_in(choice, at):
        target = weights.at[:, at * columns : (at + 1) * columns] if flat else weights.at[at]
        return pltpu.make_async_copy(choice[at], target, sems.at[at])

    def terms_out(at, part, distance, block):
        if flat:
            source = terms.at[part, :, at * columns : (at + 1) * columns]
        else:
            source = terms.at[at, part]
        target = outs[part * places + distance].at[block]
        return pltpu.make_async_copy(source, target, out_sems.at[at, part])

    def send(at):
        source = chip ^ at
        block = lax.rem(source, blocks)
        away = lax.div(source, blocks) ^ at_tp
        for distance in range(places):

            @pl.when(away == distance)
            def _(at=at, distance=distance, block=block):
                for part in range(2):
                    terms_out(at, part, distance, block).start()

    for part in range(2):
        rows_in(part).start()

    @pl.when(holder)
    def _():
        for at in range(count):
            weights_in(held, at).start()

    @pl.when(jnp.logical_not(holder))
    def _():
        for at in range(count):
            weights_in(passed, at).start()

    for part in range(2):
        rows_in(part).wait()
    there = sent = 0
    for first in range(0, count * columns, flat or columns):
        last = first + (flat or columns)
        while there * columns < last:
            weights_in(held, there).wait()
            there += 1
        block_weights = weights[:, first:last] if flat else weights[first // columns]
        product = jnp.dot(x_ref[...], block_weights, preferred_element_type=jnp.float32)
        product = product.astype(terms.dtype)
        for part in range(2):
            piece = product[part * rows : (part + 1) * rows]
            if flat:
                terms[part, :, first:last] = piece
            else:
                terms[first // columns, part] = piece
        while (sent + 1) * columns <= last:
            send(sent)
            sent += 1

    for at in range(count):
        for part in range(2):
            terms_out(at, part, 0, 0).wait()


def project(tps, own, near, held, passed, joint):
    rows = own.shape[0]
    depth, columns = held[0].shape
    count = len(held)
    flat = 512 if columns % HD == 0 and count * columns % 512 == 0 else 0
    hbm = pl.BlockSpec(memory_space=pltpu.HBM)
    out = jax.ShapeDtypeStruct((count // tps, rows, columns), jnp.bfloat16)
    return pl.pallas_call(
        functools.partial(project_kernel, count, flat, tps, joint),
        in_specs=[hbm] * (2 + 2 * count),
        out_specs=[hbm] * (2 * tps - joint),
        out_shape=(
            [out] * (2 * tps - 2) + [jax.ShapeDtypeStruct((2, *out.shape), out.dtype)]
            if joint
            else [out] * (2 * tps)
        ),
        scratch_shapes=[
            pltpu.VMEM((2 * rows, depth), jnp.bfloat16),
            pltpu.VMEM((depth, count * columns) if flat else (count, depth, columns), jnp.bfloat16),
            pltpu.VMEM(
                (2, rows, count * columns) if flat else (count, 2, rows, columns), jnp.bfloat16
            ),
            pltpu.SemaphoreType.DMA((2,)),
            pltpu.SemaphoreType.DMA((count,)),
            pltpu.SemaphoreType.DMA((count, 2)),
        ],
        compiler_params=pltpu.CompilerParams(vmem_limit_bytes=VMEM_LIMIT),
        cost_estimate=cost_of(10e-6),
        name="project",
    )(own, near, *held, *passed)


def fetch(sources, scratch, sems):
    copies = [
        pltpu.make_async_copy(source, scratch.at[at], sems.at[at])
        for at, source in enumerate(sources)
    ]
    for copy in copies:
        copy.start()
    for copy in copies:
        copy.wait()
    return [scratch[at].astype(jnp.float32) for at in range(len(copies))]


def add_kernel(halves, *refs):
    out, scratch, sems = refs[-3:]
    sources = [ref if half is None else ref.at[half] for ref, half in zip(refs, halves)]
    out[...] = sum(fetch(sources, scratch, sems)).astype(out.dtype)


def add(*terms):
    halves = tuple(term[1] if isinstance(term, tuple) else None for term in terms)
    terms = [term[0] if isinstance(term, tuple) else term for term in terms]
    shape, dtype = terms[0].shape, terms[0].dtype
    return pl.pallas_call(
        functools.partial(add_kernel, halves),
        in_specs=[pl.BlockSpec(memory_space=pltpu.HBM)] * len(terms),
        out_specs=pl.BlockSpec(memory_space=pltpu.VMEM),
        out_shape=jax.ShapeDtypeStruct(shape, dtype),
        scratch_shapes=[
            pltpu.VMEM((len(terms),) + shape, dtype),
            pltpu.SemaphoreType.DMA((len(terms),)),
        ],
        compiler_params=pltpu.CompilerParams(vmem_limit_bytes=VMEM_LIMIT),
        cost_estimate=cost_of(100e-6),
        name="add",
    )(*terms)


def join_kernel(near_ref, own_ref, far_ref, near_out, own_out, scratch, sems):
    near, own, *far = fetch((near_ref, own_ref, far_ref.at[0], far_ref.at[1]), scratch, sems)
    near_out[...] = (near + far[0]).astype(near_out.dtype)
    own_out[...] = (own + far[1]).astype(own_out.dtype)


def join(near, own, far):
    vmem = pl.BlockSpec(memory_space=pltpu.VMEM)
    return pl.pallas_call(
        join_kernel,
        in_specs=[pl.BlockSpec(memory_space=pltpu.HBM)] * 3,
        out_specs=[vmem] * 2,
        out_shape=[jax.ShapeDtypeStruct(near.shape, near.dtype)] * 2,
        scratch_shapes=[
            pltpu.VMEM((4,) + near.shape, near.dtype),
            pltpu.SemaphoreType.DMA((4,)),
        ],
        compiler_params=pltpu.CompilerParams(vmem_limit_bytes=VMEM_LIMIT),
        cost_estimate=cost_of(2e-6),
        name="join",
    )(near, own, far)


def finish_kernel(halves, side_ref, hidden_ref, received_ref, *refs):
    o_ref, rest, kept_part, near_part, parts, sems, out_sems = refs[-7:]
    sources = [ref if half is None else ref.at[half] for ref, half in zip(refs, halves)]
    half = received_ref.shape[2]
    kept = pl.ds(pl.multiple_of(side_ref[0] * half, HD), half)
    other = pl.ds(pl.multiple_of((1 - side_ref[0]) * half, HD), half)
    copies = [
        pltpu.make_async_copy(hidden_ref.at[:, other], rest.at[0], sems.at[0]),
        pltpu.make_async_copy(received_ref.at[0], near_part, sems.at[1]),
        pltpu.make_async_copy(hidden_ref.at[:, kept], rest.at[1], sems.at[2]),
    ] + [
        pltpu.make_async_copy(source.at[0], parts.at[at], sems.at[3 + at])
        for at, source in enumerate(sources)
    ]
    for copy in copies:
        copy.start()
    for copy in copies[:2]:
        copy.wait()
    near_part[...] = (
        rest[0].astype(jnp.float32) + near_part[...].astype(jnp.float32)
    ).astype(near_part.dtype)
    outs = [pltpu.make_async_copy(near_part, o_ref.at[:, other], out_sems.at[0])]
    outs[0].start()
    for copy in copies[2:]:
        copy.wait()
    total = rest[1].astype(jnp.float32)
    for at in range(len(sources)):
        total += parts[at].astype(jnp.float32)
    kept_part[...] = total.astype(kept_part.dtype)
    outs.append(pltpu.make_async_copy(kept_part, o_ref.at[:, kept], out_sems.at[1]))
    outs[1].start()
    for copy in outs:
        copy.wait()


def finish(side, hidden, received, parts):
    halves = tuple(part[1] if isinstance(part, tuple) else None for part in parts)
    parts = [part[0] if isinstance(part, tuple) else part for part in parts]
    hbm = pl.BlockSpec(memory_space=pltpu.HBM)
    half = received.shape[1:]
    return pl.pallas_call(
        functools.partial(finish_kernel, halves),
        in_specs=[pl.BlockSpec(memory_space=pltpu.SMEM)] + [hbm] * (2 + len(parts)),
        out_specs=hbm,
        out_shape=jax.ShapeDtypeStruct(hidden.shape, hidden.dtype),
        scratch_shapes=[
            pltpu.VMEM((2, *half), hidden.dtype),
            pltpu.VMEM(half, hidden.dtype),
            pltpu.VMEM(half, hidden.dtype),
            pltpu.VMEM((len(parts), *half), hidden.dtype),
            pltpu.SemaphoreType.DMA((3 + len(parts),)),
            pltpu.SemaphoreType.DMA((2,)),
        ],
        compiler_params=pltpu.CompilerParams(vmem_limit_bytes=VMEM_LIMIT),
        cost_estimate=cost_of(2e-6),
        name="finish",
    )(side.reshape(1), hidden, received, *parts)


def to_tp(value, pairs):
    return lax.ppermute(value, "tp", pairs)


def apart(tps, distance):
    return [(i, i ^ distance) for i in range(tps)]


def after(value, *others):
    return lax.optimization_barrier((value, *others))[0]


def per_device(
    reqs,
    tps,
    hidden,
    q_new,
    k_new,
    v_new,
    cache_k,
    cache_v,
    cache_len,
    w_out,
    q_cross,
    text_k,
    text_v,
    prompt_of,
):
    rows, width = q_new.shape
    chips = reqs // 2
    place = lax.axis_index("req")
    chip = place // 2
    side = chip % 2
    text_side = (chip // 2) % 2

    def swap(array, distance):
        return lax.ppermute(array, "req", [(i, i ^ distance) for i in range(reqs)])

    first_of = [2 * i + i % 2 for i in range(chips)]
    second_of = [2 * i + 1 - i % 2 for i in range(chips)]
    beside = lax.ppermute(
        w_out,
        "req",
        [(first_of[i], first_of[i ^ 2]) for i in range(chips)]
        + [(second_of[i], second_of[i ^ 1]) for i in range(chips)],
    )
    own_passed = lax.ppermute(w_out, "req", list(zip(first_of, second_of)))

    own = self_attention(q_new, k_new, v_new, cache_k[0], cache_v[0], cache_len)
    near = swap(own, 2)
    beside = after(beside, own)
    across = lax.ppermute(
        beside, "req", [(second_of[i], second_of[i ^ 2]) for i in range(chips)]
    )
    beside_passed = swap(beside, 1)
    split_heads = (width // HD) % 2 == 0
    if split_heads:
        keep, give, ask = pack(text_side, prompt_of, text_k, text_v, after(q_cross, own))
        across = after(across, keep)
        give, keep, ask = after((give, keep, ask), near)
        asked = swap(ask, 4)
        if chips == 4:
            pieces = [keep, asked, swap(keep, 2), swap(give, 6)]
        else:
            pieces = [keep, asked[: give.shape[0]]]
            for bit in range(chips.bit_length() - 1):
                if bit != 1:
                    pieces += [swap(piece, 2 << bit) for piece in pieces]
        spans = text_k.shape[:2]
    across_passed = lax.ppermute(after(across, near), "req", list(zip(second_of, first_of)))
    held = [w_out, beside_passed, beside, across_passed]
    passed = [own_passed, beside, beside_passed, across]
    bit = 4
    while bit < chips:
        held += [swap(block, 2 * bit) for block in held]
        passed += [swap(block, 2 * bit) for block in passed]
        bit *= 2
    def in_order(side, kept, received, axis):
        return jnp.where(
            side == 0,
            jnp.concatenate([kept, received], axis=axis),
            jnp.concatenate([received, kept], axis=axis),
        )

    line = split_heads and tps == 4 and chips == 4
    terms = project(tps, own, near, held, passed, line)
    if line:
        near_terms, own_terms, last = terms[:3], terms[3:6], terms[6]
        far, inner = to_tp(last, [(0, 1), (3, 2)]), to_tp(last, [(1, 2), (2, 1)])
        prompts = read_prompts(prompt_of, asked, pieces[2:])
        near_joined, own_joined = join(near_terms[2], own_terms[2], after(far, inner, prompts))
        near_outer, own_outer, *late = after(
            (near_terms[1], own_terms[1], *pieces), near_joined
        )
        near_outer, near_crossing = to_tp(near_outer, apart(4, 1)), to_tp(near_joined, apart(4, 2))
        own_outer, own_crossing = to_tp(own_outer, apart(4, 1)), to_tp(own_joined, apart(4, 2))
        pieces += [swap(piece, 1) for piece in late]
        mine, others = cross_attention(prompts, text_side, q_cross, asked, pieces, spans)
        answer = swap(others, 4)
        near_outer = after(near_outer, mine)
        given = add(near_terms[0], (inner, 0), near_outer, near_crossing)
        own_parts = [own_terms[0], (inner, 1), own_outer, own_crossing]
        cross_heads = in_order(text_side, mine, answer, 1)
        side = gate(side, own_outer, own_crossing, cross_heads)
    else:
        near_parts = [
            [part[0]] + [to_tp(part[d], apart(tps, d)) for d in range(1, tps)]
            for part in (terms[:tps], terms[tps:])
        ]
        given, own_parts = add(*near_parts[0]), near_parts[1]
        if split_heads:
            prompts = read_prompts(prompt_of, asked, [])
            pieces += [swap(piece, 1) for piece in pieces]
            mine, others = cross_attention(prompts, text_side, q_cross, asked, pieces, spans)
            answer = swap(others, 4)
            cross_heads = in_order(text_side, mine, answer, 1)

    if not split_heads:
        cross_heads = whole_cross(q_cross, prompt_of, text_k, text_v)

    received = swap(given, 2)
    if received.shape[0] == 1 and received.shape[2] % HD == 0:
        return finish(side, hidden, received, own_parts), cross_heads
    ordered = in_order(side, add(*own_parts), received, 2).transpose(1, 0, 2).reshape(rows, width)
    hidden_out = (hidden.astype(jnp.float32) + ordered.astype(jnp.float32)).astype(jnp.bfloat16)
    return (hidden_out, cross_heads)


def solution(mesh):
    placed = (
        P("req", "tp"),
        P("req", "tp"),
        P("req", "tp"),
        P("req", "tp"),
        P("req", None, "tp"),
        P("req", None, "tp"),
        P(),
        P("tp", "req"),
        P("req", "tp"),
        P(None, "req", "tp"),
        P(None, "req", "tp"),
        P("req"),
    )
    return jax.shard_map(
        functools.partial(per_device, mesh.shape["req"], mesh.shape["tp"]),
        mesh=mesh,
        in_specs=placed,
        out_specs=(P("req", "tp"), P("req", "tp")),
        check_vma=False,
    )
```

```python
import functools

import jax
import jax.numpy as jnp
from jax import lax
from jax.experimental import pallas as pl
from jax.experimental.pallas import tpu as pltpu
from jax.sharding import PartitionSpec as P

HD = 128
CACHE_BLOCK = 1024
TAG_ROWS = 16
NEG_FILL = -1e30
LOG2E = 1.4426950408889634
VMEM_LIMIT = 64 * 2**20 - 2**17
PEAK = 1.1535e15


def cost_of(seconds):
    return pl.CostEstimate(flops=int(seconds * PEAK), bytes_accessed=0, transcendentals=0)


def repeat_lanes(array, times):
    return jnp.concatenate([array] * times, axis=1) if times > 1 else array


def score(queries, keys):
    return lax.dot_general(
        queries, keys, (((1,), (1,)), ((), ())), preferred_element_type=jnp.float32
    )


def absorb(scores, values, state, visible):
    top_old, total = state
    scale = HD ** (-0.5) * LOG2E
    if visible is not None:
        scores = jnp.where(visible, scores, NEG_FILL)
    top = jnp.maximum(top_old, jnp.max(scores, axis=1, keepdims=True))
    shrink = jnp.exp2((top_old - top) * scale)
    shift = repeat_lanes(top * scale, scores.shape[1] // HD)
    weights = jnp.exp2(scores * scale - shift).astype(jnp.bfloat16)
    extended = jnp.concatenate([values, jnp.ones_like(values)], axis=1)
    total = total * repeat_lanes(shrink, 2) + jnp.dot(
        weights, extended, preferred_element_type=jnp.float32
    )
    return top, total


def empty_state(rows):
    return jnp.full((rows, HD), NEG_FILL, jnp.float32), jnp.zeros((rows, 2 * HD), jnp.float32)


def finished(total):
    return (total[:, :HD] / total[:, HD:]).astype(jnp.bfloat16)


def visit_heads(count, scores_of, use):
    ahead = scores_of(0)
    for head in range(count):
        scores = ahead
        if head + 1 < count:
            ahead = scores_of(head + 1)
        use(head, scores)


def self_kernel(
    block_rows, heads, length_ref, q_ref, kn_ref, vn_ref, kc_ref, vc_ref, o_ref, top_ref, total_ref
):
    step, steps = pl.program_id(0), pl.num_programs(0)
    left = length_ref[lax.axis_index("req")] - step * block_rows
    rows, new_rows = q_ref.shape[0], kn_ref.shape[0]

    @pl.when(step == 0)
    def _():
        for head in range(heads):
            top_ref[head], total_ref[head] = empty_state(rows)

    def visit(k_ref, v_ref, visible, last):
        def use(head, scores):
            cols = slice(head * HD, (head + 1) * HD)
            state = (top_ref[head], total_ref[head])
            top, total = absorb(scores, v_ref[:, cols], state, visible)
            if last:
                o_ref[:, cols] = finished(total)
            else:
                top_ref[head], total_ref[head] = top, total

        def scores_of(head):
            cols = slice(head * HD, (head + 1) * HD)
            return score(q_ref[:, cols], k_ref[:, cols])

        visit_heads(heads, scores_of, use)

    @pl.when(jnp.logical_and(step < steps - 1, left >= block_rows))
    def _():
        visit(kc_ref, vc_ref, None, False)

    @pl.when(jnp.logical_and(step < steps - 1, jnp.logical_and(left > 0, left < block_rows)))
    def _():
        visible = lax.broadcasted_iota(jnp.int32, (rows, block_rows), 1) < left
        visit(kc_ref, vc_ref, visible, False)

    @pl.when(step == steps - 1)
    def _():
        key_ids = lax.broadcasted_iota(jnp.int32, (rows, new_rows), 1)
        query_ids = lax.broadcasted_iota(jnp.int32, (rows, new_rows), 0)
        visit(kn_ref, vn_ref, key_ids <= query_ids, True)


def self_attention(queries, new_keys, new_values, keys, values, lengths):
    rows, width = queries.shape
    new_rows, capacity = new_keys.shape[0], keys.shape[0]
    block_rows = min(CACHE_BLOCK, capacity)
    heads = width // HD
    whole = pl.BlockSpec((rows, width), lambda i, n: (0, 0))
    new = pl.BlockSpec((new_rows, width), lambda i, n: (0, 0))

    def live_block(step, length_ref):
        length = length_ref[lax.axis_index("req")]
        return jnp.minimum(step, lax.div(length - 1, block_rows)), 0

    cached = pl.BlockSpec((block_rows, width), live_block)
    return pl.pallas_call(
        functools.partial(self_kernel, block_rows, heads),
        grid_spec=pltpu.PrefetchScalarGridSpec(
            num_scalar_prefetch=1,
            grid=(capacity // block_rows + 1,),
            in_specs=[whole, new, new, cached, cached],
            out_specs=whole,
            scratch_shapes=[
                pltpu.VMEM((heads, rows, HD), jnp.float32),
                pltpu.VMEM((heads, rows, 2 * HD), jnp.float32),
            ],
        ),
        out_shape=jax.ShapeDtypeStruct((rows, width), jnp.bfloat16),
        compiler_params=pltpu.CompilerParams(vmem_limit_bytes=VMEM_LIMIT),
        cost_estimate=cost_of(20e-6),
        name="self_attention",
    )(lengths, queries, new_keys, new_values, keys, values)


def cross_kernel(heads, pieces_count, spans, prompt_ref, side_ref, q_ref, near_ref, *refs):
    pieces, (own_ref, other_ref) = refs[:pieces_count], refs[pieces_count:]
    rows = q_ref.shape[0]
    width = heads * HD
    first = pl.multiple_of(side_ref[0] * width, HD)
    tag = near_ref[rows:, :HD].astype(jnp.float32)
    prompts = prompt_ref[0], jnp.max(tag).astype(jnp.int32)
    for part, prompt in enumerate(prompts):
        target = other_ref if part else own_ref

        def gathered(kind, head, prompt=prompt):
            cols = slice(head * HD, (head + 1) * HD)
            count, text_rows = spans
            at = pl.ds(pl.multiple_of((kind * count + prompt) * text_rows, text_rows), text_rows)
            return jnp.concatenate([piece[at, cols] for piece in pieces], axis=0)

        def scores_of(head, part=part, gathered=gathered):
            source = near_ref if part else q_ref
            queries = source[:rows, pl.ds(pl.multiple_of(first + head * HD, HD), HD)]
            return score(queries, gathered(0, head))

        def use(head, scores, target=target, gathered=gathered):
            _, total = absorb(scores, gathered(1, head), empty_state(rows), None)
            target[:, head * HD : (head + 1) * HD] = finished(total)

        visit_heads(heads, scores_of, use)


def cross_attention(prompt, side, queries, near, pieces, spans):
    rows, width = queries.shape
    half = width // 2
    scalars = pl.BlockSpec(memory_space=pltpu.SMEM)
    vmem = pl.BlockSpec(memory_space=pltpu.VMEM)
    return pl.pallas_call(
        functools.partial(cross_kernel, half // HD, len(pieces), spans),
        in_specs=[scalars, scalars] + [vmem] * (2 + len(pieces)),
        out_specs=[vmem, vmem],
        out_shape=[jax.ShapeDtypeStruct((rows, half), jnp.bfloat16)] * 2,
        compiler_params=pltpu.CompilerParams(vmem_limit_bytes=VMEM_LIMIT),
        cost_estimate=cost_of(2e-6),
        name="cross_attention",
    )(prompt, side.reshape(1), queries, near, *pieces)


def gate_kernel(value_ref, *refs):
    refs[-1][0] = value_ref[0]


def gate(value, *waited):
    scalars = pl.BlockSpec(memory_space=pltpu.SMEM)
    return pl.pallas_call(
        gate_kernel,
        in_specs=[scalars] + [pl.BlockSpec(memory_space=pltpu.HBM)] * len(waited),
        out_specs=scalars,
        out_shape=jax.ShapeDtypeStruct((1,), jnp.int32),
        cost_estimate=cost_of(100e-6),
        name="gate",
    )(value.reshape(1), *waited)


def pack_kernel(side_ref, prompt_ref, k_ref, v_ref, q_ref, keep_ref, give_ref, ask_ref):
    half = keep_ref.shape[1]
    prompts, text_rows, _ = k_ref.shape
    kept = pl.ds(pl.multiple_of(side_ref[0] * half, HD), half)
    given = pl.ds(pl.multiple_of((1 - side_ref[0]) * half, HD), half)
    for part, source in enumerate((k_ref, v_ref)):
        for prompt in range(prompts):
            first = (part * prompts + prompt) * text_rows
            at = slice(first, first + text_rows)
            keep_ref[at, :] = source[prompt, :, kept]
            give_ref[at, :] = source[prompt, :, given]
    rows = q_ref.shape[0]
    ask_ref[:rows, :] = q_ref[...]
    tag = jnp.full((TAG_ROWS, 2 * half), prompt_ref[0], jnp.int32)
    ask_ref[rows:, :] = tag.astype(jnp.float32).astype(ask_ref.dtype)


def pack(side, prompt_of, text_k, text_v, queries):
    prompts, text_rows, width = text_k.shape
    rows, half = queries.shape[0], width // 2
    text = jax.ShapeDtypeStruct((2 * prompts * text_rows, half), text_k.dtype)
    ask = jax.ShapeDtypeStruct((rows + TAG_ROWS, width), queries.dtype)
    scalars = pl.BlockSpec(memory_space=pltpu.SMEM)
    vmem = pl.BlockSpec(memory_space=pltpu.VMEM)
    return pl.pallas_call(
        pack_kernel,
        in_specs=[scalars, scalars, vmem, vmem, vmem],
        out_specs=[vmem] * 3,
        out_shape=[text, text, ask],
        compiler_params=pltpu.CompilerParams(vmem_limit_bytes=VMEM_LIMIT),
        cost_estimate=cost_of(3e-6),
        name="pack",
    )(side.reshape(1), prompt_of, text_k, text_v, queries)


def whole_cross_kernel(heads, q_ref, k_ref, v_ref, o_ref):
    def scores_of(head):
        cols = slice(head * HD, (head + 1) * HD)
        return score(q_ref[:, cols], k_ref[:, cols])

    def use(head, scores):
        cols = slice(head * HD, (head + 1) * HD)
        _, total = absorb(scores, v_ref[:, cols], empty_state(q_ref.shape[0]), None)
        o_ref[:, cols] = finished(total)

    visit_heads(heads, scores_of, use)


def whole_cross(queries, prompt_of, text_k, text_v):
    keys, values = (
        lax.dynamic_index_in_dim(
            lax.all_gather(text, "req", axis=1, tiled=True), prompt_of[0], 0, keepdims=False
        )
        for text in (text_k, text_v)
    )
    return pl.pallas_call(
        functools.partial(whole_cross_kernel, queries.shape[1] // HD),
        out_shape=jax.ShapeDtypeStruct(queries.shape, jnp.bfloat16),
        compiler_params=pltpu.CompilerParams(vmem_limit_bytes=VMEM_LIMIT),
        name="whole_cross",
    )(queries, keys, values)


def project_kernel(count, flat, places, joint, own_ref, near_ref, *refs):
    held, passed = refs[:count], refs[count : 2 * count]
    outs = refs[2 * count : -6]
    x_ref, weights, terms, x_sems, sems, out_sems = refs[-6:]
    place, at_tp = lax.axis_index("req"), lax.axis_index("tp")
    chip = lax.div(place, 2)
    holder = lax.rem(place, 2) == lax.rem(chip, 2)
    rows, columns = own_ref.shape[0], held[0].shape[1]
    blocks = outs[0].shape[0]
    if joint:
        outs = (*outs[: places - 1], outs[-1].at[0], *outs[places - 1 : -1], outs[-1].at[1])

    def rows_in(part):
        source = (near_ref, own_ref)[part]
        return pltpu.make_async_copy(
            source, x_ref.at[part * rows : (part + 1) * rows], x_sems.at[part]
        )

    def weights_in(choice, at):
        target = weights.at[:, at * columns : (at + 1) * columns] if flat else weights.at[at]
        return pltpu.make_async_copy(choice[at], target, sems.at[at])

    def terms_out(at, part, distance, block):
        if flat:
            source = terms.at[part, :, at * columns : (at + 1) * columns]
        else:
            source = terms.at[at, part]
        target = outs[part * places + distance].at[block]
        return pltpu.make_async_copy(source, target, out_sems.at[at, part])

    def send(at):
        source = chip ^ at
        block = lax.rem(source, blocks)
        away = lax.div(source, blocks) ^ at_tp
        for distance in range(places):

            @pl.when(away == distance)
            def _(at=at, distance=distance, block=block):
                for part in range(2):
                    terms_out(at, part, distance, block).start()

    for part in range(2):
        rows_in(part).start()

    @pl.when(holder)
    def _():
        for at in range(count):
            weights_in(held, at).start()

    @pl.when(jnp.logical_not(holder))
    def _():
        for at in range(count):
            weights_in(passed, at).start()

    for part in range(2):
        rows_in(part).wait()
    there = sent = 0
    for first in range(0, count * columns, flat or columns):
        last = first + (flat or columns)
        while there * columns < last:
            weights_in(held, there).wait()
            there += 1
        block_weights = weights[:, first:last] if flat else weights[first // columns]
        product = jnp.dot(x_ref[...], block_weights, preferred_element_type=jnp.float32)
        product = product.astype(terms.dtype)
        for part in range(2):
            piece = product[part * rows : (part + 1) * rows]
            if flat:
                terms[part, :, first:last] = piece
            else:
                terms[first // columns, part] = piece
        while (sent + 1) * columns <= last:
            send(sent)
            sent += 1

    for at in range(count):
        for part in range(2):
            terms_out(at, part, 0, 0).wait()


def project(tps, own, near, held, passed, joint):
    rows = own.shape[0]
    depth, columns = held[0].shape
    count = len(held)
    flat = 512 if columns % HD == 0 and count * columns % 512 == 0 else 0
    hbm = pl.BlockSpec(memory_space=pltpu.HBM)
    out = jax.ShapeDtypeStruct((count // tps, rows, columns), jnp.bfloat16)
    return pl.pallas_call(
        functools.partial(project_kernel, count, flat, tps, joint),
        in_specs=[hbm] * (2 + 2 * count),
        out_specs=[hbm] * (2 * tps - joint),
        out_shape=(
            [out] * (2 * tps - 2) + [jax.ShapeDtypeStruct((2, *out.shape), out.dtype)]
            if joint
            else [out] * (2 * tps)
        ),
        scratch_shapes=[
            pltpu.VMEM((2 * rows, depth), jnp.bfloat16),
            pltpu.VMEM((depth, count * columns) if flat else (count, depth, columns), jnp.bfloat16),
            pltpu.VMEM(
                (2, rows, count * columns) if flat else (count, 2, rows, columns), jnp.bfloat16
            ),
            pltpu.SemaphoreType.DMA((2,)),
            pltpu.SemaphoreType.DMA((count,)),
            pltpu.SemaphoreType.DMA((count, 2)),
        ],
        compiler_params=pltpu.CompilerParams(vmem_limit_bytes=VMEM_LIMIT),
        cost_estimate=cost_of(10e-6),
        name="project",
    )(own, near, *held, *passed)


def fetch(sources, scratch, sems):
    copies = [
        pltpu.make_async_copy(source, scratch.at[at], sems.at[at])
        for at, source in enumerate(sources)
    ]
    for copy in copies:
        copy.start()
    for copy in copies:
        copy.wait()
    return [scratch[at].astype(jnp.float32) for at in range(len(copies))]


def add_kernel(halves, *refs):
    out, scratch, sems = refs[-3:]
    sources = [ref if half is None else ref.at[half] for ref, half in zip(refs, halves)]
    out[...] = sum(fetch(sources, scratch, sems)).astype(out.dtype)


def add(*terms):
    halves = tuple(term[1] if isinstance(term, tuple) else None for term in terms)
    terms = [term[0] if isinstance(term, tuple) else term for term in terms]
    shape, dtype = terms[0].shape, terms[0].dtype
    return pl.pallas_call(
        functools.partial(add_kernel, halves),
        in_specs=[pl.BlockSpec(memory_space=pltpu.HBM)] * len(terms),
        out_specs=pl.BlockSpec(memory_space=pltpu.VMEM),
        out_shape=jax.ShapeDtypeStruct(shape, dtype),
        scratch_shapes=[
            pltpu.VMEM((len(terms),) + shape, dtype),
            pltpu.SemaphoreType.DMA((len(terms),)),
        ],
        compiler_params=pltpu.CompilerParams(vmem_limit_bytes=VMEM_LIMIT),
        cost_estimate=cost_of(100e-6),
        name="add",
    )(*terms)


def join_kernel(near_ref, own_ref, far_ref, near_out, own_out, scratch, sems):
    near, own, *far = fetch((near_ref, own_ref, far_ref.at[0], far_ref.at[1]), scratch, sems)
    near_out[...] = (near + far[0]).astype(near_out.dtype)
    own_out[...] = (own + far[1]).astype(own_out.dtype)


def join(near, own, far):
    vmem = pl.BlockSpec(memory_space=pltpu.VMEM)
    return pl.pallas_call(
        join_kernel,
        in_specs=[pl.BlockSpec(memory_space=pltpu.HBM)] * 3,
        out_specs=[vmem] * 2,
        out_shape=[jax.ShapeDtypeStruct(near.shape, near.dtype)] * 2,
        scratch_shapes=[
            pltpu.VMEM((4,) + near.shape, near.dtype),
            pltpu.SemaphoreType.DMA((4,)),
        ],
        compiler_params=pltpu.CompilerParams(vmem_limit_bytes=VMEM_LIMIT),
        cost_estimate=cost_of(2e-6),
        name="join",
    )(near, own, far)


def finish_kernel(halves, side_ref, hidden_ref, received_ref, *refs):
    o_ref, rest, kept_part, near_part, parts, sems, out_sems = refs[-7:]
    sources = [ref if half is None else ref.at[half] for ref, half in zip(refs, halves)]
    half = received_ref.shape[2]
    kept = pl.ds(pl.multiple_of(side_ref[0] * half, HD), half)
    other = pl.ds(pl.multiple_of((1 - side_ref[0]) * half, HD), half)
    copies = [
        pltpu.make_async_copy(hidden_ref.at[:, other], rest.at[0], sems.at[0]),
        pltpu.make_async_copy(received_ref.at[0], near_part, sems.at[1]),
        pltpu.make_async_copy(hidden_ref.at[:, kept], rest.at[1], sems.at[2]),
    ] + [
        pltpu.make_async_copy(source.at[0], parts.at[at], sems.at[3 + at])
        for at, source in enumerate(sources)
    ]
    for copy in copies:
        copy.start()
    for copy in copies[:2]:
        copy.wait()
    near_part[...] = (
        rest[0].astype(jnp.float32) + near_part[...].astype(jnp.float32)
    ).astype(near_part.dtype)
    outs = [pltpu.make_async_copy(near_part, o_ref.at[:, other], out_sems.at[0])]
    outs[0].start()
    for copy in copies[2:]:
        copy.wait()
    total = rest[1].astype(jnp.float32)
    for at in range(len(sources)):
        total += parts[at].astype(jnp.float32)
    kept_part[...] = total.astype(kept_part.dtype)
    outs.append(pltpu.make_async_copy(kept_part, o_ref.at[:, kept], out_sems.at[1]))
    outs[1].start()
    for copy in outs:
        copy.wait()


def finish(side, hidden, received, parts):
    halves = tuple(part[1] if isinstance(part, tuple) else None for part in parts)
    parts = [part[0] if isinstance(part, tuple) else part for part in parts]
    hbm = pl.BlockSpec(memory_space=pltpu.HBM)
    half = received.shape[1:]
    return pl.pallas_call(
        functools.partial(finish_kernel, halves),
        in_specs=[pl.BlockSpec(memory_space=pltpu.SMEM)] + [hbm] * (2 + len(parts)),
        out_specs=hbm,
        out_shape=jax.ShapeDtypeStruct(hidden.shape, hidden.dtype),
        scratch_shapes=[
            pltpu.VMEM((2, *half), hidden.dtype),
            pltpu.VMEM(half, hidden.dtype),
            pltpu.VMEM(half, hidden.dtype),
            pltpu.VMEM((len(parts), *half), hidden.dtype),
            pltpu.SemaphoreType.DMA((3 + len(parts),)),
            pltpu.SemaphoreType.DMA((2,)),
        ],
        compiler_params=pltpu.CompilerParams(vmem_limit_bytes=VMEM_LIMIT),
        cost_estimate=cost_of(2e-6),
        name="finish",
    )(side.reshape(1), hidden, received, *parts)


def to_tp(value, pairs):
    return lax.ppermute(value, "tp", pairs)


def apart(tps, distance):
    return [(i, i ^ distance) for i in range(tps)]


def after(value, *others):
    return lax.optimization_barrier((value, *others))[0]


def per_device(
    reqs,
    tps,
    hidden,
    q_new,
    k_new,
    v_new,
    cache_k,
    cache_v,
    cache_len,
    w_out,
    q_cross,
    text_k,
    text_v,
    prompt_of,
):
    rows, width = q_new.shape
    chips = reqs // 2
    place = lax.axis_index("req")
    chip = place // 2
    side = chip % 2
    text_side = (chip // 2) % 2

    def swap(array, distance):
        return lax.ppermute(array, "req", [(i, i ^ distance) for i in range(reqs)])

    first_of = [2 * i + i % 2 for i in range(chips)]
    second_of = [2 * i + 1 - i % 2 for i in range(chips)]
    beside = lax.ppermute(
        w_out,
        "req",
        [(first_of[i], first_of[i ^ 2]) for i in range(chips)]
        + [(second_of[i], second_of[i ^ 1]) for i in range(chips)],
    )
    own_passed = lax.ppermute(w_out, "req", list(zip(first_of, second_of)))

    own = self_attention(q_new, k_new, v_new, cache_k[0], cache_v[0], cache_len)
    near = swap(own, 2)
    beside = after(beside, own)
    across = lax.ppermute(
        beside, "req", [(second_of[i], second_of[i ^ 2]) for i in range(chips)]
    )
    beside_passed = swap(beside, 1)
    split_heads = (width // HD) % 2 == 0
    if split_heads:
        keep, give, ask = pack(text_side, prompt_of, text_k, text_v, after(q_cross, own))
        across = after(across, keep)
        give, keep, ask = after((give, keep, ask), near)
        if chips == 4:
            pieces = [keep, swap(give, 4), swap(keep, 2), swap(give, 6)]
        else:
            pieces = [keep, swap(give, 4)]
            for bit in range(chips.bit_length() - 1):
                if bit != 1:
                    pieces += [swap(piece, 2 << bit) for piece in pieces]
        spans = text_k.shape[:2]
    across_passed = lax.ppermute(after(across, near), "req", list(zip(second_of, first_of)))
    held = [w_out, beside_passed, beside, across_passed]
    passed = [own_passed, beside, beside_passed, across]
    bit = 4
    while bit < chips:
        held += [swap(block, 2 * bit) for block in held]
        passed += [swap(block, 2 * bit) for block in passed]
        bit *= 2
    def in_order(side, kept, received, axis):
        return jnp.where(
            side == 0,
            jnp.concatenate([kept, received], axis=axis),
            jnp.concatenate([received, kept], axis=axis),
        )

    line = split_heads and tps == 4 and chips == 4
    terms = project(tps, own, near, held, passed, line)
    if line:
        near_terms, own_terms, last = terms[:3], terms[3:6], terms[6]
        far, inner = to_tp(last, [(0, 1), (3, 2)]), to_tp(last, [(1, 2), (2, 1)])
        prompt = gate(prompt_of, *pieces[1:])
        near_joined, own_joined = join(near_terms[2], own_terms[2], after(far, inner, prompt))
        near_outer, own_outer, ask, *late = after(
            (near_terms[1], own_terms[1], ask, *pieces), near_joined
        )
        near_outer, near_crossing = to_tp(near_outer, apart(4, 1)), to_tp(near_joined, apart(4, 2))
        own_outer, own_crossing = to_tp(own_outer, apart(4, 1)), to_tp(own_joined, apart(4, 2))
        pieces += [swap(piece, 1) for piece in late]
        asked = swap(ask, 4)
        mine, others = cross_attention(prompt, text_side, q_cross, asked, pieces, spans)
        answer = swap(others, 4)
        near_outer = after(near_outer, mine)
        given = add(near_terms[0], (inner, 0), near_outer, near_crossing)
        own_parts = [own_terms[0], (inner, 1), own_outer, own_crossing]
        cross_heads = in_order(text_side, mine, answer, 1)
        side = gate(side, own_outer, own_crossing, cross_heads)
    else:
        near_parts = [
            [part[0]] + [to_tp(part[d], apart(tps, d)) for d in range(1, tps)]
            for part in (terms[:tps], terms[tps:])
        ]
        given, own_parts = add(*near_parts[0]), near_parts[1]
        if split_heads:
            pieces += [swap(piece, 1) for piece in pieces]
            asked = swap(ask, 4)
            mine, others = cross_attention(prompt_of, text_side, q_cross, asked, pieces, spans)
            answer = swap(others, 4)
            cross_heads = in_order(text_side, mine, answer, 1)

    if not split_heads:
        cross_heads = whole_cross(q_cross, prompt_of, text_k, text_v)

    received = swap(given, 2)
    if received.shape[0] == 1 and received.shape[2] % HD == 0:
        return finish(side, hidden, received, own_parts), cross_heads
    ordered = in_order(side, add(*own_parts), received, 2).transpose(1, 0, 2).reshape(rows, width)
    hidden_out = (hidden.astype(jnp.float32) + ordered.astype(jnp.float32)).astype(jnp.bfloat16)
    return (hidden_out, cross_heads)


def solution(mesh):
    placed = (
        P("req", "tp"),
        P("req", "tp"),
        P("req", "tp"),
        P("req", "tp"),
        P("req", None, "tp"),
        P("req", None, "tp"),
        P(),
        P("tp", "req"),
        P("req", "tp"),
        P(None, "req", "tp"),
        P(None, "req", "tp"),
        P("req"),
    )
    return jax.shard_map(
        functools.partial(per_device, mesh.shape["req"], mesh.shape["tp"]),
        mesh=mesh,
        in_specs=placed,
        out_specs=(P("req", "tp"), P("req", "tp")),
        check_vma=False,
    )
```

```python
import functools

import jax
import jax.numpy as jnp
from jax import lax
from jax.experimental import pallas as pl
from jax.experimental.pallas import tpu as pltpu
from jax.sharding import PartitionSpec as P

HD = 128
CACHE_BLOCK = 1024
TAG_ROWS = 16
NEG_FILL = -1e30
LOG2E = 1.4426950408889634
VMEM_LIMIT = 64 * 2**20 - 2**17
PEAK = 1.1535e15


def cost_of(seconds):
    return pl.CostEstimate(flops=int(seconds * PEAK), bytes_accessed=0, transcendentals=0)


def repeat_lanes(array, times):
    return jnp.concatenate([array] * times, axis=1) if times > 1 else array


def score(queries, keys):
    return lax.dot_general(
        queries, keys, (((1,), (1,)), ((), ())), preferred_element_type=jnp.float32
    )


def absorb(scores, values, state, visible):
    top_old, total = state
    scale = HD ** (-0.5) * LOG2E
    if visible is not None:
        scores = jnp.where(visible, scores, NEG_FILL)
    top = jnp.maximum(top_old, jnp.max(scores, axis=1, keepdims=True))
    shrink = jnp.exp2((top_old - top) * scale)
    shift = repeat_lanes(top * scale, scores.shape[1] // HD)
    weights = jnp.exp2(scores * scale - shift).astype(jnp.bfloat16)
    extended = jnp.concatenate([values, jnp.ones_like(values)], axis=1)
    total = total * repeat_lanes(shrink, 2) + jnp.dot(
        weights, extended, preferred_element_type=jnp.float32
    )
    return top, total


def empty_state(rows):
    return jnp.full((rows, HD), NEG_FILL, jnp.float32), jnp.zeros((rows, 2 * HD), jnp.float32)


def finished(total):
    return (total[:, :HD] / total[:, HD:]).astype(jnp.bfloat16)


def visit_heads(count, scores_of, use):
    ahead = scores_of(0)
    for head in range(count):
        scores = ahead
        if head + 1 < count:
            ahead = scores_of(head + 1)
        use(head, scores)


def self_kernel(
    block_rows, heads, length_ref, q_ref, kn_ref, vn_ref, kc_ref, vc_ref, o_ref, top_ref, total_ref
):
    step, steps = pl.program_id(0), pl.num_programs(0)
    left = length_ref[lax.axis_index("req")] - step * block_rows
    rows, new_rows = q_ref.shape[0], kn_ref.shape[0]

    @pl.when(step == 0)
    def _():
        for head in range(heads):
            top_ref[head], total_ref[head] = empty_state(rows)

    def visit(k_ref, v_ref, visible, last):
        def use(head, scores):
            cols = slice(head * HD, (head + 1) * HD)
            state = (top_ref[head], total_ref[head])
            top, total = absorb(scores, v_ref[:, cols], state, visible)
            if last:
                o_ref[:, cols] = finished(total)
            else:
                top_ref[head], total_ref[head] = top, total

        def scores_of(head):
            cols = slice(head * HD, (head + 1) * HD)
            return score(q_ref[:, cols], k_ref[:, cols])

        visit_heads(heads, scores_of, use)

    @pl.when(jnp.logical_and(step < steps - 1, left >= block_rows))
    def _():
        visit(kc_ref, vc_ref, None, False)

    @pl.when(jnp.logical_and(step < steps - 1, jnp.logical_and(left > 0, left < block_rows)))
    def _():
        visible = lax.broadcasted_iota(jnp.int32, (rows, block_rows), 1) < left
        visit(kc_ref, vc_ref, visible, False)

    @pl.when(step == steps - 1)
    def _():
        key_ids = lax.broadcasted_iota(jnp.int32, (rows, new_rows), 1)
        query_ids = lax.broadcasted_iota(jnp.int32, (rows, new_rows), 0)
        visit(kn_ref, vn_ref, key_ids <= query_ids, True)


def self_attention(queries, new_keys, new_values, keys, values, lengths):
    rows, width = queries.shape
    new_rows, capacity = new_keys.shape[0], keys.shape[0]
    block_rows = min(CACHE_BLOCK, capacity)
    heads = width // HD
    whole = pl.BlockSpec((rows, width), lambda i, n: (0, 0))
    new = pl.BlockSpec((new_rows, width), lambda i, n: (0, 0))

    def live_block(step, length_ref):
        length = length_ref[lax.axis_index("req")]
        return jnp.minimum(step, lax.div(length - 1, block_rows)), 0

    cached = pl.BlockSpec((block_rows, width), live_block)
    return pl.pallas_call(
        functools.partial(self_kernel, block_rows, heads),
        grid_spec=pltpu.PrefetchScalarGridSpec(
            num_scalar_prefetch=1,
            grid=(capacity // block_rows + 1,),
            in_specs=[whole, new, new, cached, cached],
            out_specs=whole,
            scratch_shapes=[
                pltpu.VMEM((heads, rows, HD), jnp.float32),
                pltpu.VMEM((heads, rows, 2 * HD), jnp.float32),
            ],
        ),
        out_shape=jax.ShapeDtypeStruct((rows, width), jnp.bfloat16),
        compiler_params=pltpu.CompilerParams(vmem_limit_bytes=VMEM_LIMIT),
        cost_estimate=cost_of(20e-6),
        name="self_attention",
    )(lengths, queries, new_keys, new_values, keys, values)


def cross_kernel(heads, pieces_count, spans, prompt_ref, side_ref, q_ref, near_ref, *refs):
    pieces, (own_ref, other_ref) = refs[:pieces_count], refs[pieces_count:]
    rows = q_ref.shape[0]
    width = heads * HD
    first = pl.multiple_of(side_ref[0] * width, HD)
    tag = near_ref[rows:, :HD].astype(jnp.float32)
    prompts = prompt_ref[0], jnp.max(tag).astype(jnp.int32)
    for part, prompt in enumerate(prompts):
        target = other_ref if part else own_ref

        def gathered(kind, head, prompt=prompt):
            cols = slice(head * HD, (head + 1) * HD)
            count, text_rows = spans
            at = pl.ds(pl.multiple_of((kind * count + prompt) * text_rows, text_rows), text_rows)
            return jnp.concatenate([piece[at, cols] for piece in pieces], axis=0)

        def scores_of(head, part=part, gathered=gathered):
            source = near_ref if part else q_ref
            queries = source[:rows, pl.ds(pl.multiple_of(first + head * HD, HD), HD)]
            return score(queries, gathered(0, head))

        def use(head, scores, target=target, gathered=gathered):
            _, total = absorb(scores, gathered(1, head), empty_state(rows), None)
            target[:, head * HD : (head + 1) * HD] = finished(total)

        visit_heads(heads, scores_of, use)


def cross_attention(prompt, side, queries, near, pieces, spans):
    rows, width = queries.shape
    half = width // 2
    scalars = pl.BlockSpec(memory_space=pltpu.SMEM)
    vmem = pl.BlockSpec(memory_space=pltpu.VMEM)
    return pl.pallas_call(
        functools.partial(cross_kernel, half // HD, len(pieces), spans),
        in_specs=[scalars, scalars] + [vmem] * (2 + len(pieces)),
        out_specs=[vmem, vmem],
        out_shape=[jax.ShapeDtypeStruct((rows, half), jnp.bfloat16)] * 2,
        compiler_params=pltpu.CompilerParams(vmem_limit_bytes=VMEM_LIMIT),
        cost_estimate=cost_of(2e-6),
        name="cross_attention",
    )(prompt, side.reshape(1), queries, near, *pieces)


def gate_kernel(value_ref, *refs):
    refs[-1][0] = value_ref[0]


def gate(value, *waited):
    scalars = pl.BlockSpec(memory_space=pltpu.SMEM)
    return pl.pallas_call(
        gate_kernel,
        in_specs=[scalars] + [pl.BlockSpec(memory_space=pltpu.HBM)] * len(waited),
        out_specs=scalars,
        out_shape=jax.ShapeDtypeStruct((1,), jnp.int32),
        cost_estimate=cost_of(100e-6),
        name="gate",
    )(value.reshape(1), *waited)


def pack_kernel(side_ref, prompt_ref, k_ref, v_ref, q_ref, keep_ref, give_ref, ask_ref):
    half = keep_ref.shape[1]
    prompts, text_rows, _ = k_ref.shape
    kept = pl.ds(pl.multiple_of(side_ref[0] * half, HD), half)
    given = pl.ds(pl.multiple_of((1 - side_ref[0]) * half, HD), half)
    for part, source in enumerate((k_ref, v_ref)):
        for prompt in range(prompts):
            first = (part * prompts + prompt) * text_rows
            at = slice(first, first + text_rows)
            keep_ref[at, :] = source[prompt, :, kept]
            give_ref[at, :] = source[prompt, :, given]
    rows = q_ref.shape[0]
    ask_ref[:rows, :] = q_ref[...]
    tag = jnp.full((TAG_ROWS, 2 * half), prompt_ref[0], jnp.int32)
    ask_ref[rows:, :] = tag.astype(jnp.float32).astype(ask_ref.dtype)


def pack(side, prompt_of, text_k, text_v, queries):
    prompts, text_rows, width = text_k.shape
    rows, half = queries.shape[0], width // 2
    text = jax.ShapeDtypeStruct((2 * prompts * text_rows, half), text_k.dtype)
    ask = jax.ShapeDtypeStruct((rows + TAG_ROWS, width), queries.dtype)
    scalars = pl.BlockSpec(memory_space=pltpu.SMEM)
    vmem = pl.BlockSpec(memory_space=pltpu.VMEM)
    return pl.pallas_call(
        pack_kernel,
        in_specs=[scalars, scalars, vmem, vmem, vmem],
        out_specs=[vmem] * 3,
        out_shape=[text, text, ask],
        compiler_params=pltpu.CompilerParams(vmem_limit_bytes=VMEM_LIMIT),
        cost_estimate=cost_of(3e-6),
        name="pack",
    )(side.reshape(1), prompt_of, text_k, text_v, queries)


def whole_cross_kernel(heads, q_ref, k_ref, v_ref, o_ref):
    def scores_of(head):
        cols = slice(head * HD, (head + 1) * HD)
        return score(q_ref[:, cols], k_ref[:, cols])

    def use(head, scores):
        cols = slice(head * HD, (head + 1) * HD)
        _, total = absorb(scores, v_ref[:, cols], empty_state(q_ref.shape[0]), None)
        o_ref[:, cols] = finished(total)

    visit_heads(heads, scores_of, use)


def whole_cross(queries, prompt_of, text_k, text_v):
    keys, values = (
        lax.dynamic_index_in_dim(
            lax.all_gather(text, "req", axis=1, tiled=True), prompt_of[0], 0, keepdims=False
        )
        for text in (text_k, text_v)
    )
    return pl.pallas_call(
        functools.partial(whole_cross_kernel, queries.shape[1] // HD),
        out_shape=jax.ShapeDtypeStruct(queries.shape, jnp.bfloat16),
        compiler_params=pltpu.CompilerParams(vmem_limit_bytes=VMEM_LIMIT),
        name="whole_cross",
    )(queries, keys, values)


def project_kernel(count, flat, places, joint, own_ref, near_ref, *refs):
    held, passed = refs[:count], refs[count : 2 * count]
    outs = refs[2 * count : -6]
    x_ref, weights, terms, x_sems, sems, out_sems = refs[-6:]
    place, at_tp = lax.axis_index("req"), lax.axis_index("tp")
    chip = lax.div(place, 2)
    holder = lax.rem(place, 2) == lax.rem(chip, 2)
    rows, columns = own_ref.shape[0], held[0].shape[1]
    blocks = outs[0].shape[0]
    if joint:
        outs = (*outs[: places - 1], outs[-1].at[0], *outs[places - 1 : -1], outs[-1].at[1])

    def rows_in(part):
        source = (near_ref, own_ref)[part]
        return pltpu.make_async_copy(
            source, x_ref.at[part * rows : (part + 1) * rows], x_sems.at[part]
        )

    def weights_in(choice, at):
        target = weights.at[:, at * columns : (at + 1) * columns] if flat else weights.at[at]
        return pltpu.make_async_copy(choice[at], target, sems.at[at])

    def terms_out(at, part, distance, block):
        if flat:
            source = terms.at[part, :, at * columns : (at + 1) * columns]
        else:
            source = terms.at[at, part]
        target = outs[part * places + distance].at[block]
        return pltpu.make_async_copy(source, target, out_sems.at[at, part])

    def send(at):
        source = chip ^ at
        block = lax.rem(source, blocks)
        away = lax.div(source, blocks) ^ at_tp
        for distance in range(places):

            @pl.when(away == distance)
            def _(at=at, distance=distance, block=block):
                for part in range(2):
                    terms_out(at, part, distance, block).start()

    for part in range(2):
        rows_in(part).start()

    @pl.when(holder)
    def _():
        for at in range(count):
            weights_in(held, at).start()

    @pl.when(jnp.logical_not(holder))
    def _():
        for at in range(count):
            weights_in(passed, at).start()

    for part in range(2):
        rows_in(part).wait()
    there = sent = 0
    for first in range(0, count * columns, flat or columns):
        last = first + (flat or columns)
        while there * columns < last:
            weights_in(held, there).wait()
            there += 1
        block_weights = weights[:, first:last] if flat else weights[first // columns]
        product = jnp.dot(x_ref[...], block_weights, preferred_element_type=jnp.float32)
        product = product.astype(terms.dtype)
        for part in range(2):
            piece = product[part * rows : (part + 1) * rows]
            if flat:
                terms[part, :, first:last] = piece
            else:
                terms[first // columns, part] = piece
        while (sent + 1) * columns <= last:
            send(sent)
            sent += 1

    for at in range(count):
        for part in range(2):
            terms_out(at, part, 0, 0).wait()


def project(tps, own, near, held, passed, joint):
    rows = own.shape[0]
    depth, columns = held[0].shape
    count = len(held)
    flat = 512 if columns % HD == 0 and count * columns % 512 == 0 else 0
    hbm = pl.BlockSpec(memory_space=pltpu.HBM)
    out = jax.ShapeDtypeStruct((count // tps, rows, columns), jnp.bfloat16)
    return pl.pallas_call(
        functools.partial(project_kernel, count, flat, tps, joint),
        in_specs=[hbm] * (2 + 2 * count),
        out_specs=[hbm] * (2 * tps - joint),
        out_shape=(
            [out] * (2 * tps - 2) + [jax.ShapeDtypeStruct((2, *out.shape), out.dtype)]
            if joint
            else [out] * (2 * tps)
        ),
        scratch_shapes=[
            pltpu.VMEM((2 * rows, depth), jnp.bfloat16),
            pltpu.VMEM((depth, count * columns) if flat else (count, depth, columns), jnp.bfloat16),
            pltpu.VMEM(
                (2, rows, count * columns) if flat else (count, 2, rows, columns), jnp.bfloat16
            ),
            pltpu.SemaphoreType.DMA((2,)),
            pltpu.SemaphoreType.DMA((count,)),
            pltpu.SemaphoreType.DMA((count, 2)),
        ],
        compiler_params=pltpu.CompilerParams(vmem_limit_bytes=VMEM_LIMIT),
        cost_estimate=cost_of(10e-6),
        name="project",
    )(own, near, *held, *passed)


def fetch(sources, scratch, sems):
    copies = [
        pltpu.make_async_copy(source, scratch.at[at], sems.at[at])
        for at, source in enumerate(sources)
    ]
    for copy in copies:
        copy.start()
    for copy in copies:
        copy.wait()
    return [scratch[at].astype(jnp.float32) for at in range(len(copies))]


def add_kernel(halves, *refs):
    out, scratch, sems = refs[-3:]
    sources = [ref if half is None else ref.at[half] for ref, half in zip(refs, halves)]
    out[...] = sum(fetch(sources, scratch, sems)).astype(out.dtype)


def add(*terms):
    halves = tuple(term[1] if isinstance(term, tuple) else None for term in terms)
    terms = [term[0] if isinstance(term, tuple) else term for term in terms]
    shape, dtype = terms[0].shape, terms[0].dtype
    return pl.pallas_call(
        functools.partial(add_kernel, halves),
        in_specs=[pl.BlockSpec(memory_space=pltpu.HBM)] * len(terms),
        out_specs=pl.BlockSpec(memory_space=pltpu.VMEM),
        out_shape=jax.ShapeDtypeStruct(shape, dtype),
        scratch_shapes=[
            pltpu.VMEM((len(terms),) + shape, dtype),
            pltpu.SemaphoreType.DMA((len(terms),)),
        ],
        compiler_params=pltpu.CompilerParams(vmem_limit_bytes=VMEM_LIMIT),
        cost_estimate=cost_of(100e-6),
        name="add",
    )(*terms)


def join_kernel(near_ref, own_ref, far_ref, near_out, own_out, scratch, sems):
    near, own, *far = fetch((near_ref, own_ref, far_ref.at[0], far_ref.at[1]), scratch, sems)
    near_out[...] = (near + far[0]).astype(near_out.dtype)
    own_out[...] = (own + far[1]).astype(own_out.dtype)


def join(near, own, far):
    vmem = pl.BlockSpec(memory_space=pltpu.VMEM)
    return pl.pallas_call(
        join_kernel,
        in_specs=[pl.BlockSpec(memory_space=pltpu.HBM)] * 3,
        out_specs=[vmem] * 2,
        out_shape=[jax.ShapeDtypeStruct(near.shape, near.dtype)] * 2,
        scratch_shapes=[
            pltpu.VMEM((4,) + near.shape, near.dtype),
            pltpu.SemaphoreType.DMA((4,)),
        ],
        compiler_params=pltpu.CompilerParams(vmem_limit_bytes=VMEM_LIMIT),
        cost_estimate=cost_of(100e-6),
        name="join",
    )(near, own, far)


def finish_kernel(halves, side_ref, hidden_ref, received_ref, *refs):
    o_ref, rest, kept_part, near_part, parts, sems, out_sems = refs[-7:]
    sources = [ref if half is None else ref.at[half] for ref, half in zip(refs, halves)]
    half = received_ref.shape[2]
    kept = pl.ds(pl.multiple_of(side_ref[0] * half, HD), half)
    other = pl.ds(pl.multiple_of((1 - side_ref[0]) * half, HD), half)
    copies = [
        pltpu.make_async_copy(hidden_ref.at[:, other], rest.at[0], sems.at[0]),
        pltpu.make_async_copy(received_ref.at[0], near_part, sems.at[1]),
        pltpu.make_async_copy(hidden_ref.at[:, kept], rest.at[1], sems.at[2]),
    ] + [
        pltpu.make_async_copy(source.at[0], parts.at[at], sems.at[3 + at])
        for at, source in enumerate(sources)
    ]
    for copy in copies:
        copy.start()
    for copy in copies[:2]:
        copy.wait()
    near_part[...] = (
        rest[0].astype(jnp.float32) + near_part[...].astype(jnp.float32)
    ).astype(near_part.dtype)
    outs = [pltpu.make_async_copy(near_part, o_ref.at[:, other], out_sems.at[0])]
    outs[0].start()
    for copy in copies[2:]:
        copy.wait()
    total = rest[1].astype(jnp.float32)
    for at in range(len(sources)):
        total += parts[at].astype(jnp.float32)
    kept_part[...] = total.astype(kept_part.dtype)
    outs.append(pltpu.make_async_copy(kept_part, o_ref.at[:, kept], out_sems.at[1]))
    outs[1].start()
    for copy in outs:
        copy.wait()


def finish(side, hidden, received, parts):
    halves = tuple(part[1] if isinstance(part, tuple) else None for part in parts)
    parts = [part[0] if isinstance(part, tuple) else part for part in parts]
    hbm = pl.BlockSpec(memory_space=pltpu.HBM)
    half = received.shape[1:]
    return pl.pallas_call(
        functools.partial(finish_kernel, halves),
        in_specs=[pl.BlockSpec(memory_space=pltpu.SMEM)] + [hbm] * (2 + len(parts)),
        out_specs=hbm,
        out_shape=jax.ShapeDtypeStruct(hidden.shape, hidden.dtype),
        scratch_shapes=[
            pltpu.VMEM((2, *half), hidden.dtype),
            pltpu.VMEM(half, hidden.dtype),
            pltpu.VMEM(half, hidden.dtype),
            pltpu.VMEM((len(parts), *half), hidden.dtype),
            pltpu.SemaphoreType.DMA((3 + len(parts),)),
            pltpu.SemaphoreType.DMA((2,)),
        ],
        compiler_params=pltpu.CompilerParams(vmem_limit_bytes=VMEM_LIMIT),
        cost_estimate=cost_of(2e-6),
        name="finish",
    )(side.reshape(1), hidden, received, *parts)


def to_tp(value, pairs):
    return lax.ppermute(value, "tp", pairs)


def apart(tps, distance):
    return [(i, i ^ distance) for i in range(tps)]


def after(value, *others):
    return lax.optimization_barrier((value, *others))[0]


def per_device(
    reqs,
    tps,
    hidden,
    q_new,
    k_new,
    v_new,
    cache_k,
    cache_v,
    cache_len,
    w_out,
    q_cross,
    text_k,
    text_v,
    prompt_of,
):
    rows, width = q_new.shape
    chips = reqs // 2
    place = lax.axis_index("req")
    chip = place // 2
    side = chip % 2
    text_side = (chip // 2) % 2

    def swap(array, distance):
        return lax.ppermute(array, "req", [(i, i ^ distance) for i in range(reqs)])

    first_of = [2 * i + i % 2 for i in range(chips)]
    second_of = [2 * i + 1 - i % 2 for i in range(chips)]
    beside = lax.ppermute(
        w_out,
        "req",
        [(first_of[i], first_of[i ^ 2]) for i in range(chips)]
        + [(second_of[i], second_of[i ^ 1]) for i in range(chips)],
    )
    own_passed = lax.ppermute(w_out, "req", list(zip(first_of, second_of)))

    own = self_attention(q_new, k_new, v_new, cache_k[0], cache_v[0], cache_len)
    near = swap(own, 2)
    beside = after(beside, own)
    across = lax.ppermute(
        beside, "req", [(second_of[i], second_of[i ^ 2]) for i in range(chips)]
    )
    beside_passed = swap(beside, 1)
    split_heads = (width // HD) % 2 == 0
    if split_heads:
        keep, give, ask = pack(text_side, prompt_of, text_k, text_v, after(q_cross, own))
        across = after(across, keep)
        give, keep, ask = after((give, keep, ask), near)
        if chips == 4:
            pieces = [keep, swap(give, 4), swap(keep, 2), swap(give, 6)]
        else:
            pieces = [keep, swap(give, 4)]
            for bit in range(chips.bit_length() - 1):
                if bit != 1:
                    pieces += [swap(piece, 2 << bit) for piece in pieces]
        spans = text_k.shape[:2]
    across_passed = lax.ppermute(after(across, near), "req", list(zip(second_of, first_of)))
    held = [w_out, beside_passed, beside, across_passed]
    passed = [own_passed, beside, beside_passed, across]
    bit = 4
    while bit < chips:
        held += [swap(block, 2 * bit) for block in held]
        passed += [swap(block, 2 * bit) for block in passed]
        bit *= 2
    def in_order(side, kept, received, axis):
        return jnp.where(
            side == 0,
            jnp.concatenate([kept, received], axis=axis),
            jnp.concatenate([received, kept], axis=axis),
        )

    line = split_heads and tps == 4 and chips == 4
    terms = project(tps, own, near, held, passed, line)
    if line:
        near_terms, own_terms, last = terms[:3], terms[3:6], terms[6]
        far, inner = to_tp(last, [(0, 1), (3, 2)]), to_tp(last, [(1, 2), (2, 1)])
        prompt = prompt_of
        near_joined, own_joined = join(near_terms[2], own_terms[2], after(far, inner, *pieces[1:]))
        near_outer, own_outer, ask, *late = after(
            (near_terms[1], own_terms[1], ask, *pieces), near_joined
        )
        near_outer, near_crossing = to_tp(near_outer, apart(4, 1)), to_tp(near_joined, apart(4, 2))
        own_outer, own_crossing = to_tp(own_outer, apart(4, 1)), to_tp(own_joined, apart(4, 2))
        pieces += [swap(piece, 1) for piece in late]
        asked = swap(ask, 4)
        mine, others = cross_attention(prompt, text_side, q_cross, asked, pieces, spans)
        answer = swap(others, 4)
        near_outer = after(near_outer, mine)
        given = add(near_terms[0], (inner, 0), near_outer, near_crossing)
        own_parts = [own_terms[0], (inner, 1), own_outer, own_crossing]
        cross_heads = in_order(text_side, mine, answer, 1)
        side = gate(side, own_outer, own_crossing, cross_heads)
    else:
        near_parts = [
            [part[0]] + [to_tp(part[d], apart(tps, d)) for d in range(1, tps)]
            for part in (terms[:tps], terms[tps:])
        ]
        given, own_parts = add(*near_parts[0]), near_parts[1]
        if split_heads:
            pieces += [swap(piece, 1) for piece in pieces]
            asked = swap(ask, 4)
            mine, others = cross_attention(prompt_of, text_side, q_cross, asked, pieces, spans)
            answer = swap(others, 4)
            cross_heads = in_order(text_side, mine, answer, 1)

    if not split_heads:
        cross_heads = whole_cross(q_cross, prompt_of, text_k, text_v)

    received = swap(given, 2)
    if received.shape[0] == 1 and received.shape[2] % HD == 0:
        return finish(side, hidden, received, own_parts), cross_heads
    ordered = in_order(side, add(*own_parts), received, 2).transpose(1, 0, 2).reshape(rows, width)
    hidden_out = (hidden.astype(jnp.float32) + ordered.astype(jnp.float32)).astype(jnp.bfloat16)
    return (hidden_out, cross_heads)


def solution(mesh):
    placed = (
        P("req", "tp"),
        P("req", "tp"),
        P("req", "tp"),
        P("req", "tp"),
        P("req", None, "tp"),
        P("req", None, "tp"),
        P(),
        P("tp", "req"),
        P("req", "tp"),
        P(None, "req", "tp"),
        P(None, "req", "tp"),
        P("req"),
    )
    return jax.shard_map(
        functools.partial(per_device, mesh.shape["req"], mesh.shape["tp"]),
        mesh=mesh,
        in_specs=placed,
        out_specs=(P("req", "tp"), P("req", "tp")),
        check_vma=False,
    )
```

```python
import functools

import jax
import jax.numpy as jnp
from jax import lax
from jax.experimental import pallas as pl
from jax.experimental.pallas import tpu as pltpu
from jax.sharding import PartitionSpec as P

HD = 128
CACHE_BLOCK = 1024
TAG_ROWS = 16
NEG_FILL = -1e30
LOG2E = 1.4426950408889634
VMEM_LIMIT = 64 * 2**20 - 2**17
PEAK = 1.1535e15


def cost_of(seconds):
    return pl.CostEstimate(flops=int(seconds * PEAK), bytes_accessed=0, transcendentals=0)


def repeat_lanes(array, times):
    return jnp.concatenate([array] * times, axis=1) if times > 1 else array


def score(queries, keys):
    return lax.dot_general(
        queries, keys, (((1,), (1,)), ((), ())), preferred_element_type=jnp.float32
    )


def absorb(scores, values, state, visible):
    top_old, total = state
    scale = HD ** (-0.5) * LOG2E
    if visible is not None:
        scores = jnp.where(visible, scores, NEG_FILL)
    top = jnp.maximum(top_old, jnp.max(scores, axis=1, keepdims=True))
    shrink = jnp.exp2((top_old - top) * scale)
    shift = repeat_lanes(top * scale, scores.shape[1] // HD)
    weights = jnp.exp2(scores * scale - shift).astype(jnp.bfloat16)
    extended = jnp.concatenate([values, jnp.ones_like(values)], axis=1)
    total = total * repeat_lanes(shrink, 2) + jnp.dot(
        weights, extended, preferred_element_type=jnp.float32
    )
    return top, total


def empty_state(rows):
    return jnp.full((rows, HD), NEG_FILL, jnp.float32), jnp.zeros((rows, 2 * HD), jnp.float32)


def finished(total):
    return (total[:, :HD] / total[:, HD:]).astype(jnp.bfloat16)


def visit_heads(count, scores_of, use):
    ahead = scores_of(0)
    for head in range(count):
        scores = ahead
        if head + 1 < count:
            ahead = scores_of(head + 1)
        use(head, scores)


def self_kernel(
    block_rows, heads, length_ref, q_ref, kn_ref, vn_ref, kc_ref, vc_ref, o_ref, top_ref, total_ref
):
    step, steps = pl.program_id(0), pl.num_programs(0)
    left = length_ref[lax.axis_index("req")] - step * block_rows
    rows, new_rows = q_ref.shape[0], kn_ref.shape[0]

    @pl.when(step == 0)
    def _():
        for head in range(heads):
            top_ref[head], total_ref[head] = empty_state(rows)

    def visit(k_ref, v_ref, visible, last):
        def use(head, scores):
            cols = slice(head * HD, (head + 1) * HD)
            state = (top_ref[head], total_ref[head])
            top, total = absorb(scores, v_ref[:, cols], state, visible)
            if last:
                o_ref[:, cols] = finished(total)
            else:
                top_ref[head], total_ref[head] = top, total

        def scores_of(head):
            cols = slice(head * HD, (head + 1) * HD)
            return score(q_ref[:, cols], k_ref[:, cols])

        visit_heads(heads, scores_of, use)

    @pl.when(jnp.logical_and(step < steps - 1, left >= block_rows))
    def _():
        visit(kc_ref, vc_ref, None, False)

    @pl.when(jnp.logical_and(step < steps - 1, jnp.logical_and(left > 0, left < block_rows)))
    def _():
        visible = lax.broadcasted_iota(jnp.int32, (rows, block_rows), 1) < left
        visit(kc_ref, vc_ref, visible, False)

    @pl.when(step == steps - 1)
    def _():
        key_ids = lax.broadcasted_iota(jnp.int32, (rows, new_rows), 1)
        query_ids = lax.broadcasted_iota(jnp.int32, (rows, new_rows), 0)
        visit(kn_ref, vn_ref, key_ids <= query_ids, True)


def self_attention(queries, new_keys, new_values, keys, values, lengths):
    rows, width = queries.shape
    new_rows, capacity = new_keys.shape[0], keys.shape[0]
    block_rows = min(CACHE_BLOCK, capacity)
    heads = width // HD
    whole = pl.BlockSpec((rows, width), lambda i, n: (0, 0))
    new = pl.BlockSpec((new_rows, width), lambda i, n: (0, 0))

    def live_block(step, length_ref):
        length = length_ref[lax.axis_index("req")]
        return jnp.minimum(step, lax.div(length - 1, block_rows)), 0

    cached = pl.BlockSpec((block_rows, width), live_block)
    return pl.pallas_call(
        functools.partial(self_kernel, block_rows, heads),
        grid_spec=pltpu.PrefetchScalarGridSpec(
            num_scalar_prefetch=1,
            grid=(capacity // block_rows + 1,),
            in_specs=[whole, new, new, cached, cached],
            out_specs=whole,
            scratch_shapes=[
                pltpu.VMEM((heads, rows, HD), jnp.float32),
                pltpu.VMEM((heads, rows, 2 * HD), jnp.float32),
            ],
        ),
        out_shape=jax.ShapeDtypeStruct((rows, width), jnp.bfloat16),
        compiler_params=pltpu.CompilerParams(vmem_limit_bytes=VMEM_LIMIT),
        cost_estimate=cost_of(20e-6),
        name="self_attention",
    )(lengths, queries, new_keys, new_values, keys, values)


def cross_kernel(heads, pieces_count, spans, prompt_ref, side_ref, q_ref, near_ref, *refs):
    pieces, (own_ref, other_ref) = refs[:pieces_count], refs[pieces_count:]
    rows = q_ref.shape[0]
    width = heads * HD
    first = pl.multiple_of(side_ref[0] * width, HD)
    tag = near_ref[rows:, :HD].astype(jnp.float32)
    prompts = prompt_ref[0], jnp.max(tag).astype(jnp.int32)
    for part, prompt in enumerate(prompts):
        target = other_ref if part else own_ref

        def gathered(kind, head, prompt=prompt):
            cols = slice(head * HD, (head + 1) * HD)
            count, text_rows = spans
            at = pl.ds(pl.multiple_of((kind * count + prompt) * text_rows, text_rows), text_rows)
            return jnp.concatenate([piece[at, cols] for piece in pieces], axis=0)

        def scores_of(head, part=part, gathered=gathered):
            source = near_ref if part else q_ref
            queries = source[:rows, pl.ds(pl.multiple_of(first + head * HD, HD), HD)]
            return score(queries, gathered(0, head))

        def use(head, scores, target=target, gathered=gathered):
            _, total = absorb(scores, gathered(1, head), empty_state(rows), None)
            target[:, head * HD : (head + 1) * HD] = finished(total)

        visit_heads(heads, scores_of, use)


def cross_attention(prompt, side, queries, near, pieces, spans):
    rows, width = queries.shape
    half = width // 2
    scalars = pl.BlockSpec(memory_space=pltpu.SMEM)
    vmem = pl.BlockSpec(memory_space=pltpu.VMEM)
    return pl.pallas_call(
        functools.partial(cross_kernel, half // HD, len(pieces), spans),
        in_specs=[scalars, scalars] + [vmem] * (2 + len(pieces)),
        out_specs=[vmem, vmem],
        out_shape=[jax.ShapeDtypeStruct((rows, half), jnp.bfloat16)] * 2,
        compiler_params=pltpu.CompilerParams(vmem_limit_bytes=VMEM_LIMIT),
        cost_estimate=cost_of(2e-6),
        name="cross_attention",
    )(prompt, side.reshape(1), queries, near, *pieces)


def gate_kernel(*refs):
    refs[-1][...] = jnp.zeros_like(refs[-1])


def gate(*waited):
    return pl.pallas_call(
        gate_kernel,
        in_specs=[pl.BlockSpec(memory_space=pltpu.HBM)] * len(waited),
        out_specs=pl.BlockSpec(memory_space=pltpu.VMEM),
        out_shape=jax.ShapeDtypeStruct((8, HD), jnp.float32),
        compiler_params=pltpu.CompilerParams(vmem_limit_bytes=VMEM_LIMIT),
        cost_estimate=cost_of(100e-6),
        name="gate",
    )(*waited)


def pack_kernel(side_ref, prompt_ref, k_ref, v_ref, q_ref, keep_ref, give_ref, ask_ref):
    half = keep_ref.shape[1]
    prompts, text_rows, _ = k_ref.shape
    kept = pl.ds(pl.multiple_of(side_ref[0] * half, HD), half)
    given = pl.ds(pl.multiple_of((1 - side_ref[0]) * half, HD), half)
    for part, source in enumerate((k_ref, v_ref)):
        for prompt in range(prompts):
            first = (part * prompts + prompt) * text_rows
            at = slice(first, first + text_rows)
            keep_ref[at, :] = source[prompt, :, kept]
            give_ref[at, :] = source[prompt, :, given]
    rows = q_ref.shape[0]
    ask_ref[:rows, :] = q_ref[...]
    tag = jnp.full((TAG_ROWS, 2 * half), prompt_ref[0], jnp.int32)
    ask_ref[rows:, :] = tag.astype(jnp.float32).astype(ask_ref.dtype)


def pack(side, prompt_of, text_k, text_v, queries):
    prompts, text_rows, width = text_k.shape
    rows, half = queries.shape[0], width // 2
    text = jax.ShapeDtypeStruct((2 * prompts * text_rows, half), text_k.dtype)
    ask = jax.ShapeDtypeStruct((rows + TAG_ROWS, width), queries.dtype)
    scalars = pl.BlockSpec(memory_space=pltpu.SMEM)
    vmem = pl.BlockSpec(memory_space=pltpu.VMEM)
    return pl.pallas_call(
        pack_kernel,
        in_specs=[scalars, scalars, vmem, vmem, vmem],
        out_specs=[vmem] * 3,
        out_shape=[text, text, ask],
        compiler_params=pltpu.CompilerParams(vmem_limit_bytes=VMEM_LIMIT),
        cost_estimate=cost_of(3e-6),
        name="pack",
    )(side.reshape(1), prompt_of, text_k, text_v, queries)


def whole_cross_kernel(heads, q_ref, k_ref, v_ref, o_ref):
    def scores_of(head):
        cols = slice(head * HD, (head + 1) * HD)
        return score(q_ref[:, cols], k_ref[:, cols])

    def use(head, scores):
        cols = slice(head * HD, (head + 1) * HD)
        _, total = absorb(scores, v_ref[:, cols], empty_state(q_ref.shape[0]), None)
        o_ref[:, cols] = finished(total)

    visit_heads(heads, scores_of, use)


def whole_cross(queries, prompt_of, text_k, text_v):
    keys, values = (
        lax.dynamic_index_in_dim(
            lax.all_gather(text, "req", axis=1, tiled=True), prompt_of[0], 0, keepdims=False
        )
        for text in (text_k, text_v)
    )
    return pl.pallas_call(
        functools.partial(whole_cross_kernel, queries.shape[1] // HD),
        out_shape=jax.ShapeDtypeStruct(queries.shape, jnp.bfloat16),
        compiler_params=pltpu.CompilerParams(vmem_limit_bytes=VMEM_LIMIT),
        name="whole_cross",
    )(queries, keys, values)


def project_kernel(count, flat, places, joint, own_ref, near_ref, *refs):
    held, passed = refs[:count], refs[count : 2 * count]
    outs = refs[2 * count : -6]
    x_ref, weights, terms, x_sems, sems, out_sems = refs[-6:]
    place, at_tp = lax.axis_index("req"), lax.axis_index("tp")
    chip = lax.div(place, 2)
    holder = lax.rem(place, 2) == lax.rem(chip, 2)
    rows, columns = own_ref.shape[0], held[0].shape[1]
    blocks = outs[0].shape[0]
    if joint:
        outs = (*outs[: places - 1], outs[-1].at[0], *outs[places - 1 : -1], outs[-1].at[1])

    def rows_in(part):
        source = (near_ref, own_ref)[part]
        return pltpu.make_async_copy(
            source, x_ref.at[part * rows : (part + 1) * rows], x_sems.at[part]
        )

    def weights_in(choice, at):
        target = weights.at[:, at * columns : (at + 1) * columns] if flat else weights.at[at]
        return pltpu.make_async_copy(choice[at], target, sems.at[at])

    def terms_out(at, part, distance, block):
        if flat:
            source = terms.at[part, :, at * columns : (at + 1) * columns]
        else:
            source = terms.at[at, part]
        target = outs[part * places + distance].at[block]
        return pltpu.make_async_copy(source, target, out_sems.at[at, part])

    def send(at):
        source = chip ^ at
        block = lax.rem(source, blocks)
        away = lax.div(source, blocks) ^ at_tp
        for distance in range(places):

            @pl.when(away == distance)
            def _(at=at, distance=distance, block=block):
                for part in range(2):
                    terms_out(at, part, distance, block).start()

    for part in range(2):
        rows_in(part).start()

    @pl.when(holder)
    def _():
        for at in range(count):
            weights_in(held, at).start()

    @pl.when(jnp.logical_not(holder))
    def _():
        for at in range(count):
            weights_in(passed, at).start()

    for part in range(2):
        rows_in(part).wait()
    there = sent = 0
    for first in range(0, count * columns, flat or columns):
        last = first + (flat or columns)
        while there * columns < last:
            weights_in(held, there).wait()
            there += 1
        block_weights = weights[:, first:last] if flat else weights[first // columns]
        product = jnp.dot(x_ref[...], block_weights, preferred_element_type=jnp.float32)
        product = product.astype(terms.dtype)
        for part in range(2):
            piece = product[part * rows : (part + 1) * rows]
            if flat:
                terms[part, :, first:last] = piece
            else:
                terms[first // columns, part] = piece
        while (sent + 1) * columns <= last:
            send(sent)
            sent += 1

    for at in range(count):
        for part in range(2):
            terms_out(at, part, 0, 0).wait()


def project(tps, own, near, held, passed, joint):
    rows = own.shape[0]
    depth, columns = held[0].shape
    count = len(held)
    flat = 512 if columns % HD == 0 and count * columns % 512 == 0 else 0
    hbm = pl.BlockSpec(memory_space=pltpu.HBM)
    out = jax.ShapeDtypeStruct((count // tps, rows, columns), jnp.bfloat16)
    return pl.pallas_call(
        functools.partial(project_kernel, count, flat, tps, joint),
        in_specs=[hbm] * (2 + 2 * count),
        out_specs=[hbm] * (2 * tps - joint),
        out_shape=(
            [out] * (2 * tps - 2) + [jax.ShapeDtypeStruct((2, *out.shape), out.dtype)]
            if joint
            else [out] * (2 * tps)
        ),
        scratch_shapes=[
            pltpu.VMEM((2 * rows, depth), jnp.bfloat16),
            pltpu.VMEM((depth, count * columns) if flat else (count, depth, columns), jnp.bfloat16),
            pltpu.VMEM(
                (2, rows, count * columns) if flat else (count, 2, rows, columns), jnp.bfloat16
            ),
            pltpu.SemaphoreType.DMA((2,)),
            pltpu.SemaphoreType.DMA((count,)),
            pltpu.SemaphoreType.DMA((count, 2)),
        ],
        compiler_params=pltpu.CompilerParams(vmem_limit_bytes=VMEM_LIMIT),
        cost_estimate=cost_of(10e-6),
        name="project",
    )(own, near, *held, *passed)


def fetch(sources, scratch, sems):
    copies = [
        pltpu.make_async_copy(source, scratch.at[at], sems.at[at])
        for at, source in enumerate(sources)
    ]
    for copy in copies:
        copy.start()
    for copy in copies:
        copy.wait()
    return [scratch[at].astype(jnp.float32) for at in range(len(copies))]


def add_kernel(halves, *refs):
    out, scratch, sems = refs[-3:]
    sources = [ref if half is None else ref.at[half] for ref, half in zip(refs, halves)]
    out[...] = sum(fetch(sources, scratch, sems)).astype(out.dtype)


def add(*terms):
    halves = tuple(term[1] if isinstance(term, tuple) else None for term in terms)
    terms = [term[0] if isinstance(term, tuple) else term for term in terms]
    shape, dtype = terms[0].shape, terms[0].dtype
    return pl.pallas_call(
        functools.partial(add_kernel, halves),
        in_specs=[pl.BlockSpec(memory_space=pltpu.HBM)] * len(terms),
        out_specs=pl.BlockSpec(memory_space=pltpu.VMEM),
        out_shape=jax.ShapeDtypeStruct(shape, dtype),
        scratch_shapes=[
            pltpu.VMEM((len(terms),) + shape, dtype),
            pltpu.SemaphoreType.DMA((len(terms),)),
        ],
        compiler_params=pltpu.CompilerParams(vmem_limit_bytes=VMEM_LIMIT),
        cost_estimate=cost_of(100e-6),
        name="add",
    )(*terms)


def join_kernel(near_ref, own_ref, far_ref, near_out, own_out, scratch, sems):
    near, own, *far = fetch((near_ref, own_ref, far_ref.at[0], far_ref.at[1]), scratch, sems)
    near_out[...] = (near + far[0]).astype(near_out.dtype)
    own_out[...] = (own + far[1]).astype(own_out.dtype)


def join(near, own, far):
    vmem = pl.BlockSpec(memory_space=pltpu.VMEM)
    return pl.pallas_call(
        join_kernel,
        in_specs=[pl.BlockSpec(memory_space=pltpu.HBM)] * 3,
        out_specs=[vmem] * 2,
        out_shape=[jax.ShapeDtypeStruct(near.shape, near.dtype)] * 2,
        scratch_shapes=[
            pltpu.VMEM((4,) + near.shape, near.dtype),
            pltpu.SemaphoreType.DMA((4,)),
        ],
        compiler_params=pltpu.CompilerParams(vmem_limit_bytes=VMEM_LIMIT),
        cost_estimate=cost_of(100e-6),
        name="join",
    )(near, own, far)


def finish_kernel(halves, gates, *refs):
    hidden_ref, received_ref, *refs = refs[gates:]
    side = lax.rem(lax.div(lax.axis_index("req"), 2), 2)
    o_ref, rest, kept_part, near_part, parts, sems, out_sems = refs[-7:]
    sources = [ref if half is None else ref.at[half] for ref, half in zip(refs, halves)]
    half = received_ref.shape[2]
    kept = pl.ds(pl.multiple_of(side * half, HD), half)
    other = pl.ds(pl.multiple_of((1 - side) * half, HD), half)
    copies = [
        pltpu.make_async_copy(hidden_ref.at[:, other], rest.at[0], sems.at[0]),
        pltpu.make_async_copy(received_ref.at[0], near_part, sems.at[1]),
        pltpu.make_async_copy(hidden_ref.at[:, kept], rest.at[1], sems.at[2]),
    ] + [
        pltpu.make_async_copy(source.at[0], parts.at[at], sems.at[3 + at])
        for at, source in enumerate(sources)
    ]
    for copy in copies:
        copy.start()
    for copy in copies[:2]:
        copy.wait()
    near_part[...] = (
        rest[0].astype(jnp.float32) + near_part[...].astype(jnp.float32)
    ).astype(near_part.dtype)
    outs = [pltpu.make_async_copy(near_part, o_ref.at[:, other], out_sems.at[0])]
    outs[0].start()
    for copy in copies[2:]:
        copy.wait()
    total = rest[1].astype(jnp.float32)
    for at in range(len(sources)):
        total += parts[at].astype(jnp.float32)
    kept_part[...] = total.astype(kept_part.dtype)
    outs.append(pltpu.make_async_copy(kept_part, o_ref.at[:, kept], out_sems.at[1]))
    outs[1].start()
    for copy in outs:
        copy.wait()


def finish(hidden, received, parts, waited):
    halves = tuple(part[1] if isinstance(part, tuple) else None for part in parts)
    parts = [part[0] if isinstance(part, tuple) else part for part in parts]
    hbm = pl.BlockSpec(memory_space=pltpu.HBM)
    half = received.shape[1:]
    return pl.pallas_call(
        functools.partial(finish_kernel, halves, len(waited)),
        in_specs=[hbm] * (2 + len(parts) + len(waited)),
        out_specs=hbm,
        out_shape=jax.ShapeDtypeStruct(hidden.shape, hidden.dtype),
        scratch_shapes=[
            pltpu.VMEM((2, *half), hidden.dtype),
            pltpu.VMEM(half, hidden.dtype),
            pltpu.VMEM(half, hidden.dtype),
            pltpu.VMEM((len(parts), *half), hidden.dtype),
            pltpu.SemaphoreType.DMA((3 + len(parts),)),
            pltpu.SemaphoreType.DMA((2,)),
        ],
        compiler_params=pltpu.CompilerParams(vmem_limit_bytes=VMEM_LIMIT),
        cost_estimate=cost_of(2e-6),
        name="finish",
    )(*waited, hidden, received, *parts)


def to_tp(value, pairs):
    return lax.ppermute(value, "tp", pairs)


def apart(tps, distance):
    return [(i, i ^ distance) for i in range(tps)]


def after(value, *others):
    return lax.optimization_barrier((value, *others))[0]


def per_device(
    reqs,
    tps,
    hidden,
    q_new,
    k_new,
    v_new,
    cache_k,
    cache_v,
    cache_len,
    w_out,
    q_cross,
    text_k,
    text_v,
    prompt_of,
):
    rows, width = q_new.shape
    chips = reqs // 2
    place = lax.axis_index("req")
    chip = place // 2
    side = chip % 2
    text_side = (chip // 2) % 2

    def swap(array, distance):
        return lax.ppermute(array, "req", [(i, i ^ distance) for i in range(reqs)])

    first_of = [2 * i + i % 2 for i in range(chips)]
    second_of = [2 * i + 1 - i % 2 for i in range(chips)]
    beside = lax.ppermute(
        w_out,
        "req",
        [(first_of[i], first_of[i ^ 2]) for i in range(chips)]
        + [(second_of[i], second_of[i ^ 1]) for i in range(chips)],
    )
    own_passed = lax.ppermute(w_out, "req", list(zip(first_of, second_of)))

    own = self_attention(q_new, k_new, v_new, cache_k[0], cache_v[0], cache_len)
    near = swap(own, 2)
    beside = after(beside, own)
    across = lax.ppermute(
        beside, "req", [(second_of[i], second_of[i ^ 2]) for i in range(chips)]
    )
    beside_passed = swap(beside, 1)
    split_heads = (width // HD) % 2 == 0
    if split_heads:
        keep, give, ask = pack(text_side, prompt_of, text_k, text_v, after(q_cross, own))
        across = after(across, keep)
        give, keep, ask = after((give, keep, ask), near)
        if chips == 4:
            pieces = [keep, swap(give, 4), swap(keep, 2), swap(give, 6)]
        else:
            pieces = [keep, swap(give, 4)]
            for bit in range(chips.bit_length() - 1):
                if bit != 1:
                    pieces += [swap(piece, 2 << bit) for piece in pieces]
        spans = text_k.shape[:2]
    across_passed = lax.ppermute(after(across, near), "req", list(zip(second_of, first_of)))
    held = [w_out, beside_passed, beside, across_passed]
    passed = [own_passed, beside, beside_passed, across]
    bit = 4
    while bit < chips:
        held += [swap(block, 2 * bit) for block in held]
        passed += [swap(block, 2 * bit) for block in passed]
        bit *= 2
    def in_order(side, kept, received, axis):
        return jnp.where(
            side == 0,
            jnp.concatenate([kept, received], axis=axis),
            jnp.concatenate([received, kept], axis=axis),
        )

    line = split_heads and tps == 4 and chips == 4
    terms = project(tps, own, near, held, passed, line)
    if line:
        near_terms, own_terms, last = terms[:3], terms[3:6], terms[6]
        far, inner = to_tp(last, [(0, 1), (3, 2)]), to_tp(last, [(1, 2), (2, 1)])
        prompt = prompt_of
        near_joined, own_joined = join(near_terms[2], own_terms[2], after(far, inner, *pieces[1:]))
        near_outer, own_outer, ask, *late = after(
            (near_terms[1], own_terms[1], ask, *pieces), near_joined
        )
        near_outer, near_crossing = to_tp(near_outer, apart(4, 1)), to_tp(near_joined, apart(4, 2))
        own_outer, own_crossing = to_tp(own_outer, apart(4, 1)), to_tp(own_joined, apart(4, 2))
        pieces += [swap(piece, 1) for piece in late]
        asked = swap(ask, 4)
        mine, others = cross_attention(prompt, text_side, q_cross, asked, pieces, spans)
        answer = swap(others, 4)
        near_outer = after(near_outer, mine)
        given = add(near_terms[0], (inner, 0), near_outer, near_crossing)
        own_parts = [own_terms[0], (inner, 1), own_outer, own_crossing]
        cross_heads = in_order(text_side, mine, answer, 1)
        waited = [gate(own_outer, own_crossing, cross_heads)]
    else:
        near_parts = [
            [part[0]] + [to_tp(part[d], apart(tps, d)) for d in range(1, tps)]
            for part in (terms[:tps], terms[tps:])
        ]
        given, own_parts, waited = add(*near_parts[0]), near_parts[1], []
        if split_heads:
            pieces += [swap(piece, 1) for piece in pieces]
            asked = swap(ask, 4)
            mine, others = cross_attention(prompt_of, text_side, q_cross, asked, pieces, spans)
            answer = swap(others, 4)
            cross_heads = in_order(text_side, mine, answer, 1)

    if not split_heads:
        cross_heads = whole_cross(q_cross, prompt_of, text_k, text_v)

    received = swap(given, 2)
    if received.shape[0] == 1 and received.shape[2] % HD == 0:
        return finish(hidden, received, own_parts, waited), cross_heads
    ordered = in_order(side, add(*own_parts), received, 2).transpose(1, 0, 2).reshape(rows, width)
    hidden_out = (hidden.astype(jnp.float32) + ordered.astype(jnp.float32)).astype(jnp.bfloat16)
    return (hidden_out, cross_heads)


def solution(mesh):
    placed = (
        P("req", "tp"),
        P("req", "tp"),
        P("req", "tp"),
        P("req", "tp"),
        P("req", None, "tp"),
        P("req", None, "tp"),
        P(),
        P("tp", "req"),
        P("req", "tp"),
        P(None, "req", "tp"),
        P(None, "req", "tp"),
        P("req"),
    )
    return jax.shard_map(
        functools.partial(per_device, mesh.shape["req"], mesh.shape["tp"]),
        mesh=mesh,
        in_specs=placed,
        out_specs=(P("req", "tp"), P("req", "tp")),
        check_vma=False,
    )
```
